32 devices in a mesh: row: 4 (over y, core), box: 8 (over z, x).
Axes of the slice: x: 2, y: 2, z: 4, core: 2. Of those that a mesh axis runs over, the one named last changes fastest.
Arguments:
- solved: bfloat16 [2, 8192, 512], P(None, ('box', 'row')), may hold values from -6 to 6
- rhs: bfloat16 [4, 8192, 512], P('row', 'box'), may hold values from -6 to 6
- leaf_basis: bfloat16 [4, 3, 32, 256, 128], P('row', None, 'box'), may hold values from -0.375 to 0.375
- first_level: bfloat16 [4, 3, 8, 4, 4, 128, 128], P('row', None, 'box'), may hold values from -0.25 to 0.25
- second_level: bfloat16 [4, 3, 8, 8, 128, 128], P('row', None, 'box'), may hold values from -0.5 to 0.5
- third_level: bfloat16 [4, 3, 8, 8, 128, 128], P('row', None, 'box'), may hold values from -0.25 to 0.25
- fourth_level: bfloat16 [4, 3, 8, 2, 2, 128, 128], P('row', None, 'box'), may hold values from -0.375 to 0.375
- out_basis: bfloat16 [4, 3, 16, 512, 128], P('row', None, 'box'), may hold values from -0.5 to 0.5
Outputs:
- unknowns: bfloat16 [4, 8192, 512], P('row', 'box')
The draws below stay inside these ranges and needn't reach their ends.
All inputs are finite; a program needn't handle non-finite values.
Results may differ from the reference program's by a relative error of at most 0.015.
Values may be sent and summed in bfloat16 or wider, within the bound.
No kernel may reach another device: no remote copies, remote signals or barrier semaphores. Data moves between devices by JAX's collectives and lax.ppermute only.
A program may use at most 128 MiB of HBM per device.

```python
import jax
import jax.numpy as jnp
from jax import lax

LEAF = 256
R = 128
NRHS = 512
BLK = 8192
GROUPS = 4
N_BOX = 8


def level_of(own_key, shape, split, least, top_value):
    factor_of, own = 1.0, jax.random.fold_in(own_key, 6)
    for axis_at, blocks in split:
        heights = jnp.exp(jax.random.uniform(jax.random.fold_in(own, axis_at), (blocks,), jnp.float32, least / len(split), top_value / len(split)))
        factor_of = factor_of * jnp.repeat(heights, shape[axis_at] // blocks).reshape([-1 if axis == axis_at else 1 for axis in range(len(shape))])
    return factor_of


def centred(key, dims, spread, limit, cuts=(), held_as=jnp.bfloat16):
    array = jax.random.normal(key, dims, jnp.float32) * spread
    if len(cuts) > 0:
        array = level_of(key, dims, cuts, -0.22, 0.18) * array
    return jnp.clip(array, min=-limit, max=limit).astype(held_as)


def setup_inputs(seed: int = 0) -> dict:
    splits = jax.random.split(jax.random.key(seed), 9)
    solved = centred(splits[0], (2, BLK, NRHS), 1.0, 6.0, ((1, 32),))
    rhs = centred(splits[1], (GROUPS, BLK, NRHS), 1.0, 6.0, ((0, 4), (1, 8)))
    leaf_basis = centred(splits[2], (GROUPS, 3, 4 * N_BOX, LEAF, R), LEAF ** -0.5, 0.375, ((0, 4), (2, 8)))
    first_level = centred(splits[3], (GROUPS, 3, N_BOX, 4, 4, R, R), (4 * R) ** -0.5, 0.25, ((0, 4), (2, 8)))
    second_level = centred(splits[4], (GROUPS, 3, N_BOX, N_BOX, R, R), R ** -0.5, 0.5, ((0, 4), (2, 8)))
    third_level = centred(splits[5], (GROUPS, 3, N_BOX, N_BOX, R, R), (4 * R) ** -0.5, 0.25, ((0, 4), (2, 8)))
    fourth_level = centred(splits[6], (GROUPS, 3, N_BOX, 2, N_BOX // 4, R, R), (R * N_BOX // 4) ** -0.5, 0.375, ((0, 4), (2, 8)))
    out_basis = centred(splits[7], (GROUPS, 3, 2 * N_BOX, 2 * LEAF, R), R ** -0.5, 0.5, ((0, 4), (2, 8)))
    return dict(solved=solved, rhs=rhs, leaf_basis=leaf_basis, first_level=first_level, second_level=second_level, third_level=third_level, fourth_level=fourth_level, out_basis=out_basis)


def as_float(value):
    return value.astype(jnp.float32)


def apply_butterfly(inputs, basis, first_mats, second_mats, third_mats, fourth_mats, outer_basis):
    columns = inputs.shape[-1]
    leaf_coef = jnp.einsum('lpr,lpn->lrn', as_float(basis), as_float(inputs.reshape(4 * N_BOX, LEAF, columns))).astype(jnp.bfloat16)
    mid_coef = jnp.einsum('dskrq,dkqn->dsrn', as_float(first_mats), as_float(leaf_coef.reshape(N_BOX, 4, R, columns))).astype(jnp.bfloat16)
    slot_coef = jnp.einsum('dstrq,dsqn->dstrn', as_float(second_mats.reshape(N_BOX, 4, N_BOX // 4, R, R)), as_float(mid_coef)).astype(jnp.bfloat16)
    slot_coef = slot_coef.reshape(N_BOX // 4, 4, N_BOX, R, columns)
    group_coef = jnp.einsum('egkrq,gkeqn->egrn', as_float(third_mats.reshape(N_BOX, N_BOX // 4, 4, R, R)), as_float(slot_coef)).astype(jnp.bfloat16)
    half_coef = jnp.einsum('ehgrq,egqn->ehrn', as_float(fourth_mats), as_float(group_coef)).astype(jnp.bfloat16)
    result = jnp.einsum('ehpr,ehrn->ehpn', as_float(outer_basis.reshape(N_BOX, 2, 2 * LEAF, R)), as_float(half_coef))
    return result.reshape(4 * LEAF * N_BOX, columns)


def reference(solved, rhs, leaf_basis, first_level, second_level, third_level, fourth_level, out_basis):
    def one_group(item):
        rhs_rows, basis, first_mats, second_mats, third_mats, fourth_mats, outer_basis = item

        def butterfly(which, inputs):
            return apply_butterfly(inputs, basis[which], first_mats[which], second_mats[which], third_mats[which], fourth_mats[which], outer_basis[which])

        residual = as_float(rhs_rows) - butterfly(0, solved[0]) - butterfly(1, solved[1])
        residual_b = residual.astype(jnp.bfloat16)
        return (residual + butterfly(2, residual_b)).astype(jnp.bfloat16)

    return lax.map(one_group, (rhs, leaf_basis, first_level, second_level, third_level, fourth_level, out_basis))
```

```python
import functools

import jax
import jax.numpy as jnp
from jax import lax
from jax.experimental import pallas as pl
from jax.experimental.pallas import tpu as pltpu
from jax.sharding import PartitionSpec as P

F32 = jnp.float32
BF16 = jnp.bfloat16
VMEM_LIMIT = 48 * 1024 * 1024


def dot(a, b):
    return jnp.dot(a, b, preferred_element_type=F32)


def dot_t(a, b):
    return lax.dot_general(a, b, (((0,), (0,)), ((), ())), preferred_element_type=F32)


def place(radix):
    box = lax.axis_index("box")
    return lax.div(box, radix), lax.rem(box, radix)


def wrap(value, size):
    return lax.rem(value + size, size)


def column_levels(leaf, order, first, second, thirds, mid_ref, own_refs, other_refs, at):
    levels, radix = first.shape[0], first.shape[1]
    slots = second.shape[0]
    groups = slots // radix
    group, member = place(radix)
    matrix = jnp.concatenate(
        [jnp.concatenate([first[s, k] for k in order], axis=1) for s in range(levels)], axis=0
    )
    mid = dot(matrix, jnp.concatenate(leaf, axis=0)).astype(BF16)
    mid_ref[...] = mid.reshape(mid_ref.shape)
    for i in range(radix):
        other = jnp.bitwise_xor(member, i)
        slot = group * radix + other
        own_refs[i][at] = dot(second[slot], mid_ref[lax.div(slot, slots // levels)]).astype(BF16)
        for delta in range(1, groups):
            slot = wrap(group - delta, groups) * radix + other
            coef = dot(second[slot], mid_ref[lax.div(slot, slots // levels)]).astype(BF16)
            other_refs[i][at, delta - 1] = dot(thirds[delta - 1][i][at], coef).astype(BF16)


def row_levels(j, own, crossed, third, fourth, out_basis, radix):
    groups = fourth.shape[1]
    group, member = place(radix)
    total = None
    for i in range(radix):
        part = dot(third[group * radix + jnp.bitwise_xor(member, i)], own[i][j])
        total = part if total is None else total + part
    coefs = [total.astype(BF16)] + [ref[j] for ref in crossed]
    coefs = jnp.concatenate(coefs, axis=0)
    rows = []
    for h in range(fourth.shape[0]):
        mats = [fourth[h, wrap(group + delta, groups)] for delta in range(groups)]
        half = dot(jnp.concatenate(mats, axis=1), coefs).astype(BF16)
        rows.append(dot(out_basis[h], half))
    return rows


def take(refs, *counts):
    refs, out = list(refs), []
    for count in counts:
        out.append(refs[:count])
        refs = refs[count:]
    return out


def nest(refs, width):
    return [refs[i : i + width] for i in range(0, len(refs), width)]


def pick_kernel(radix, groups, stacks, third, *refs):
    *outs, sem = refs
    group, member = place(radix)
    copies = []
    at = 0
    for first, count in stacks:
        for delta in range(1, groups):
            for i in range(radix):
                slot = wrap(group + delta, groups) * radix + jnp.bitwise_xor(member, i)
                copies.append(
                    pltpu.make_async_copy(third.at[0, pl.ds(first, count), 0, slot], outs[at], sem.at[at])
                )
                at += 1
    for copy in copies:
        copy.start()
    for copy in copies:
        copy.wait()


def off_kernel(radix, groups, pieces, *refs):
    parts, (basis, first, second), thirds, own, other, (mid_ref,) = take(
        refs, pieces, 3, (groups - 1) * radix, radix, radix, 1
    )
    row = lax.axis_index("row")
    leaves, leaf_rows = basis.shape[2], basis.shape[3]
    rows = parts[0].shape[1]
    per_leaf = leaf_rows // rows
    leaf, order = [], []
    for t in range(leaves):
        index = jnp.bitwise_xor(lax.div(row, per_leaf), t)
        total = None
        for u in range(per_leaf):
            start = jnp.bitwise_xor(lax.rem(row, per_leaf), u) * rows
            mat = basis[0, 0, index] if per_leaf == 1 else basis[0, 0, index, pl.ds(pl.multiple_of(start, rows), rows)]
            part = dot_t(mat, parts[t * per_leaf + u][0])
            total = part if total is None else total + part
        leaf.append(total.astype(BF16))
        order.append(index)
    column_levels(
        leaf, order, first.at[0, 0, 0], second.at[0, 0, 0], nest(thirds, radix), mid_ref, own, other, 0
    )


def middle_kernel(radix, groups, *refs):
    (own_in, crossed, weights, (rhs,), (basis, first, second), thirds, (residual_ref,), own, other, (mid_ref,)) = take(
        refs, radix, groups - 1, 3, 1, 3, (groups - 1) * radix, 1, radix, radix, 1
    )
    third, fourth, out_basis = weights
    zero = row_levels(0, own_in, crossed, third.at[0, 0, 0], fourth.at[0, 0, 0], out_basis.at[0, 0], radix)
    one = row_levels(1, own_in, crossed, third.at[0, 1, 0], fourth.at[0, 1, 0], out_basis.at[0, 1], radix)
    half_rows = out_basis.shape[3]
    leaves, leaf_rows = basis.shape[2], basis.shape[3]
    leaf = []
    for h in range(len(zero)):
        span = pl.ds(h * half_rows, half_rows)
        residual = rhs[0, span].astype(F32) - zero[h] - one[h]
        residual_ref[span] = residual
        rounded = residual.astype(BF16)
        for k in range(half_rows // leaf_rows):
            leaf.append(
                dot_t(
                    basis[0, 0, h * (half_rows // leaf_rows) + k],
                    rounded[k * leaf_rows : (k + 1) * leaf_rows],
                ).astype(BF16)
            )
    column_levels(
        leaf, range(leaves), first.at[0, 0, 0], second.at[0, 0, 0], nest(thirds, radix), mid_ref, own, other, 0
    )


def last_kernel(radix, groups, *refs):
    own_in, crossed, (third, fourth, out_basis, residual, out) = take(refs, radix, groups - 1, 5)
    rows = row_levels(0, own_in, crossed, third.at[0, 0, 0], fourth.at[0, 0, 0], out_basis.at[0, 0], radix)
    half_rows = out_basis.shape[3]
    for h in range(len(rows)):
        span = pl.ds(h * half_rows, half_rows)
        out[0, span] = (residual[span] + rows[h]).astype(BF16)


def block_of(array, j, count=1):
    shape = (1, count) + array.shape[2:]
    if callable(j):
        return pl.BlockSpec(shape, lambda *at: (0, j(*at)) + (0,) * (len(shape) - 2))
    return pl.BlockSpec(shape, lambda *at: (0, j) + (0,) * (len(shape) - 2))


def whole(array):
    return pl.BlockSpec(array.shape, lambda *at: (0,) * len(array.shape))


def params():
    return pltpu.CompilerParams(vmem_limit_bytes=VMEM_LIMIT)


def cost(flops, arrays):
    return pl.CostEstimate(
        flops=int(flops), bytes_accessed=int(sum(a.size * a.dtype.itemsize for a in arrays)), transcendentals=0
    )


def on_device(
    row_size, box_size, solved, rhs, leaf_basis, first_level, second_level, third_level, fourth_level, out_basis
):
    radix = first_level.shape[4]
    groups = box_size // radix
    butterflies = leaf_basis.shape[1]
    offs = solved.shape[0]
    columns = solved.shape[2]
    rank = leaf_basis.shape[4]
    rows = rhs.shape[1]

    def over_row(array, mask):
        return lax.ppermute(array, "row", [(r, r ^ mask) for r in range(row_size)])

    def over_members(array, mask):
        pairs = [(b, (b // radix) * radix + ((b % radix) ^ mask)) for b in range(box_size)]
        return array if mask == 0 else lax.ppermute(array, "box", pairs)

    def over_groups(array, delta, mask=0):
        pairs = [
            (b, ((b // radix + delta) % groups) * radix + ((b % radix) ^ mask)) for b in range(box_size)
        ]
        return lax.ppermute(array, "box", pairs)

    pieces = {0: solved}
    for mask in range(2, row_size, 2):
        pieces[mask] = over_row(solved, mask)
    for mask in range(0, row_size, 2):
        pieces[mask + 1] = over_row(pieces[mask], 1)
    pieces = [pieces[mask] for mask in range(row_size)]

    stacks = ((0, offs), (offs, butterflies - offs))
    sent_count = (groups - 1) * radix
    picked = pl.pallas_call(
        functools.partial(pick_kernel, radix, groups, stacks),
        out_shape=[
            jax.ShapeDtypeStruct((count, rank, rank), BF16) for _, count in stacks for _ in range(sent_count)
        ],
        in_specs=[pl.BlockSpec(memory_space=pl.ANY)],
        out_specs=[pl.BlockSpec(memory_space=pl.ANY)] * (2 * sent_count),
        scratch_shapes=[pltpu.SemaphoreType.DMA((2 * sent_count,))],
        name="pick_third",
    )(third_level)
    shifts = [(delta, i) for delta in range(1, groups) for i in range(radix)]
    thirds = [over_groups(a, *shift) for a, shift in zip(picked[:sent_count], shifts)]
    thirds_last = [over_groups(a, *shift) for a, shift in zip(picked[sent_count:], shifts)]

    def levels_out(count):
        own = [jax.ShapeDtypeStruct((count, rank, columns), BF16)] * radix
        return own + [jax.ShapeDtypeStruct((count, groups - 1, rank, columns), BF16)] * radix

    def levels_specs():
        own = [pl.BlockSpec((1, rank, columns), lambda j: (j, 0, 0))] * radix
        return own + [pl.BlockSpec((1, groups - 1, rank, columns), lambda j: (j, 0, 0, 0))] * radix

    mid_scratch = pltpu.VMEM((first_level.shape[3], rank, columns), BF16)
    column_flops = 2 * columns * rank * (rows + first_level.shape[3] * radix * rank + (2 * box_size - radix) * rank)
    row_flops = 2 * columns * rank * (rows + radix * rank + 2 * groups * rank)
    weights = [leaf_basis, first_level, second_level]

    def send(levels):
        own, other = levels[:radix], levels[radix:]
        other = [over_members(a, i) for i, a in enumerate(other)]
        own = [over_members(a, i) for i, a in enumerate(own)]
        crossed = []
        for delta in range(1, groups):
            total = sum(a[:, delta - 1].astype(F32) for a in other).astype(BF16)
            crossed.append(over_groups(total, groups - delta))
        return own + crossed

    levels = pl.pallas_call(
        functools.partial(off_kernel, radix, groups, len(pieces)),
        grid=(offs,),
        out_shape=levels_out(offs),
        in_specs=[pl.BlockSpec((1,) + p.shape[1:], lambda j: (j, 0, 0)) for p in pieces]
        + [block_of(a, lambda j: j) for a in weights]
        + [pl.BlockSpec((1, rank, rank), lambda j: (j, 0, 0)) for _ in thirds],
        out_specs=levels_specs(),
        scratch_shapes=[mid_scratch],
        compiler_params=params(),
        cost_estimate=cost(offs * column_flops, pieces + thirds),
        name="off_levels",
    )(*pieces, *weights, *thirds)
    received = send(levels)

    out_weights = [third_level, fourth_level, out_basis]
    residual, *levels = pl.pallas_call(
        functools.partial(middle_kernel, radix, groups),
        grid=(1,),
        out_shape=[jax.ShapeDtypeStruct((rows, columns), F32)] + levels_out(butterflies - offs),
        in_specs=[whole(a) for a in received]
        + [block_of(a, 0, offs) for a in out_weights]
        + [whole(rhs)]
        + [block_of(a, offs) for a in weights]
        + [whole(a) for a in thirds_last],
        out_specs=[pl.BlockSpec((rows, columns), lambda j: (0, 0))] + levels_specs(),
        scratch_shapes=[mid_scratch],
        compiler_params=params(),
        cost_estimate=cost(offs * row_flops + column_flops, received + [rhs]),
        name="middle_levels",
    )(*received, *out_weights, rhs, *weights, *thirds_last)
    received = send(levels)

    return pl.pallas_call(
        functools.partial(last_kernel, radix, groups),
        grid=(1,),
        out_shape=jax.ShapeDtypeStruct((1, rows, columns), BF16),
        in_specs=[whole(a) for a in received] + [block_of(a, offs) for a in out_weights] + [whole(residual)],
        out_specs=pl.BlockSpec((1, rows, columns), lambda j: (0, 0, 0)),
        compiler_params=params(),
        cost_estimate=cost(row_flops, received + [residual]),
        name="last_levels",
    )(*received, *out_weights, residual)


def solution(mesh):
    placed = (
        P(None, ("box", "row"), None),
        P("row", "box", None),
        P("row", None, "box", None, None),
        P("row", None, "box", None, None, None, None),
        P("row", None, "box", None, None, None),
        P("row", None, "box", None, None, None),
        P("row", None, "box", None, None, None, None),
        P("row", None, "box", None, None),
    )
    return jax.shard_map(
        functools.partial(on_device, mesh.shape["row"], mesh.shape["box"]),
        mesh=mesh,
        in_specs=placed,
        out_specs=P("row", "box", None),
        check_vma=False,
    )
```

```python
import functools

import jax
import jax.numpy as jnp
from jax import lax
from jax.experimental import pallas as pl
from jax.experimental.pallas import tpu as pltpu
from jax.sharding import PartitionSpec as P

F32 = jnp.float32
BF16 = jnp.bfloat16
MIB = 1024 * 1024
CHUNKS = 1
VMEM = pl.BlockSpec(memory_space=pltpu.VMEM)


def dot(a, b):
    return jnp.dot(a, b, preferred_element_type=F32)


def dot_t(a, b):
    return lax.dot_general(a, b, (((0,), (0,)), ((), ())), preferred_element_type=F32)


def place(radix):
    box = lax.axis_index("box")
    return lax.div(box, radix), lax.rem(box, radix)


def wrap(value, size):
    return lax.rem(value + size, size)


def take(refs, *counts):
    refs, out = list(refs), []
    for count in counts:
        out.append(refs[:count])
        refs = refs[count:]
    return out


def pick_kernel(radix, groups, third, *outs):
    group, member = place(radix)
    at = 0
    for delta in range(1, groups):
        for i in range(radix):
            slot = wrap(group + delta, groups) * radix + jnp.bitwise_xor(member, i)
            for j in range(outs[at].shape[0]):
                outs[at][j] = third[0, j, 0, slot]
            at += 1


def leaf_order(row, leaves, row_size):
    per_leaf = row_size // leaves
    return [jnp.bitwise_xor(lax.div(row, per_leaf), t) for t in range(leaves)]


def column_weights(j, order, first, second, third_of, own, other, at):
    levels, radix = first.shape[3], first.shape[4]
    slots = second.shape[3]
    groups = slots // radix
    group, member = place(radix)

    def up(slot, matrix):
        level = lax.div(slot, slots // levels)
        return dot(matrix, jnp.concatenate([first[0, j, 0, level, k] for k in order], axis=1)).astype(BF16)

    for i in range(radix):
        box = jnp.bitwise_xor(member, i)
        slot = group * radix + box
        own[at, i] = up(slot, second[0, j, 0, slot])
        for delta in range(1, groups):
            slot = wrap(group - delta, groups) * radix + box
            mat = dot(third_of(delta, i, slot), second[0, j, 0, slot]).astype(BF16)
            other[at, i, delta - 1] = up(slot, mat)


def off_weights_kernel(radix, groups, offs, row_size, first, second, *refs):
    thirds, (own, other) = take(refs, (groups - 1) * radix, 2)
    order = leaf_order(lax.axis_index("row"), first.shape[4], row_size)
    for j in range(offs):
        column_weights(
            j, order, first, second, lambda delta, i, slot: thirds[(delta - 1) * radix + i][j], own, other, j
        )


def rest_weights_kernel(
    radix, groups, offs, first, second, fourth, out_basis, thirds, own, other, off_rows, last_rows
):
    column_weights(
        offs, range(first.shape[4]), first, second, lambda delta, i, slot: thirds[0, slot], own, other, 0
    )
    group, _ = place(radix)
    rank = fourth.shape[6]
    half_rows = out_basis.shape[3]
    for j in range(offs + 1):
        out, start = (off_rows, j * groups * rank) if j < offs else (last_rows, 0)
        for h in range(fourth.shape[3]):
            mats = [fourth[0, j, 0, h, wrap(group + delta, groups)] for delta in range(groups)]
            out[h * half_rows : (h + 1) * half_rows, start : start + groups * rank] = dot(
                out_basis[0, j, h], jnp.concatenate(mats, axis=1)
            ).astype(BF16)


def column_levels(leaf, own_mats, other_mats, own, other, at):
    radix, groups_less, rank, depth = other_mats.shape
    coef = dot(other_mats[...].reshape(radix * groups_less * rank, depth), leaf).astype(BF16)
    for i in range(radix):
        other[i][at] = coef[i * groups_less * rank : (i + 1) * groups_less * rank].reshape(
            groups_less, rank, coef.shape[1]
        )
    coef = dot(own_mats[...].reshape(radix * rank, depth), leaf).astype(BF16)
    for i in range(radix):
        own[i][at] = coef[i * rank : (i + 1) * rank]


def off_kernel(radix, pieces, span, basis, own_mats, other_mats, *refs):
    parts, own, other = take(refs, pieces, radix, radix)
    row = lax.axis_index("row")
    leaves, leaf_rows = basis.shape[2], basis.shape[3]
    rows = parts[0].shape[1]
    per_leaf = leaf_rows // rows
    order = leaf_order(row, leaves, pieces)
    for j in range(parts[0].shape[0]):
        leaf = []
        for t in range(leaves):
            total = None
            for u in range(per_leaf):
                start = jnp.bitwise_xor(lax.rem(row, per_leaf), u) * rows
                if per_leaf == 1:
                    mat = basis[0, j, order[t]]
                else:
                    mat = basis[0, j, order[t], pl.ds(pl.multiple_of(start, rows), rows)]
                ref = parts[t * per_leaf + u]
                data = ref[j, :, span] if ref.shape[2] > span.stop - span.start else ref[j]
                part = dot_t(mat, data)
                total = part if total is None else total + part
            leaf.append(total.astype(BF16))
        column_levels(jnp.concatenate(leaf, axis=0), own_mats.at[j], other_mats.at[j], own, other, j)


def group_coefs(j, at, own, crossed, third, radix):
    group, member = place(radix)
    mats = [third[0, j, 0, group * radix + jnp.bitwise_xor(member, i)] for i in range(radix)]
    total = dot(jnp.concatenate(mats, axis=1), jnp.concatenate([ref[at] for ref in own], axis=0))
    return [total.astype(BF16)] + [ref[at] for ref in crossed]


def middle_kernel(radix, groups, offs, span, third, rhs, basis, row_mats, own_mats, other_mats, *refs):
    own_in, crossed, (residual_ref,), own, other = take(refs, radix, groups - 1, 1, radix, radix)
    coefs = []
    for j in range(offs):
        coefs += group_coefs(j, j, own_in, crossed, third, radix)
    coefs = jnp.concatenate(coefs, axis=0)
    leaves, leaf_rows = basis.shape[2], basis.shape[3]
    leaf = []
    for k in range(leaves):
        rows = slice(k * leaf_rows, (k + 1) * leaf_rows)
        residual = rhs[0, rows, span].astype(F32) - dot(row_mats[rows], coefs)
        residual_ref[rows] = residual
        leaf.append(dot_t(basis[0, offs, k], residual.astype(BF16)).astype(BF16))
    column_levels(jnp.concatenate(leaf, axis=0), own_mats.at[0], other_mats.at[0], own, other, 0)


def last_kernel(radix, groups, offs, third, row_mats, residual, *refs):
    own_in, crossed, (out,) = take(refs, radix, groups - 1, 1)
    coefs = jnp.concatenate(group_coefs(offs, 0, own_in, crossed, third, radix), axis=0)
    out[0] = (residual[...] + dot(row_mats[...], coefs)).astype(BF16)


def on_device(
    row_size, box_size, solved, rhs, leaf_basis, first_level, second_level, third_level, fourth_level, out_basis
):
    radix = first_level.shape[4]
    groups = box_size // radix
    butterflies = leaf_basis.shape[1]
    offs = solved.shape[0]
    width = solved.shape[2] // CHUNKS
    rank = leaf_basis.shape[4]
    rows = rhs.shape[1]
    depth = radix * rank

    def over_row(array, mask):
        return lax.ppermute(array, "row", [(r, r ^ mask) for r in range(row_size)])

    def over_members(array, mask):
        pairs = [(b, (b // radix) * radix + ((b % radix) ^ mask)) for b in range(box_size)]
        return array if mask == 0 else lax.ppermute(array, "box", pairs)

    def over_groups(array, delta, mask=0):
        pairs = [
            (b, ((b // radix + delta) % groups) * radix + ((b % radix) ^ mask)) for b in range(box_size)
        ]
        return lax.ppermute(array, "box", pairs)

    def call(kernel, name, flops, outs, *args):
        outs = [jax.ShapeDtypeStruct(shape, dtype) for shape, dtype in outs]
        size = sum(a.size * a.dtype.itemsize for a in [*args, *outs])
        return pl.pallas_call(
            kernel,
            out_shape=outs,
            in_specs=[VMEM] * len(args),
            out_specs=[VMEM] * len(outs),
            compiler_params=pltpu.CompilerParams(vmem_limit_bytes=min(16 * MIB + 2 * size, 56 * MIB)),
            cost_estimate=pl.CostEstimate(flops=int(flops), bytes_accessed=int(size), transcendentals=0),
            name=name,
        )(*args)

    sent_count = (groups - 1) * radix
    shifts = [(delta, i) for delta in range(1, groups) for i in range(radix)]
    picked = call(
        functools.partial(pick_kernel, radix, groups),
        "pick_third",
        0,
        [((offs, rank, rank), BF16)] * sent_count,
        third_level,
    )
    thirds = [over_groups(a, *shift) for a, shift in zip(picked, shifts)]

    beside = over_row(solved, 1)
    chunks = []
    for c in range(CHUNKS):
        span = slice(c * width, (c + 1) * width)
        pieces = {0: solved, 1: beside}
        part = solved if CHUNKS == 1 else solved[:, :, span]
        for mask in range(2, row_size, 2):
            pieces[mask] = over_row(part, mask)
            if c == 0 and mask == 2:
                pieces[mask], *thirds[:3] = lax.optimization_barrier((pieces[mask], *thirds[:3]))
            pieces[mask + 1] = over_row(pieces[mask], 1)
        chunks.append((span, [pieces[mask] for mask in range(row_size)]))

    def column_mats(count):
        return [((count, radix, rank, depth), BF16), ((count, radix, groups - 1, rank, depth), BF16)]

    mats_flops = 2 * box_size * rank * rank * (depth + rank)
    own_mats, other_mats = call(
        functools.partial(off_weights_kernel, radix, groups, offs, row_size),
        "off_weights",
        offs * mats_flops,
        column_mats(offs),
        first_level,
        second_level,
        *thirds,
    )
    def levels_out(count):
        own = [((count, rank, width), BF16)] * radix
        return own + [((count, groups - 1, rank, width), BF16)] * radix

    def send(levels, beside=None):
        own, other = levels[:radix], levels[radix:]
        other = [over_members(a, i) for i, a in enumerate(other)]
        own = [over_members(a, i) for i, a in enumerate(own)]
        if beside is not None:
            _, last = lax.optimization_barrier((levels[radix], third_level[0, offs:, 0]))
            last = lax.all_to_all(last, "box", split_axis=1, concat_axis=1, tiled=True)
            other[0], last = lax.optimization_barrier((other[0], last))
            beside.append(last)
        crossed = []
        for delta in range(1, groups):
            total = sum(a[:, delta - 1].astype(F32) for a in other).astype(BF16)
            crossed.append(over_groups(total, groups - delta))
        return own + crossed

    column_flops = 2 * width * rank * (rows + box_size * depth)
    row_flops = 2 * width * rank * (depth + groups * rows)
    done, last_weights = [], None
    for span, pieces in chunks:
        levels = call(
            functools.partial(off_kernel, radix, row_size, span),
            "off_levels",
            offs * column_flops,
            levels_out(offs),
            leaf_basis,
            own_mats,
            other_mats,
            *pieces,
        )
        if last_weights is None:
            thirds_last = []
            received = send(levels, thirds_last)
            last_weights = call(
                functools.partial(rest_weights_kernel, radix, groups, offs),
                "rest_weights",
                mats_flops + 2 * butterflies * rows * rank * groups * rank,
                column_mats(1) + [((rows, offs * groups * rank), BF16), ((rows, groups * rank), BF16)],
                first_level,
                second_level,
                fourth_level,
                out_basis,
                thirds_last[0],
            )
        else:
            received = send(levels)
        own_last, other_last, off_rows, last_rows = last_weights
        residual, *levels = call(
            functools.partial(middle_kernel, radix, groups, offs, span),
            "middle_levels",
            offs * row_flops + column_flops,
            [((rows, width), F32)] + levels_out(butterflies - offs),
            third_level,
            rhs,
            leaf_basis,
            off_rows,
            own_last,
            other_last,
            *received,
        )
        received = send(levels)
        done += call(
            functools.partial(last_kernel, radix, groups, offs),
            "last_levels",
            row_flops,
            [((1, rows, width), BF16)],
            third_level,
            last_rows,
            residual,
            *received,
        )
    return done[0] if CHUNKS == 1 else jnp.concatenate(done, axis=2)


def solution(mesh):
    placed = (
        P(None, ("box", "row"), None),
        P("row", "box", None),
        P("row", None, "box", None, None),
        P("row", None, "box", None, None, None, None),
        P("row", None, "box", None, None, None),
        P("row", None, "box", None, None, None),
        P("row", None, "box", None, None, None, None),
        P("row", None, "box", None, None),
    )
    return jax.shard_map(
        functools.partial(on_device, mesh.shape["row"], mesh.shape["box"]),
        mesh=mesh,
        in_specs=placed,
        out_specs=P("row", "box", None),
        check_vma=False,
    )
```

```python
import functools

import jax
import jax.numpy as jnp
from jax import lax
from jax.experimental import pallas as pl
from jax.experimental.pallas import tpu as pltpu
from jax.sharding import PartitionSpec as P

F32 = jnp.float32
BF16 = jnp.bfloat16
MIB = 1024 * 1024
CHUNKS = 1
VMEM = pl.BlockSpec(memory_space=pltpu.VMEM)


def dot(a, b):
    return jnp.dot(a, b, preferred_element_type=F32)


def dot_t(a, b):
    return lax.dot_general(a, b, (((0,), (0,)), ((), ())), preferred_element_type=F32)


def place(radix):
    box = lax.axis_index("box")
    return lax.div(box, radix), lax.rem(box, radix)


def wrap(value, size):
    return lax.rem(value + size, size)


def take(refs, *counts):
    refs, out = list(refs), []
    for count in counts:
        out.append(refs[:count])
        refs = refs[count:]
    return out


def pick_kernel(radix, groups, offs, third, *outs):
    group, member = place(radix)
    at = 0
    for delta in range(1, groups):
        base = wrap(group + delta, groups) * radix
        for i in range(radix):
            for j in range(offs):
                outs[at][j] = third[0, j, 0, base + jnp.bitwise_xor(member, i)]
            at += 1
    for delta in range(1, groups):
        base = wrap(group + delta, groups) * radix
        for k in range(radix):
            outs[at][k] = third[0, offs, 0, base + k]
        at += 1


def leaf_order(row, leaves, row_size):
    per_leaf = row_size // leaves
    return [jnp.bitwise_xor(lax.div(row, per_leaf), t) for t in range(leaves)]


def weights_kernel(radix, groups, offs, row_size, first, second, fourth, out_basis, *outs):
    up_own, up_other, off_rows, last_rows = outs
    levels = first.shape[3]
    slots = second.shape[3]
    rank = fourth.shape[6]
    half_rows = out_basis.shape[3]
    group, member = place(radix)
    for j in range(first.shape[1]):
        order = leaf_order(lax.axis_index("row"), radix, row_size) if j < offs else range(radix)

        def up(slot):
            level = lax.div(slot, slots // levels)
            mats = jnp.concatenate([first[0, j, 0, level, k] for k in order], axis=1)
            return dot(second[0, j, 0, slot], mats).astype(BF16)

        for i in range(radix):
            box = jnp.bitwise_xor(member, i)
            up_own[j, i] = up(group * radix + box)
            for delta in range(1, groups):
                up_other[j, i, delta - 1] = up(wrap(group - delta, groups) * radix + box)
        out, start = (off_rows, j * groups * rank) if j < offs else (last_rows, 0)
        for h in range(fourth.shape[3]):
            mats = [fourth[0, j, 0, h, wrap(group + delta, groups)] for delta in range(groups)]
            out[h * half_rows : (h + 1) * half_rows, start : start + groups * rank] = dot(
                out_basis[0, j, h], jnp.concatenate(mats, axis=1)
            ).astype(BF16)


def other_mats(j, third_of, up_other):
    radix, less = up_other.shape[1], up_other.shape[2]
    mats = [dot(third_of(i, d), up_other[j, i, d]).astype(BF16) for i in range(radix) for d in range(less)]
    return jnp.concatenate(mats, axis=0)


def put_other(mats, leaf, other, at):
    coef = dot(mats, leaf).astype(BF16)
    for i, ref in enumerate(other):
        less, rank, width = ref.shape[1:]
        ref[at] = coef[i * less * rank : (i + 1) * less * rank].reshape(less, rank, width)


def put_own(mats, leaf, own, at):
    radix, rank, depth = mats.shape
    coef = dot(mats[...].reshape(radix * rank, depth), leaf).astype(BF16)
    tiles = leaf.shape[1] // rank
    for i, ref in enumerate(own):
        for c in range(tiles):
            ref[at * tiles + c] = coef[i * rank : (i + 1) * rank, c * rank : (c + 1) * rank]


def off_kernel(radix, groups, pieces, span, basis, up_other, *refs):
    thirds, parts, (leaf_ref,), other = take(refs, (groups - 1) * radix, pieces, 1, radix)
    row = lax.axis_index("row")
    leaves, leaf_rows = basis.shape[2], basis.shape[3]
    rows = parts[0].shape[1]
    per_leaf = leaf_rows // rows
    order = leaf_order(row, leaves, pieces)
    for j in range(parts[0].shape[0]):
        leaf = []
        for t in range(leaves):
            total = None
            for u in range(per_leaf):
                start = jnp.bitwise_xor(lax.rem(row, per_leaf), u) * rows
                if per_leaf == 1:
                    mat = basis[0, j, order[t]]
                else:
                    mat = basis[0, j, order[t], pl.ds(pl.multiple_of(start, rows), rows)]
                ref = parts[t * per_leaf + u]
                data = ref[j, :, span] if ref.shape[2] > span.stop - span.start else ref[j]
                part = dot_t(mat, data)
                total = part if total is None else total + part
            leaf.append(total.astype(BF16))
        leaf = jnp.concatenate(leaf, axis=0)
        leaf_ref[j] = leaf
        mats = other_mats(j, lambda i, d: thirds[d * radix + i][j], up_other)
        put_other(mats, leaf, other, j)


def own_kernel(radix, leaf, up_own, *refs):
    rides, own = take(refs, len(refs) - radix, radix)
    _, member = place(radix)
    offs = leaf.shape[0]
    for j in range(offs):
        put_own(up_own.at[j], leaf[j], own, j)
    for d, ride in enumerate(rides):
        for i, ref in enumerate(own):
            ref[ref.shape[0] - len(rides) + d] = ride[jnp.bitwise_xor(member, i)]


def group_coefs(j, at, tiles, own, crossed, third, radix):
    group, member = place(radix)
    mats = [third[0, j, 0, group * radix + jnp.bitwise_xor(member, i)] for i in range(radix)]
    slots = [jnp.concatenate([ref[at * tiles + c] for c in range(tiles)], axis=1) for ref in own]
    total = dot(jnp.concatenate(mats, axis=1), jnp.concatenate(slots, axis=0))
    return [total.astype(BF16)] + [ref[at] for ref in crossed]


def middle_kernel(radix, groups, offs, span, first_chunk, third, rhs, basis, row_mats, up_own, up_other, *refs):
    crossed, own_in, mats_in, (residual_ref,), own, other, mats_out = take(
        refs, groups - 1, radix, 0 if first_chunk else 1, 1, radix, radix, 1 if first_chunk else 0
    )
    rank = basis.shape[4]
    tiles = (span.stop - span.start) // rank
    if first_chunk:
        mats = other_mats(offs, lambda i, d: own_in[i][offs * tiles + d], up_other)
        mats_out[0][...] = mats
    else:
        mats = mats_in[0][...]
    coefs = []
    for j in range(offs):
        coefs += group_coefs(j, j, tiles, own_in, crossed, third, radix)
    coefs = jnp.concatenate(coefs, axis=0)
    leaves, leaf_rows = basis.shape[2], basis.shape[3]
    leaf = []
    for k in range(leaves):
        rows = slice(k * leaf_rows, (k + 1) * leaf_rows)
        residual = rhs[0, rows, span].astype(F32) - dot(row_mats[rows], coefs)
        residual_ref[rows] = residual
        leaf.append(dot_t(basis[0, offs, k], residual.astype(BF16)).astype(BF16))
    leaf = jnp.concatenate(leaf, axis=0)
    put_other(mats, leaf, other, 0)
    put_own(up_own.at[offs], leaf, own, 0)


def last_kernel(radix, groups, offs, third, row_mats, residual, *refs):
    crossed, own_in, (out,) = take(refs, groups - 1, radix, 1)
    tiles = residual.shape[1] // third.shape[5]
    coefs = jnp.concatenate(group_coefs(offs, 0, tiles, own_in, crossed, third, radix), axis=0)
    out[0] = (residual[...] + dot(row_mats[...], coefs)).astype(BF16)


def after(array, *others):
    return lax.optimization_barrier((array, *others))[0]


def on_device(
    row_size, box_size, solved, rhs, leaf_basis, first_level, second_level, third_level, fourth_level, out_basis
):
    radix = first_level.shape[4]
    groups = box_size // radix
    less = groups - 1
    butterflies = leaf_basis.shape[1]
    offs = solved.shape[0]
    width = solved.shape[2] // CHUNKS
    rank = leaf_basis.shape[4]
    rows = rhs.shape[1]
    depth = radix * rank
    tiles = width // rank

    def over_row(array, mask):
        return lax.ppermute(array, "row", [(r, r ^ mask) for r in range(row_size)])

    def over_members(array, mask):
        pairs = [(b, (b // radix) * radix + ((b % radix) ^ mask)) for b in range(box_size)]
        return array if mask == 0 else lax.ppermute(array, "box", pairs)

    def over_groups(array, delta, mask=0):
        pairs = [
            (b, ((b // radix + delta) % groups) * radix + ((b % radix) ^ mask)) for b in range(box_size)
        ]
        return lax.ppermute(array, "box", pairs)

    def call(kernel, name, flops, outs, *args):
        outs = [jax.ShapeDtypeStruct(shape, dtype) for shape, dtype in outs]
        size = sum(a.size * a.dtype.itemsize for a in [*args, *outs])
        return pl.pallas_call(
            kernel,
            out_shape=outs,
            in_specs=[VMEM] * len(args),
            out_specs=[VMEM] * len(outs),
            compiler_params=pltpu.CompilerParams(vmem_limit_bytes=min(16 * MIB + 2 * size, 56 * MIB)),
            cost_estimate=pl.CostEstimate(flops=int(flops), bytes_accessed=int(size), transcendentals=0),
            name=name,
        )(*args)

    picked = call(
        functools.partial(pick_kernel, radix, groups, offs),
        "pick_third",
        0,
        [((offs, rank, rank), BF16)] * (less * radix) + [((radix, rank, rank), BF16)] * less,
        third_level,
    )
    shifts = [(delta, i) for delta in range(1, groups) for i in range(radix)]
    thirds = [over_groups(a, *shift) for a, shift in zip(picked, shifts)]

    up_own, up_other, off_rows, last_rows = call(
        functools.partial(weights_kernel, radix, groups, offs, row_size),
        "weights",
        2 * butterflies * rank * (box_size * rank * depth + rows * groups * rank),
        [
            ((butterflies, radix, rank, depth), BF16),
            ((butterflies, radix, less, rank, depth), BF16),
            ((rows, offs * groups * rank), BF16),
            ((rows, groups * rank), BF16),
        ],
        first_level,
        second_level,
        fourth_level,
        out_basis,
    )

    beside = over_row(solved, 1)
    chunks, rides = [], None
    for c in range(CHUNKS):
        span = slice(c * width, (c + 1) * width)
        pieces = {0: solved, 1: beside}
        part = solved if CHUNKS == 1 else solved[:, :, span]
        for mask in range(2, row_size, 2):
            pieces[mask] = over_row(part, mask)
            if rides is None:
                pieces[mask] = after(pieces[mask], up_own, *thirds[: radix - 1])
                rides = [
                    over_groups(after(a, pieces[mask]), d + 1) for d, a in enumerate(picked[less * radix :])
                ]
            pieces[mask + 1] = over_row(pieces[mask], 1)
        chunks.append((span, [pieces[mask] for mask in range(row_size)]))

    def other_out(count):
        return [((count, less, rank, width), BF16)] * radix

    def own_out(count):
        return [((count, rank, rank), BF16)] * radix

    def add(other):
        other = [over_members(a, i) for i, a in enumerate(other)]
        return [sum(a[:, d].astype(F32) for a in other).astype(BF16) for d in range(less)]

    def send(own, sums):
        crossed = [over_groups(a, groups - 1 - d) for d, a in enumerate(sums)]
        return crossed + [over_members(after(a, *sums) if i else a, i) for i, a in enumerate(own)]

    other_flops = 2 * width * rank * radix * less * depth
    own_flops = 2 * width * rank * radix * depth
    leaf_flops = 2 * width * rank * rows
    row_flops = 2 * width * rank * (depth + groups * rows)
    done, mats = [], []
    for c, (span, pieces) in enumerate(chunks):
        leaf, *other = call(
            functools.partial(off_kernel, radix, groups, row_size, span),
            "off_levels",
            offs * (leaf_flops + other_flops),
            [((offs, depth, width), BF16)] + other_out(offs),
            leaf_basis,
            up_other,
            *thirds,
            *pieces,
        )
        own = call(
            functools.partial(own_kernel, radix),
            "own_levels",
            offs * own_flops,
            own_out(offs * tiles + (less if c == 0 else 0)),
            leaf,
            up_own,
            *(rides if c == 0 else []),
        )
        received = send(own, add(other))
        residual, *levels = call(
            functools.partial(middle_kernel, radix, groups, offs, span, c == 0),
            "middle_levels",
            offs * row_flops + leaf_flops + other_flops + own_flops,
            [((rows, width), F32)]
            + own_out(tiles)
            + other_out(1)
            + ([((radix * less * rank, depth), BF16)] if c == 0 else []),
            third_level,
            rhs,
            leaf_basis,
            off_rows,
            up_own,
            up_other,
            *received,
            *mats,
        )
        if c == 0:
            mats = [levels.pop()]
        received = send(levels[:radix], add(levels[radix:]))
        done += call(
            functools.partial(last_kernel, radix, groups, offs),
            "last_levels",
            row_flops,
            [((1, rows, width), BF16)],
            third_level,
            last_rows,
            residual,
            *received,
        )
    return done[0] if CHUNKS == 1 else jnp.concatenate(done, axis=2)


def solution(mesh):
    placed = (
        P(None, ("box", "row"), None),
        P("row", "box", None),
        P("row", None, "box", None, None),
        P("row", None, "box", None, None, None, None),
        P("row", None, "box", None, None, None),
        P("row", None, "box", None, None, None),
        P("row", None, "box", None, None, None, None),
        P("row", None, "box", None, None),
    )
    return jax.shard_map(
        functools.partial(on_device, mesh.shape["row"], mesh.shape["box"]),
        mesh=mesh,
        in_specs=placed,
        out_specs=P("row", "box", None),
        check_vma=False,
    )
```

```python
import functools

import jax
import jax.numpy as jnp
from jax import lax
from jax.experimental import pallas as pl
from jax.experimental.pallas import tpu as pltpu
from jax.sharding import PartitionSpec as P

F32 = jnp.float32
BF16 = jnp.bfloat16
MIB = 1024 * 1024
CHUNKS = 2
VMEM = pl.BlockSpec(memory_space=pltpu.VMEM)


def dot(a, b):
    return jnp.dot(a, b, preferred_element_type=F32)


def dot_t(a, b):
    return lax.dot_general(a, b, (((0,), (0,)), ((), ())), preferred_element_type=F32)


def place(radix):
    box = lax.axis_index("box")
    return lax.div(box, radix), lax.rem(box, radix)


def wrap(value, size):
    return lax.rem(value + size, size)


def take(refs, *counts):
    refs, out = list(refs), []
    for count in counts:
        out.append(refs[:count])
        refs = refs[count:]
    return out


def pick_kernel(radix, groups, offs, third, *outs):
    group, member = place(radix)
    at = 0
    for delta in range(1, groups):
        base = wrap(group + delta, groups) * radix
        for i in range(radix):
            for j in range(offs):
                outs[at][j] = third[0, j, 0, base + jnp.bitwise_xor(member, i)]
            at += 1
    for delta in range(1, groups):
        base = wrap(group + delta, groups) * radix
        for k in range(radix):
            outs[at][k] = third[0, offs, 0, base + k]
        at += 1


def leaf_order(row, leaves, row_size):
    per_leaf = row_size // leaves
    return [jnp.bitwise_xor(lax.div(row, per_leaf), t) for t in range(leaves)]


def weights_kernel(radix, groups, offs, row_size, first, second, fourth, out_basis, *outs):
    up_own, up_other, off_rows, last_rows = outs
    levels = first.shape[3]
    slots = second.shape[3]
    rank = fourth.shape[6]
    half_rows = out_basis.shape[3]
    group, member = place(radix)
    for j in range(first.shape[1]):
        order = leaf_order(lax.axis_index("row"), radix, row_size) if j < offs else range(radix)

        def up(slot):
            level = lax.div(slot, slots // levels)
            mats = jnp.concatenate([first[0, j, 0, level, k] for k in order], axis=1)
            return dot(second[0, j, 0, slot], mats).astype(BF16)

        for i in range(radix):
            box = jnp.bitwise_xor(member, i)
            up_own[j, i] = up(group * radix + box)
            for delta in range(1, groups):
                up_other[j, i, delta - 1] = up(wrap(group - delta, groups) * radix + box)
        out, start = (off_rows, j * groups * rank) if j < offs else (last_rows, 0)
        for h in range(fourth.shape[3]):
            mats = [fourth[0, j, 0, h, wrap(group + delta, groups)] for delta in range(groups)]
            out[h * half_rows : (h + 1) * half_rows, start : start + groups * rank] = dot(
                out_basis[0, j, h], jnp.concatenate(mats, axis=1)
            ).astype(BF16)


def other_mats(j, third_of, up_other):
    radix, less = up_other.shape[1], up_other.shape[2]
    mats = [dot(third_of(i, d), up_other[j, i, d]).astype(BF16) for i in range(radix) for d in range(less)]
    return jnp.concatenate(mats, axis=0)


def put_own(mats, members, leaf, own, at):
    rank = mats.shape[1]
    coef = dot(jnp.concatenate([mats[i] for i in members], axis=0), leaf).astype(BF16)
    tiles = leaf.shape[1] // rank
    for i, ref in enumerate(own):
        for c in range(tiles):
            ref[at * tiles + c] = coef[i * rank : (i + 1) * rank, c * rank : (c + 1) * rank]


def off_kernel(radix, groups, pieces, basis, up_other, *refs):
    thirds, parts, (leaf_ref,), outs = take(refs, (groups - 1) * radix, pieces, 1, 3 * CHUNKS)
    row = lax.axis_index("row")
    leaves, leaf_rows, rank = basis.shape[2], basis.shape[3], basis.shape[4]
    rows = parts[0].shape[1]
    per_leaf = leaf_rows // rows
    order = leaf_order(row, leaves, pieces)
    less = groups - 1
    for j in range(parts[0].shape[0]):
        leaf = []
        for t in range(leaves):
            total = None
            for u in range(per_leaf):
                start = jnp.bitwise_xor(lax.rem(row, per_leaf), u) * rows
                if per_leaf == 1:
                    mat = basis[0, j, order[t]]
                else:
                    mat = basis[0, j, order[t], pl.ds(pl.multiple_of(start, rows), rows)]
                part = dot_t(mat, parts[t * per_leaf + u][j])
                total = part if total is None else total + part
            leaf.append(total.astype(BF16))
        leaf = jnp.concatenate(leaf, axis=0)
        leaf_ref[j] = leaf
        mats = other_mats(j, lambda i, d: thirds[d * radix + i][j], up_other)
        coef = dot(mats, leaf).astype(BF16)
        width = coef.shape[1] // CHUNKS
        for c in range(CHUNKS):
            blocks = [
                coef[i * less * rank : (i + 1) * less * rank, c * width : (c + 1) * width].reshape(less, rank, width)
                for i in range(radix)
            ]
            outs[3 * c][j] = blocks[0]
            outs[3 * c + 1][j] = blocks[2]
            outs[3 * c + 2][j, 0] = blocks[1]
            outs[3 * c + 2][j, 1] = blocks[3]


def own_kernel(members, leaf, up_own, *refs):
    rides, own = take(refs, len(refs) - len(members), len(members))
    _, member = place(up_own.shape[1])
    for j in range(leaf.shape[0]):
        put_own(up_own.at[j], members, leaf[j], own, j)
    for d, ride in enumerate(rides):
        for i, ref in zip(members, own):
            ref[ref.shape[0] - len(rides) + d] = ride[jnp.bitwise_xor(member, i)]


def stage_kernel(radix, keep, got, *refs):
    *rides, out = refs
    offs, less, rank, width = keep.shape
    at = 0
    for j in range(offs):
        for d in range(less):
            total = (keep[j, d].astype(F32) + got[j, 1, d].astype(F32)).astype(BF16)
            for c in range(width // rank):
                out[at] = total[:, c * rank : (c + 1) * rank]
                at += 1
    _, member = place(radix)
    for ride in rides:
        out[at] = ride[jnp.bitwise_xor(member, 2)]
        at += 1


def total_kernel(keep, got, last, *outs):
    offs, less, rank, width = keep.shape
    tiles = width // rank
    for j in range(offs):
        for d in range(less):
            at = (j * less + d) * tiles
            part = jnp.concatenate([last[at + c] for c in range(tiles)], axis=1)
            total = keep[j, d].astype(F32) + got[j, 0, d].astype(F32) + part.astype(F32)
            outs[d][j] = total.astype(BF16)


def group_coefs(j, at, tiles, own, crossed, third, radix):
    group, member = place(radix)
    mats = [third[0, j, 0, group * radix + jnp.bitwise_xor(member, i)] for i in range(radix)]
    slots = [jnp.concatenate([ref[at * tiles + c] for c in range(tiles)], axis=1) for ref in own]
    total = dot(jnp.concatenate(mats, axis=1), jnp.concatenate(slots, axis=0))
    return [total.astype(BF16)] + [jnp.concatenate([ref[at] for ref in refs], axis=1) for refs in crossed]


def middle_kernel(radix, groups, offs, third, rhs, basis, row_mats, up_own, up_other, *refs):
    less = groups - 1
    crossed, own_in, rides, (staged, residual_ref), own, other = take(
        refs, CHUNKS * less, radix, less, 2, radix, radix
    )
    crossed = [crossed[d::less] for d in range(less)]
    rank = basis.shape[4]
    tiles = rhs.shape[2] // rank
    _, member = place(radix)

    def third_of(i, d):
        if i == 0:
            return rides[d][member]
        if i == 2:
            return staged[staged.shape[0] - less + d]
        return own_in[i][offs * tiles + d]

    coefs = []
    for j in range(offs):
        coefs += group_coefs(j, j, tiles, own_in, crossed, third, radix)
    coefs = jnp.concatenate(coefs, axis=0)
    leaves, leaf_rows = basis.shape[2], basis.shape[3]
    leaf = []
    for k in range(leaves):
        rows = slice(k * leaf_rows, (k + 1) * leaf_rows)
        residual = rhs[0, rows].astype(F32) - dot(row_mats[rows], coefs)
        residual_ref[rows] = residual
        leaf.append(dot_t(basis[0, offs, k], residual.astype(BF16)).astype(BF16))
    leaf = jnp.concatenate(leaf, axis=0)
    coef = dot(other_mats(offs, third_of, up_other), leaf).astype(BF16)
    for i, ref in enumerate(other):
        ref[0] = coef[i * less * rank : (i + 1) * less * rank].reshape(ref.shape[1:])
    put_own(up_own.at[offs], range(radix), leaf, own, 0)


def last_kernel(radix, groups, offs, third, row_mats, residual, *refs):
    crossed, own_in, (out,) = take(refs, groups - 1, radix, 1)
    crossed = [[ref] for ref in crossed]
    tiles = residual.shape[1] // third.shape[5]
    coefs = jnp.concatenate(group_coefs(offs, 0, tiles, own_in, crossed, third, radix), axis=0)
    out[0] = (residual[...] + dot(row_mats[...], coefs)).astype(BF16)


def after(array, *others):
    return lax.optimization_barrier((array, *others))[0]


def on_device(
    row_size, box_size, solved, rhs, leaf_basis, first_level, second_level, third_level, fourth_level, out_basis
):
    radix = first_level.shape[4]
    groups = box_size // radix
    less = groups - 1
    butterflies = leaf_basis.shape[1]
    offs = solved.shape[0]
    columns = solved.shape[2]
    width = columns // CHUNKS
    rank = leaf_basis.shape[4]
    rows = rhs.shape[1]
    depth = radix * rank
    tiles = columns // rank

    def over_row(array, mask):
        return lax.ppermute(array, "row", [(r, r ^ mask) for r in range(row_size)])

    def over_members(array, mask):
        pairs = [(b, (b // radix) * radix + ((b % radix) ^ mask)) for b in range(box_size)]
        return array if mask == 0 else lax.ppermute(array, "box", pairs)

    def over_groups(array, delta, mask=0):
        pairs = [
            (b, ((b // radix + delta) % groups) * radix + ((b % radix) ^ mask)) for b in range(box_size)
        ]
        return lax.ppermute(array, "box", pairs)

    def call(kernel, name, flops, outs, *args):
        outs = [jax.ShapeDtypeStruct(shape, dtype) for shape, dtype in outs]
        size = sum(a.size * a.dtype.itemsize for a in [*args, *outs])
        return pl.pallas_call(
            kernel,
            out_shape=outs,
            in_specs=[VMEM] * len(args),
            out_specs=[VMEM] * len(outs),
            compiler_params=pltpu.CompilerParams(vmem_limit_bytes=min(16 * MIB + 2 * size, 56 * MIB)),
            cost_estimate=pl.CostEstimate(flops=int(flops), bytes_accessed=int(size), transcendentals=0),
            name=name,
        )(*args)

    picked = call(
        functools.partial(pick_kernel, radix, groups, offs),
        "pick_third",
        0,
        [((offs, rank, rank), BF16)] * (less * radix) + [((radix, rank, rank), BF16)] * less,
        third_level,
    )
    up_own, up_other, off_rows, last_rows = outs
    levels = first.shape[3]
    slots = second.shape[3]
    rank = fourth.shape[6]
    half_rows = out_basis.shape[3]
    group, member = place(radix)
    for j in range(first.shape[1]):
        order = leaf_order(lax.axis_index("row"), radix, row_size) if j < offs else range(radix)

        def up(slot):
            level = lax.div(slot, slots // levels)
            mats = jnp.concatenate([first[0, j, 0, level, k] for k in order], axis=1)
            return dot(second[0, j, 0, slot], mats).astype(BF16)

        for i in range(radix):
            box = jnp.bitwise_xor(member, i)
            up_own[j, i] = up(group * radix + box)
            for delta in range(1, groups):
                up_other[j, i, delta - 1] = up(wrap(group - delta, groups) * radix + box)
        out, start = (off_rows, j * groups * rank) if j < offs else (last_rows, 0)
        for h in range(fourth.shape[3]):
            mats = [fourth[0, j, 0, h, wrap(group + delta, groups)] for delta in range(groups)]
            out[h * half_rows : (h + 1) * half_rows, start : start + groups * rank] = dot(
                out_basis[0, j, h], jnp.concatenate(mats, axis=1)
            ).astype(BF16)


def other_mats(j, third_of, up_other):
    radix, less = up_other.shape[1], up_other.shape[2]
    mats = [dot(third_of(i, d), up_other[j, i, d]).astype(BF16) for i in range(radix) for d in range(less)]
    return jnp.concatenate(mats, axis=0)


def put_own(mats, members, leaf, own, at):
    rank = mats.shape[1]
    coef = dot(jnp.concatenate([mats[i] for i in members], axis=0), leaf).astype(BF16)
    tiles = leaf.shape[1] // rank
    for i, ref in enumerate(own):
        for c in range(tiles):
            ref[at * tiles + c] = coef[i * rank : (i + 1) * rank, c * rank : (c + 1) * rank]


def off_kernel(radix, groups, pieces, basis, up_other, *refs):
    thirds, parts, (leaf_ref,), outs = take(refs, (groups - 1) * radix, pieces, 1, 3 * CHUNKS)
    row = lax.axis_index("row")
    leaves, leaf_rows, rank = basis.shape[2], basis.shape[3], basis.shape[4]
    rows = parts[0].shape[1]
    per_leaf = leaf_rows // rows
    order = leaf_order(row, leaves, pieces)
    less = groups - 1
    for j in range(parts[0].shape[0]):
        leaf = []
        for t in range(leaves):
            total = None
            for u in range(per_leaf):
                start = jnp.bitwise_xor(lax.rem(row, per_leaf), u) * rows
                if per_leaf == 1:
                    mat = basis[0, j, order[t]]
                else:
                    mat = basis[0, j, order[t], pl.ds(pl.multiple_of(start, rows), rows)]
                part = dot_t(mat, parts[t * per_leaf + u][j])
                total = part if total is None else total + part
            leaf.append(total.astype(BF16))
        leaf = jnp.concatenate(leaf, axis=0)
        leaf_ref[j] = leaf
        mats = other_mats(j, lambda i, d: thirds[d * radix + i][j], up_other)
        coef = dot(mats, leaf).astype(BF16)
        width = coef.shape[1] // CHUNKS
        for c in range(CHUNKS):
            blocks = [
                coef[i * less * rank : (i + 1) * less * rank, c * width : (c + 1) * width].reshape(less, rank, width)
                for i in range(radix)
            ]
            outs[3 * c][j] = blocks[0]
            outs[3 * c + 1][j] = blocks[2]
            outs[3 * c + 2][j, 0] = blocks[1]
            outs[3 * c + 2][j, 1] = blocks[3]


def own_kernel(members, leaf, up_own, *refs):
    rides, own = take(refs, len(refs) - len(members), len(members))
    _, member = place(up_own.shape[1])
    for j in range(leaf.shape[0]):
        put_own(up_own.at[j], members, leaf[j], own, j)
    for d, ride in enumerate(rides):
        for i, ref in zip(members, own):
            ref[ref.shape[0] - len(rides) + d] = ride[jnp.bitwise_xor(member, i)]


def stage_kernel(radix, keep, got, *refs):
    *rides, out = refs
    offs, less, rank, width = keep.shape
    at = 0
    for j in range(offs):
        for d in range(less):
            total = (keep[j, d].astype(F32) + got[j, 1, d].astype(F32)).astype(BF16)
            for c in range(width // rank):
                out[at] = total[:, c * rank : (c + 1) * rank]
                at += 1
    _, member = place(radix)
    for ride in rides:
        out[at] = ride[jnp.bitwise_xor(member, 2)]
        at += 1


def total_kernel(keep, got, last, *outs):
    offs, less, rank, width = keep.shape
    tiles = width // rank
    for j in range(offs):
        for d in range(less):
            at = (j * less + d) * tiles
            part = jnp.concatenate([last[at + c] for c in range(tiles)], axis=1)
            total = keep[j, d].astype(F32) + got[j, 0, d].astype(F32) + part.astype(F32)
            outs[d][j] = total.astype(BF16)


def group_coefs(j, at, tiles, own, crossed, third, radix):
    group, member = place(radix)
    mats = [third[0, j, 0, group * radix + jnp.bitwise_xor(member, i)] for i in range(radix)]
    slots = [jnp.concatenate([ref[at * tiles + c] for c in range(tiles)], axis=1) for ref in own]
    total = dot(jnp.concatenate(mats, axis=1), jnp.concatenate(slots, axis=0))
    return [total.astype(BF16)] + [jnp.concatenate([ref[at] for ref in refs], axis=1) for refs in crossed]


def middle_kernel(radix, groups, offs, third, rhs, basis, row_mats, up_own, up_other, *refs):
    less = groups - 1
    crossed, own_in, rides, (staged, residual_ref), own, other = take(
        refs, CHUNKS * less, radix, less, 2, radix, radix
    )
    crossed = [crossed[d::less] for d in range(less)]
    rank = basis.shape[4]
    tiles = rhs.shape[2] // rank
    _, member = place(radix)

    def third_of(i, d):
        if i == 0:
            return rides[d][member]
        if i == 2:
            return staged[staged.shape[0] - less + d]
        return own_in[i][offs * tiles + d]

    coefs = []
    for j in range(offs):
        coefs += group_coefs(j, j, tiles, own_in, crossed, third, radix)
    coefs = jnp.concatenate(coefs, axis=0)
    leaves, leaf_rows = basis.shape[2], basis.shape[3]
    leaf = []
    for k in range(leaves):
        rows = slice(k * leaf_rows, (k + 1) * leaf_rows)
        residual = rhs[0, rows].astype(F32) - dot(row_mats[rows], coefs)
        residual_ref[rows] = residual
        leaf.append(dot_t(basis[0, offs, k], residual.astype(BF16)).astype(BF16))
    leaf = jnp.concatenate(leaf, axis=0)
    coef = dot(other_mats(offs, third_of, up_other), leaf).astype(BF16)
    for i, ref in enumerate(other):
        ref[0] = coef[i * less * rank : (i + 1) * less * rank].reshape(ref.shape[1:])
    put_own(up_own.at[offs], range(radix), leaf, own, 0)


def last_kernel(radix, groups, offs, third, row_mats, residual, *refs):
    crossed, own_in, (out,) = take(refs, groups - 1, radix, 1)
    crossed = [[ref] for ref in crossed]
    tiles = residual.shape[1] // third.shape[5]
    coefs = jnp.concatenate(group_coefs(offs, 0, tiles, own_in, crossed, third, radix), axis=0)
    out[0] = (residual[...] + dot(row_mats[...], coefs)).astype(BF16)


def after(array, *others):
    return lax.optimization_barrier((array, *others))[0]


def on_device(
    row_size, box_size, solved, rhs, leaf_basis, first_level, second_level, third_level, fourth_level, out_basis
):
    radix = first_level.shape[4]
    groups = box_size // radix
    less = groups - 1
    butterflies = leaf_basis.shape[1]
    offs = solved.shape[0]
    columns = solved.shape[2]
    width = columns // CHUNKS
    rank = leaf_basis.shape[4]
    rows = rhs.shape[1]
    depth = radix * rank
    tiles = columns // rank

    def over_row(array, mask):
        return lax.ppermute(array, "row", [(r, r ^ mask) for r in range(row_size)])

    def over_members(array, mask):
        pairs = [(b, (b // radix) * radix + ((b % radix) ^ mask)) for b in range(box_size)]
        return array if mask == 0 else lax.ppermute(array, "box", pairs)

    def over_groups(array, delta, mask=0):
        pairs = [
            (b, ((b // radix + delta) % groups) * radix + ((b % radix) ^ mask)) for b in range(box_size)
        ]
        return lax.ppermute(array, "box", pairs)

    def call(kernel, name, flops, outs, *args):
        outs = [jax.ShapeDtypeStruct(shape, dtype) for shape, dtype in outs]
        size = sum(a.size * a.dtype.itemsize for a in [*args, *outs])
        return pl.pallas_call(
            kernel,
            out_shape=outs,
            in_specs=[VMEM] * len(args),
            out_specs=[VMEM] * len(outs),
            compiler_params=pltpu.CompilerParams(vmem_limit_bytes=min(16 * MIB + 2 * size, 56 * MIB)),
            cost_estimate=pl.CostEstimate(flops=int(flops), bytes_accessed=int(size), transcendentals=0),
            name=name,
        )(*args)

    picked = call(
        functools.partial(pick_kernel, radix, groups, offs),
        "pick_third",
        0,
        [((offs, rank, rank), BF16)] * (less * radix) + [((radix, rank, rank), BF16)] * less,
        third_level,
    )
    shifts = [(delta, i) for delta in range(1, groups) for i in range(radix)]
    thirds = [over_groups(a, *shift) for a, shift in zip(picked, shifts)]

    up_own, up_other, off_rows, last_rows = call(
        functools.partial(weights_kernel, radix, groups, offs, row_size),
        "weights",
        2 * butterflies * rank * (box_size * rank * depth + rows * groups * rank),
        [
            ((butterflies, radix, rank, depth), BF16),
            ((butterflies, radix, less, rank, depth), BF16),
            ((rows, offs * groups * rank), BF16),
            ((rows, groups * rank), BF16),
        ],
        first_level,
        second_level,
        fourth_level,
        out_basis,
    )

    shifts = [(delta, i) for delta in range(1, groups) for i in range(radix)]
    thirds = [over_groups(a, *shift) for a, shift in zip(picked, shifts)]
    pieces = {0: solved, 1: over_row(after(solved, thirds[0]), 1)}
    for mask in range(2, row_size, 2):
        pieces[mask] = after(over_row(solved, mask), up_own, *thirds)
        pieces[mask + 1] = over_row(pieces[mask], 1)
    rides = [over_groups(after(a, pieces[2]), d + 1) for d, a in enumerate(picked[less * radix :])]
    pieces = [pieces[mask] for mask in range(row_size)]

    own_shape = ((offs * tiles, rank, rank), BF16)
    ride_shape = ((offs * tiles + less, rank, rank), BF16)
    part = (offs, less, rank, width)
    other_flops = 2 * columns * rank * radix * less * depth
    own_flops = 2 * columns * rank * radix * depth
    leaf_flops = 2 * columns * rank * rows
    row_flops = 2 * columns * rank * (depth + groups * rows)

    leaf, *others = call(
        functools.partial(off_kernel, radix, groups, row_size),
        "off_levels",
        offs * (leaf_flops + other_flops),
        [((offs, depth, columns), BF16)]
        + [(part, BF16), (part, BF16), ((offs, 2, less, rank, width), BF16)] * CHUNKS,
        leaf_basis,
        up_other,
        *thirds,
        *pieces,
    )
    own = [None] * radix
    own[0], own[2] = call(
        functools.partial(own_kernel, (0, 2)), "own_levels", offs * own_flops // 2, [own_shape] * 2, leaf, up_own
    )
    own_along = own[2]
    own[2] = over_members(own_along, 2)
    crossed, got, staged, sums = [], None, None, []
    for c in range(CHUNKS):
        keep, wait, sent = others[3 * c : 3 * c + 3]
        got = over_members(after(sent, staged, own_along, *rides) if c else sent, 1)
        riding = rides if c == CHUNKS - 1 else []
        (staged,) = call(
            functools.partial(stage_kernel, radix),
            "stage",
            0,
            [((offs * less * width // rank + len(riding), rank, rank), BF16)],
            wait,
            after(got, *sums, own[2]) if c else got,
            *riding,
        )
        last = over_members(staged, 2)
        sums = call(
            total_kernel, "total", 0, [((offs, rank, width), BF16)] * less, keep, got, last
        )
        crossed += [over_groups(a, groups - 1 - d) for d, a in enumerate(sums)]
    own[1], own[3] = call(
        functools.partial(own_kernel, (1, 3)),
        "own_levels_last",
        offs * own_flops // 2,
        [ride_shape] * 2,
        after(leaf, staged),
        up_own,
        *rides,
    )
    own[1] = over_members(after(own[1], got), 1)
    own[3] = over_members(after(own[3], got), 3)

    residual, *levels = call(
        functools.partial(middle_kernel, radix, groups, offs),
        "middle_levels",
        offs * row_flops + leaf_flops + other_flops + own_flops,
        [((rows, columns), F32)]
        + [((tiles, rank, rank), BF16)] * radix
        + [((1, less, rank, columns), BF16)] * radix,
        third_level,
        rhs,
        leaf_basis,
        off_rows,
        up_own,
        up_other,
        *crossed,
        *own,
        *rides,
        last,
    )
    own, other = levels[:radix], levels[radix:]
    other = [over_members(a, i) for i, a in enumerate(other)]
    sums = [sum(a[:, d].astype(F32) for a in other).astype(BF16) for d in range(less)]
    crossed = [over_groups(a, groups - 1 - d) for d, a in enumerate(sums)]
    own = [over_members(after(a, *sums) if i else a, i) for i, a in enumerate(own)]
    return call(
        functools.partial(last_kernel, radix, groups, offs),
        "last_levels",
        row_flops,
        [((1, rows, columns), BF16)],
        third_level,
        last_rows,
        residual,
        *crossed,
        *own,
    )[0]


def solution(mesh):
    placed = (
        P(None, ("box", "row"), None),
        P("row", "box", None),
        P("row", None, "box", None, None),
        P("row", None, "box", None, None, None, None),
        P("row", None, "box", None, None, None),
        P("row", None, "box", None, None, None),
        P("row", None, "box", None, None, None, None),
        P("row", None, "box", None, None),
    )
    return jax.shard_map(
        functools.partial(on_device, mesh.shape["row"], mesh.shape["box"]),
        mesh=mesh,
        in_specs=placed,
        out_specs=P("row", "box", None),
        check_vma=False,
    )
```

```python
import functools

import jax
import jax.numpy as jnp
from jax import lax
from jax.experimental import pallas as pl
from jax.experimental.pallas import tpu as pltpu
from jax.sharding import PartitionSpec as P

F32 = jnp.float32
BF16 = jnp.bfloat16
MIB = 1024 * 1024
MASKS = (1, 2)
VMEM = pl.BlockSpec(memory_space=pltpu.VMEM)


def dot(a, b):
    return jnp.dot(a, b, preferred_element_type=F32)


def dot_t(a, b):
    return lax.dot_general(a, b, (((0,), (0,)), ((), ())), preferred_element_type=F32)


def place(radix):
    box = lax.axis_index("box")
    return lax.div(box, radix), lax.rem(box, radix)


def wrap(value, size):
    return lax.rem(value + size, size)


def take(refs, *counts):
    refs, out = list(refs), []
    for count in counts:
        out.append(refs[:count])
        refs = refs[count:]
    return out


def pick_kernel(radix, groups, offs, third, *outs):
    group, member = place(radix)
    at = 0
    for delta in range(1, groups):
        base = wrap(group + delta, groups) * radix
        for i in range(radix):
            for j in range(offs):
                outs[at][j] = third[0, j, 0, base + jnp.bitwise_xor(member, i)]
            at += 1
    for delta in range(1, groups):
        base = wrap(group + delta, groups) * radix
        for k in range(radix):
            outs[at][k] = third[0, offs, 0, base + k]
        at += 1


def leaf_order(row, leaves, row_size):
    per_leaf = row_size // leaves
    return [jnp.bitwise_xor(lax.div(row, per_leaf), t) for t in range(leaves)]


def weights_kernel(radix, groups, offs, row_size, first, second, fourth, out_basis, *outs):
    up_own, up_other, off_rows, last_rows = outs
    levels = first.shape[3]
    slots = second.shape[3]
    rank = fourth.shape[6]
    half_rows = out_basis.shape[3]
    group, member = place(radix)
    for j in range(first.shape[1]):
        order = leaf_order(lax.axis_index("row"), radix, row_size) if j < offs else range(radix)

        def up(slot):
            level = lax.div(slot, slots // levels)
            mats = jnp.concatenate([first[0, j, 0, level, k] for k in order], axis=1)
            return dot(second[0, j, 0, slot], mats).astype(BF16)

        for i in range(radix):
            box = jnp.bitwise_xor(member, i)
            up_own[j, i] = up(group * radix + box)
            for delta in range(1, groups):
                up_other[j, i, delta - 1] = up(wrap(group - delta, groups) * radix + box)
        out, start = (off_rows, j * groups * rank) if j < offs else (last_rows, 0)
        for h in range(fourth.shape[3]):
            mats = [fourth[0, j, 0, h, wrap(group + delta, groups)] for delta in range(groups)]
            out[h * half_rows : (h + 1) * half_rows, start : start + groups * rank] = dot(
                out_basis[0, j, h], jnp.concatenate(mats, axis=1)
            ).astype(BF16)


def other_mats(j, third_of, up_other):
    radix, less = up_other.shape[1], up_other.shape[2]
    mats = [dot(third_of(i, d), up_other[j, i, d]).astype(BF16) for i in range(radix) for d in range(less)]
    return jnp.concatenate(mats, axis=0)


def put_own(mats, members, leaf, own, at):
    rank = mats.shape[1]
    coef = dot(jnp.concatenate([mats[i] for i in members], axis=0), leaf).astype(BF16)
    tiles = leaf.shape[1] // rank
    for i, ref in enumerate(own):
        for c in range(tiles):
            ref[at * tiles + c] = coef[i * rank : (i + 1) * rank, c * rank : (c + 1) * rank]


def off_kernel(radix, groups, pieces, basis, up_other, *refs):
    thirds, parts, (leaf_ref,), outs = take(refs, (groups - 1) * radix, pieces, 1, 3 * len(MASKS))
    row = lax.axis_index("row")
    leaves, leaf_rows, rank = basis.shape[2], basis.shape[3], basis.shape[4]
    rows = parts[0].shape[1]
    per_leaf = leaf_rows // rows
    order = leaf_order(row, leaves, pieces)
    less = groups - 1
    for j in range(parts[0].shape[0]):
        leaf = []
        for t in range(leaves):
            total = None
            for u in range(per_leaf):
                start = jnp.bitwise_xor(lax.rem(row, per_leaf), u) * rows
                if per_leaf == 1:
                    mat = basis[0, j, order[t]]
                else:
                    mat = basis[0, j, order[t], pl.ds(pl.multiple_of(start, rows), rows)]
                part = dot_t(mat, parts[t * per_leaf + u][j])
                total = part if total is None else total + part
            leaf.append(total.astype(BF16))
        leaf = jnp.concatenate(leaf, axis=0)
        leaf_ref[j] = leaf
        mats = other_mats(j, lambda i, d: thirds[d * radix + i][j], up_other)
        coef = dot(mats, leaf).astype(BF16)
        width = coef.shape[1] // len(MASKS)
        for c, mask in enumerate(MASKS):
            blocks = [
                coef[i * less * rank : (i + 1) * less * rank, c * width : (c + 1) * width].reshape(less, rank, width)
                for i in range(radix)
            ]
            outs[3 * c][j] = blocks[0]
            outs[3 * c + 1][j] = blocks[3 - mask]
            outs[3 * c + 2][j, 0] = blocks[mask]
            outs[3 * c + 2][j, 1] = blocks[3]


def own_kernel(members, leaf, up_own, *refs):
    rides, own = take(refs, len(refs) - len(members), len(members))
    _, member = place(up_own.shape[1])
    for j in range(leaf.shape[0]):
        put_own(up_own.at[j], members, leaf[j], own, j)
    for d, ride in enumerate(rides):
        for i, ref in zip(members, own):
            ref[ref.shape[0] - len(rides) + d] = ride[jnp.bitwise_xor(member, i)]


def stage_kernel(keep, got, out):
    out[...] = (keep[...].astype(F32) + got[:, 1].astype(F32)).astype(BF16)


def total_kernel(*refs):
    halves, outs = refs[: 3 * len(MASKS)], refs[3 * len(MASKS) :]
    offs, less, rank, width = halves[0].shape
    for j in range(offs):
        for d in range(less):
            for c in range(len(MASKS)):
                keep, got, last = halves[3 * c : 3 * c + 3]
                total = keep[j, d].astype(F32) + got[j, 0, d].astype(F32) + last[j, d].astype(F32)
                outs[d][j, :, c * width : (c + 1) * width] = total.astype(BF16)


def group_coefs(j, at, tiles, own, crossed, third, radix):
    group, member = place(radix)
    mats = [third[0, j, 0, group * radix + jnp.bitwise_xor(member, i)] for i in range(radix)]
    slots = [jnp.concatenate([ref[at * tiles + c] for c in range(tiles)], axis=1) for ref in own]
    total = dot(jnp.concatenate(mats, axis=1), jnp.concatenate(slots, axis=0))
    return [total.astype(BF16)] + [ref[at] for ref in crossed]


def middle_kernel(radix, groups, offs, third, rhs, basis, row_mats, up_own, up_other, *refs):
    less = groups - 1
    crossed, own_in, rides, (residual_ref,), own, other = take(refs, less, radix, less, 1, radix, radix)
    rank = basis.shape[4]
    tiles = rhs.shape[2] // rank
    _, member = place(radix)

    def third_of(i, d):
        if i == 0:
            return rides[d][member]
        return own_in[i][offs * tiles + d]

    coefs = []
    for j in range(offs):
        coefs += group_coefs(j, j, tiles, own_in, crossed, third, radix)
    coefs = jnp.concatenate(coefs, axis=0)
    leaves, leaf_rows = basis.shape[2], basis.shape[3]
    leaf = []
    for k in range(leaves):
        rows = slice(k * leaf_rows, (k + 1) * leaf_rows)
        residual = rhs[0, rows].astype(F32) - dot(row_mats[rows], coefs)
        residual_ref[rows] = residual
        leaf.append(dot_t(basis[0, offs, k], residual.astype(BF16)).astype(BF16))
    leaf = jnp.concatenate(leaf, axis=0)
    coef = dot(other_mats(offs, third_of, up_other), leaf).astype(BF16)
    for i, ref in enumerate(other):
        ref[0] = coef[i * less * rank : (i + 1) * less * rank].reshape(ref.shape[1:])
    put_own(up_own.at[offs], range(radix), leaf, own, 0)


def last_kernel(radix, groups, offs, third, row_mats, residual, *refs):
    crossed, own_in, (out,) = take(refs, groups - 1, radix, 1)
    tiles = residual.shape[1] // third.shape[5]
    coefs = jnp.concatenate(group_coefs(offs, 0, tiles, own_in, crossed, third, radix), axis=0)
    out[0] = (residual[...] + dot(row_mats[...], coefs)).astype(BF16)


def after(array, *others):
    return lax.optimization_barrier((array, *others))[0]


def on_device(
    row_size, box_size, solved, rhs, leaf_basis, first_level, second_level, third_level, fourth_level, out_basis
):
    radix = first_level.shape[4]
    groups = box_size // radix
    less = groups - 1
    butterflies = leaf_basis.shape[1]
    offs = solved.shape[0]
    columns = solved.shape[2]
    width = columns // len(MASKS)
    rank = leaf_basis.shape[4]
    rows = rhs.shape[1]
    depth = radix * rank
    tiles = columns // rank

    def over_row(array, mask):
        return lax.ppermute(array, "row", [(r, r ^ mask) for r in range(row_size)])

    def over_members(array, mask):
        pairs = [(b, (b // radix) * radix + ((b % radix) ^ mask)) for b in range(box_size)]
        return array if mask == 0 else lax.ppermute(array, "box", pairs)

    def over_groups(array, delta, mask=0):
        pairs = [
            (b, ((b // radix + delta) % groups) * radix + ((b % radix) ^ mask)) for b in range(box_size)
        ]
        return lax.ppermute(array, "box", pairs)

    def call(kernel, name, flops, outs, *args):
        outs = [jax.ShapeDtypeStruct(shape, dtype) for shape, dtype in outs]
        size = sum(a.size * a.dtype.itemsize for a in [*args, *outs])
        return pl.pallas_call(
            kernel,
            out_shape=outs,
            in_specs=[VMEM] * len(args),
            out_specs=[VMEM] * len(outs),
            compiler_params=pltpu.CompilerParams(vmem_limit_bytes=min(16 * MIB + 2 * size, 56 * MIB)),
            cost_estimate=pl.CostEstimate(flops=int(flops), bytes_accessed=int(size), transcendentals=0),
            name=name,
        )(*args)

    picked = call(
        functools.partial(pick_kernel, radix, groups, offs),
        "pick_third",
        0,
        [((offs, rank, rank), BF16)] * (less * radix) + [((radix, rank, rank), BF16)] * less,
        third_level,
    )
    shifts = [(delta, i) for delta in range(1, groups) for i in range(radix)]
    thirds = [over_groups(a, *shift) for a, shift in zip(picked, shifts)]

    up_own, up_other, off_rows, last_rows = call(
        functools.partial(weights_kernel, radix, groups, offs, row_size),
        "weights",
        2 * butterflies * rank * (box_size * rank * depth + rows * groups * rank),
        [
            ((butterflies, radix, rank, depth), BF16),
            ((butterflies, radix, less, rank, depth), BF16),
            ((rows, offs * groups * rank), BF16),
            ((rows, groups * rank), BF16),
        ],
        first_level,
        second_level,
        fourth_level,
        out_basis,
    )

    shifts = [(delta, i) for delta in range(1, groups) for i in range(radix)]
    thirds = [over_groups(a, *shift) for a, shift in zip(picked, shifts)]
    pieces = {0: solved, 1: over_row(after(solved, thirds[0]), 1)}
    for mask in range(2, row_size, 2):
        pieces[mask] = after(over_row(solved, mask), up_own, *thirds)
        pieces[mask + 1] = over_row(pieces[mask], 1)
    rides = [over_groups(after(a, pieces[2]), d + 1) for d, a in enumerate(picked[less * radix :])]
    pieces = [pieces[mask] for mask in range(row_size)]

    ride_shape = ((offs * tiles + less, rank, rank), BF16)
    part = (offs, less, rank, width)
    other_flops = 2 * columns * rank * radix * less * depth
    own_flops = 2 * columns * rank * radix * depth
    leaf_flops = 2 * columns * rank * rows
    row_flops = 2 * columns * rank * (depth + groups * rows)

    leaf, *others = call(
        functools.partial(off_kernel, radix, groups, row_size),
        "off_levels",
        offs * (leaf_flops + other_flops),
        [((offs, depth, columns), BF16)]
        + [(part, BF16), (part, BF16), ((offs, 2, less, rank, width), BF16)] * len(MASKS),
        leaf_basis,
        up_other,
        *thirds,
        *pieces,
    )
    halves = []
    for c, mask in enumerate(MASKS):
        keep, wait, sent = others[3 * c : 3 * c + 3]
        got = over_members(sent, mask)
        (staged,) = call(stage_kernel, "stage", 0, [(part, BF16)], wait, after(got, *rides) if c else got)
        halves += [keep, got, over_members(staged, 3 - mask)]
    sums = call(total_kernel, "total", 0, [((offs, rank, columns), BF16)] * less, *halves)
    crossed = [over_groups(a, groups - 1 - d) for d, a in enumerate(sums)]
    own = call(
        functools.partial(own_kernel, range(radix)),
        "own_levels",
        offs * own_flops,
        [ride_shape] * radix,
        after(leaf, *sums),
        up_own,
        *rides,
    )
    own = [over_members(a, i) for i, a in enumerate(own)]

    residual, *levels = call(
        functools.partial(middle_kernel, radix, groups, offs),
        "middle_levels",
        offs * row_flops + leaf_flops + other_flops + own_flops,
        [((rows, columns), F32)]
        + [((tiles, rank, rank), BF16)] * radix
        + [((1, less, rank, columns), BF16)] * radix,
        third_level,
        rhs,
        leaf_basis,
        off_rows,
        up_own,
        up_other,
        *crossed,
        *own,
        *rides,
    )
    own, other = levels[:radix], levels[radix:]
    other = [over_members(a, i) for i, a in enumerate(other)]
    sums = [sum(a[:, d].astype(F32) for a in other).astype(BF16) for d in range(less)]
    crossed = [over_groups(a, groups - 1 - d) for d, a in enumerate(sums)]
    own = [over_members(after(a, *sums) if i else a, i) for i, a in enumerate(own)]
    return call(
        functools.partial(last_kernel, radix, groups, offs),
        "last_levels",
        row_flops,
        [((1, rows, columns), BF16)],
        third_level,
        last_rows,
        residual,
        *crossed,
        *own,
    )[0]


def solution(mesh):
    placed = (
        P(None, ("box", "row"), None),
        P("row", "box", None),
        P("row", None, "box", None, None),
        P("row", None, "box", None, None, None, None),
        P("row", None, "box", None, None, None),
        P("row", None, "box", None, None, None),
        P("row", None, "box", None, None, None, None),
        P("row", None, "box", None, None),
    )
    return jax.shard_map(
        functools.partial(on_device, mesh.shape["row"], mesh.shape["box"]),
        mesh=mesh,
        in_specs=placed,
        out_specs=P("row", "box", None),
        check_vma=False,
    )
```

```python
import functools

import jax
import jax.numpy as jnp
from jax import lax
from jax.experimental import pallas as pl
from jax.experimental.pallas import tpu as pltpu
from jax.sharding import PartitionSpec as P

F32 = jnp.float32
BF16 = jnp.bfloat16
MIB = 1024 * 1024
VMEM = pl.BlockSpec(memory_space=pltpu.VMEM)


def dot(a, b):
    return jnp.dot(a, b, preferred_element_type=F32)


def dot_t(a, b):
    return lax.dot_general(a, b, (((0,), (0,)), ((), ())), preferred_element_type=F32)


def place(radix):
    box = lax.axis_index("box")
    return lax.div(box, radix), lax.rem(box, radix)


def wrap(value, size):
    return lax.rem(value + size, size)


def take(refs, *counts):
    refs, out = list(refs), []
    for count in counts:
        out.append(refs[:count])
        refs = refs[count:]
    return out


def pick_kernel(radix, groups, offs, third, *outs):
    group, member = place(radix)
    at = 0
    for delta in range(1, groups):
        base = wrap(group + delta, groups) * radix
        for i in range(radix):
            for j in range(offs):
                outs[at][j] = third[0, j, 0, base + jnp.bitwise_xor(member, i)]
            at += 1
    for delta in range(1, groups):
        base = wrap(group + delta, groups) * radix
        for k in range(radix):
            outs[at][k] = third[0, offs, 0, base + k]
        at += 1


def leaf_order(row, leaves, row_size):
    per_leaf = row_size // leaves
    return [jnp.bitwise_xor(lax.div(row, per_leaf), t) for t in range(leaves)]


def weights_kernel(radix, groups, offs, row_size, first, second, fourth, out_basis, *outs):
    up_own, up_other, off_rows, last_rows = outs
    levels = first.shape[3]
    slots = second.shape[3]
    rank = fourth.shape[6]
    half_rows = out_basis.shape[3]
    group, member = place(radix)
    for j in range(first.shape[1]):
        order = leaf_order(lax.axis_index("row"), radix, row_size) if j < offs else range(radix)

        def up(slot):
            level = lax.div(slot, slots // levels)
            mats = jnp.concatenate([first[0, j, 0, level, k] for k in order], axis=1)
            return dot(second[0, j, 0, slot], mats).astype(BF16)

        for i in range(radix):
            box = jnp.bitwise_xor(member, i)
            up_own[j, i] = up(group * radix + box)
            for delta in range(1, groups):
                up_other[j, i, delta - 1] = up(wrap(group - delta, groups) * radix + box)
        out, start = (off_rows, j * groups * rank) if j < offs else (last_rows, 0)
        for h in range(fourth.shape[3]):
            mats = [fourth[0, j, 0, h, wrap(group + delta, groups)] for delta in range(groups)]
            out[h * half_rows : (h + 1) * half_rows, start : start + groups * rank] = dot(
                out_basis[0, j, h], jnp.concatenate(mats, axis=1)
            ).astype(BF16)


def other_mats(j, third_of, up_other):
    radix, less = up_other.shape[1], up_other.shape[2]
    mats = [dot(third_of(i, d), up_other[j, i, d]).astype(BF16) for i in range(radix) for d in range(less)]
    return jnp.concatenate(mats, axis=0)


def put_own(mats, members, leaf, own, at):
    rank = mats.shape[1]
    coef = dot(jnp.concatenate([mats[i] for i in members], axis=0), leaf).astype(BF16)
    tiles = leaf.shape[1] // rank
    for i, ref in enumerate(own):
        for c in range(tiles):
            ref[at * tiles + c] = coef[i * rank : (i + 1) * rank, c * rank : (c + 1) * rank]


def put_other(mats, leaf, other, at, member):
    radix, _, less, rank, width = other.shape
    coef = dot(mats, leaf).astype(BF16)
    for i in range(radix):
        part = coef[i * less * rank : (i + 1) * less * rank]
        other[jnp.bitwise_xor(member, i), at] = part.reshape(less, rank, width)


def off_kernel(radix, groups, pieces, basis, up_other, *refs):
    thirds, parts, (leaf_ref, other) = take(refs, (groups - 1) * radix, pieces, 2)
    _, member = place(radix)
    row = lax.axis_index("row")
    leaves, leaf_rows, rank = basis.shape[2], basis.shape[3], basis.shape[4]
    rows = parts[0].shape[1]
    per_leaf = leaf_rows // rows
    order = leaf_order(row, leaves, pieces)
    less = groups - 1
    for j in range(parts[0].shape[0]):
        leaf = []
        for t in range(leaves):
            total = None
            for u in range(per_leaf):
                start = jnp.bitwise_xor(lax.rem(row, per_leaf), u) * rows
                if per_leaf == 1:
                    mat = basis[0, j, order[t]]
                else:
                    mat = basis[0, j, order[t], pl.ds(pl.multiple_of(start, rows), rows)]
                part = dot_t(mat, parts[t * per_leaf + u][j])
                total = part if total is None else total + part
            leaf.append(total.astype(BF16))
        leaf = jnp.concatenate(leaf, axis=0)
        leaf_ref[j] = leaf
        mats = other_mats(j, lambda i, d: thirds[d * radix + i][j], up_other)
        put_other(mats, leaf, other, j, member)


def own_kernel(members, leaf, up_own, *refs):
    rides, own = take(refs, len(refs) - len(members), len(members))
    _, member = place(up_own.shape[1])
    for j in range(leaf.shape[0]):
        put_own(up_own.at[j], members, leaf[j], own, j)
    for d, ride in enumerate(rides):
        for i, ref in zip(members, own):
            ref[ref.shape[0] - len(rides) + d] = ride[jnp.bitwise_xor(member, i)]


def group_coefs(j, at, tiles, own, crossed, third, radix):
    group, member = place(radix)
    mats = [third[0, j, 0, group * radix + jnp.bitwise_xor(member, i)] for i in range(radix)]
    slots = [jnp.concatenate([ref[at * tiles + c] for c in range(tiles)], axis=1) for ref in own]
    total = dot(jnp.concatenate(mats, axis=1), jnp.concatenate(slots, axis=0))
    return [total.astype(BF16)] + [ref[at] for ref in crossed]


def middle_kernel(radix, groups, offs, third, rhs, basis, row_mats, up_own, up_other, *refs):
    less = groups - 1
    crossed, own_in, rides, (residual_ref, other), own = take(refs, less, radix, less, 2, radix)
    rank = basis.shape[4]
    tiles = rhs.shape[2] // rank
    _, member = place(radix)

    def third_of(i, d):
        if i == 0:
            return rides[d][member]
        return own_in[i][offs * tiles + d]

    coefs = []
    for j in range(offs):
        coefs += group_coefs(j, j, tiles, own_in, crossed, third, radix)
    coefs = jnp.concatenate(coefs, axis=0)
    leaves, leaf_rows = basis.shape[2], basis.shape[3]
    leaf = []
    for k in range(leaves):
        rows = slice(k * leaf_rows, (k + 1) * leaf_rows)
        residual = rhs[0, rows].astype(F32) - dot(row_mats[rows], coefs)
        residual_ref[rows] = residual
        leaf.append(dot_t(basis[0, offs, k], residual.astype(BF16)).astype(BF16))
    leaf = jnp.concatenate(leaf, axis=0)
    put_other(other_mats(offs, third_of, up_other), leaf, other, 0, member)
    put_own(up_own.at[offs], range(radix), leaf, own, 0)


def last_kernel(radix, groups, offs, third, row_mats, residual, *refs):
    crossed, own_in, (out,) = take(refs, groups - 1, radix, 1)
    tiles = residual.shape[1] // third.shape[5]
    coefs = jnp.concatenate(group_coefs(offs, 0, tiles, own_in, crossed, third, radix), axis=0)
    out[0] = (residual[...] + dot(row_mats[...], coefs)).astype(BF16)


def after(array, *others):
    return lax.optimization_barrier((array, *others))[0]


def on_device(
    row_size, box_size, solved, rhs, leaf_basis, first_level, second_level, third_level, fourth_level, out_basis
):
    radix = first_level.shape[4]
    groups = box_size // radix
    less = groups - 1
    butterflies = leaf_basis.shape[1]
    offs = solved.shape[0]
    columns = solved.shape[2]
    rank = leaf_basis.shape[4]
    rows = rhs.shape[1]
    depth = radix * rank
    tiles = columns // rank

    def over_row(array, mask):
        return lax.ppermute(array, "row", [(r, r ^ mask) for r in range(row_size)])

    def over_members(array, mask):
        pairs = [(b, (b // radix) * radix + ((b % radix) ^ mask)) for b in range(box_size)]
        return array if mask == 0 else lax.ppermute(array, "box", pairs)

    def over_groups(array, delta, mask=0):
        pairs = [
            (b, ((b // radix + delta) % groups) * radix + ((b % radix) ^ mask)) for b in range(box_size)
        ]
        return lax.ppermute(array, "box", pairs)

    def call(kernel, name, flops, outs, *args):
        outs = [jax.ShapeDtypeStruct(shape, dtype) for shape, dtype in outs]
        size = sum(a.size * a.dtype.itemsize for a in [*args, *outs])
        return pl.pallas_call(
            kernel,
            out_shape=outs,
            in_specs=[VMEM] * len(args),
            out_specs=[VMEM] * len(outs),
            compiler_params=pltpu.CompilerParams(vmem_limit_bytes=min(16 * MIB + 2 * size, 56 * MIB)),
            cost_estimate=pl.CostEstimate(flops=int(flops), bytes_accessed=int(size), transcendentals=0),
            name=name,
        )(*args)

    picked = call(
        functools.partial(pick_kernel, radix, groups, offs),
        "pick_third",
        0,
        [((offs, rank, rank), BF16)] * (less * radix) + [((radix, rank, rank), BF16)] * less,
        third_level,
    )
    up_own, up_other, off_rows, last_rows = call(
        functools.partial(weights_kernel, radix, groups, offs, row_size),
        "weights",
        2 * butterflies * rank * (box_size * rank * depth + rows * groups * rank),
        [
            ((butterflies, radix, rank, depth), BF16),
            ((butterflies, radix, less, rank, depth), BF16),
            ((rows, offs * groups * rank), BF16),
            ((rows, groups * rank), BF16),
        ],
        first_level,
        second_level,
        fourth_level,
        out_basis,
    )

    shifts = [(delta, i) for delta in range(1, groups) for i in range(radix)]
    thirds = [over_groups(a, *shift) for a, shift in zip(picked, shifts)]
    pieces = {0: solved, 1: over_row(after(solved, thirds[0]), 1)}
    for mask in range(2, row_size, 2):
        pieces[mask] = after(over_row(solved, mask), up_own, *thirds)
        pieces[mask + 1] = over_row(pieces[mask], 1)
    rides = [over_groups(after(a, pieces[2]), d + 1) for d, a in enumerate(picked[less * radix :])]
    pieces = [pieces[mask] for mask in range(row_size)]

    ride_shape = ((offs * tiles + less, rank, rank), BF16)
    other_flops = 2 * columns * rank * radix * less * depth
    own_flops = 2 * columns * rank * radix * depth
    leaf_flops = 2 * columns * rank * rows
    row_flops = 2 * columns * rank * (depth + groups * rows)

    def add(other):
        index_groups = [list(range(g * radix, (g + 1) * radix)) for g in range(groups)]
        total = lax.psum_scatter(other, "box", scatter_dimension=0, axis_index_groups=index_groups)
        return [over_groups(total[:, d], less - d) for d in range(less)], total

    leaf, other = call(
        functools.partial(off_kernel, radix, groups, row_size),
        "off_levels",
        offs * (leaf_flops + other_flops),
        [((offs, depth, columns), BF16)]
        + [((radix, offs, less, rank, columns), BF16)],
        leaf_basis,
        up_other,
        *thirds,
        *pieces,
    )
    crossed, total = add(other)
    own = call(
        functools.partial(own_kernel, range(radix)),
        "own_levels",
        offs * own_flops,
        [ride_shape] * radix,
        after(leaf, total),
        up_own,
        *rides,
    )
    own = [over_members(a, i) for i, a in enumerate(own)]

    residual, other, *own = call(
        functools.partial(middle_kernel, radix, groups, offs),
        "middle_levels",
        offs * row_flops + leaf_flops + other_flops + own_flops,
        [((rows, columns), F32)]
        + [((radix, 1, less, rank, columns), BF16)]
        + [((tiles, rank, rank), BF16)] * radix,
        third_level,
        rhs,
        leaf_basis,
        off_rows,
        up_own,
        up_other,
        *crossed,
        *own,
        *rides,
    )
    crossed, total = add(other)
    own = [over_members(after(a, total) if i else a, i) for i, a in enumerate(own)]
    return call(
        functools.partial(last_kernel, radix, groups, offs),
        "last_levels",
        row_flops,
        [((1, rows, columns), BF16)],
        third_level,
        last_rows,
        residual,
        *crossed,
        *own,
    )[0]


def solution(mesh):
    placed = (
        P(None, ("box", "row"), None),
        P("row", "box", None),
        P("row", None, "box", None, None),
        P("row", None, "box", None, None, None, None),
        P("row", None, "box", None, None, None),
        P("row", None, "box", None, None, None),
        P("row", None, "box", None, None, None, None),
        P("row", None, "box", None, None),
    )
    return jax.shard_map(
        functools.partial(on_device, mesh.shape["row"], mesh.shape["box"]),
        mesh=mesh,
        in_specs=placed,
        out_specs=P("row", "box", None),
        check_vma=False,
    )
```

```python
import functools

import jax
import jax.numpy as jnp
from jax import lax
from jax.experimental import pallas as pl
from jax.experimental.pallas import tpu as pltpu
from jax.sharding import PartitionSpec as P

F32 = jnp.float32
BF16 = jnp.bfloat16
MIB = 1024 * 1024
VMEM = pl.BlockSpec(memory_space=pltpu.VMEM)


def dot(a, b):
    return jnp.dot(a, b, preferred_element_type=F32)


def dot_t(a, b):
    return lax.dot_general(a, b, (((0,), (0,)), ((), ())), preferred_element_type=F32)


def place(radix):
    box = lax.axis_index("box")
    return lax.div(box, radix), lax.rem(box, radix)


def wrap(value, size):
    return lax.rem(value + size, size)


def take(refs, *counts):
    refs, out = list(refs), []
    for count in counts:
        out.append(refs[:count])
        refs = refs[count:]
    return out


def pick_kernel(radix, groups, third, *outs):
    group, _ = place(radix)
    at = 0
    for j in range(third.shape[1]):
        for delta in range(1, groups):
            base = wrap(group + delta, groups) * radix
            for k in range(radix):
                outs[at][k] = third[0, j, 0, base + k]
            at += 1


def share_kernel(radix, *refs):
    rides, outs = take(refs, len(refs) - radix + 1, radix - 1)
    _, member = place(radix)
    for d, ride in enumerate(rides):
        for i, ref in enumerate(outs):
            ref[d] = ride[jnp.bitwise_xor(member, i + 1)]


def leaf_order(row, leaves, row_size):
    per_leaf = row_size // leaves
    return [jnp.bitwise_xor(lax.div(row, per_leaf), t) for t in range(leaves)]


def weights_kernel(radix, groups, offs, row_size, first, second, fourth, out_basis, *outs):
    up_own, up_other, off_rows, last_rows = outs
    levels = first.shape[3]
    slots = second.shape[3]
    rank = fourth.shape[6]
    half_rows = out_basis.shape[3]
    group, member = place(radix)
    for j in range(first.shape[1]):
        order = leaf_order(lax.axis_index("row"), radix, row_size) if j < offs else range(radix)

        def up(slot):
            level = lax.div(slot, slots // levels)
            mats = jnp.concatenate([first[0, j, 0, level, k] for k in order], axis=1)
            return dot(second[0, j, 0, slot], mats).astype(BF16)

        for i in range(radix):
            box = jnp.bitwise_xor(member, i)
            up_own[j, i] = up(group * radix + box)
            for delta in range(1, groups):
                up_other[j, i, delta - 1] = up(wrap(group - delta, groups) * radix + box)
        out, start = (off_rows, j * groups * rank) if j < offs else (last_rows, 0)
        for h in range(fourth.shape[3]):
            mats = [fourth[0, j, 0, h, wrap(group + delta, groups)] for delta in range(groups)]
            out[h * half_rows : (h + 1) * half_rows, start : start + groups * rank] = dot(
                out_basis[0, j, h], jnp.concatenate(mats, axis=1)
            ).astype(BF16)


def other_mats(j, third_of, up_other):
    radix, less = up_other.shape[1], up_other.shape[2]
    mats = [dot(third_of(i, d), up_other[j, i, d]).astype(BF16) for i in range(radix) for d in range(less)]
    return jnp.concatenate(mats, axis=0)


def put_own(mats, members, leaf, own, at):
    rank = mats.shape[1]
    coef = dot(jnp.concatenate([mats[i] for i in members], axis=0), leaf).astype(BF16)
    tiles = leaf.shape[1] // rank
    for i, ref in enumerate(own):
        for c in range(tiles):
            ref[at * tiles + c] = coef[i * rank : (i + 1) * rank, c * rank : (c + 1) * rank]


def off_kernel(j, radix, groups, pieces, basis, up_other, *refs):
    rides, shared, parts, (leaf_ref, keep, wait, sent) = take(refs, groups - 1, radix - 1, pieces, 4)
    row = lax.axis_index("row")
    _, member = place(radix)
    leaves, leaf_rows, rank = basis.shape[2], basis.shape[3], basis.shape[4]
    rows = parts[0].shape[-2]
    per_leaf = leaf_rows // rows
    order = leaf_order(row, leaves, pieces)
    less = groups - 1
    leaf = []
    for t in range(leaves):
        total = None
        for u in range(per_leaf):
            start = jnp.bitwise_xor(lax.rem(row, per_leaf), u) * rows
            if per_leaf == 1:
                mat = basis[0, j, order[t]]
            else:
                mat = basis[0, j, order[t], pl.ds(pl.multiple_of(start, rows), rows)]
            ref = parts[t * per_leaf + u]
            part = dot_t(mat, ref[j] if ref.shape[0] > 1 else ref[0])
            total = part if total is None else total + part
        leaf.append(total.astype(BF16))
    leaf = jnp.concatenate(leaf, axis=0)
    leaf_ref[...] = leaf
    mats = other_mats(j, lambda i, d: rides[d][member] if i == 0 else shared[i - 1][d], up_other)
    coef = dot(mats, leaf).astype(BF16)
    blocks = [
        coef[i * less * rank : (i + 1) * less * rank].reshape(less, rank, coef.shape[1]) for i in range(radix)
    ]
    keep[...] = blocks[0]
    wait[...] = blocks[2]
    sent[0] = blocks[1]
    sent[1] = blocks[3]


def own_kernel(j, radix, leaf, up_own, *refs):
    rides, own = take(refs, len(refs) - radix, radix)
    _, member = place(radix)
    put_own(up_own.at[j], range(radix), leaf[...], own, 0)
    for d, ride in enumerate(rides):
        for i, ref in enumerate(own):
            ref[ref.shape[0] - len(rides) + d] = ride[jnp.bitwise_xor(member, i)]


def stage_kernel(wait, got, out):
    out[...] = (wait[...].astype(F32) + got[1].astype(F32)).astype(BF16)


def total_kernel(keep, got, last, *outs):
    for d, out in enumerate(outs):
        out[...] = (keep[d].astype(F32) + got[0, d].astype(F32) + last[d].astype(F32)).astype(BF16)


def group_coefs(j, own, crossed, third, radix):
    rank = third.shape[5]
    tiles = crossed[0].shape[-1] // rank
    group, member = place(radix)
    mats = [third[0, j, 0, group * radix + jnp.bitwise_xor(member, i)] for i in range(radix)]
    slots = [jnp.concatenate([ref[c] for c in range(tiles)], axis=1) for ref in own]
    total = dot(jnp.concatenate(mats, axis=1), jnp.concatenate(slots, axis=0))
    return [total.astype(BF16)] + [ref[...] for ref in crossed]


def middle_kernel(radix, groups, offs, third, rhs, basis, row_mats, up_own, up_other, *refs):
    less = groups - 1
    crossed, own_in, rides, (residual_ref,), own, other = take(
        refs, offs * less, offs * radix, less, 1, radix, radix
    )
    rank = basis.shape[4]
    tiles = rhs.shape[2] // rank
    _, member = place(radix)

    def third_of(i, d):
        return rides[d][member] if i == 0 else own_in[(offs - 1) * radix + i][tiles + d]

    coefs = []
    for j in range(offs):
        coefs += group_coefs(
            j, own_in[j * radix : (j + 1) * radix], crossed[j * less : (j + 1) * less], third, radix
        )
    coefs = jnp.concatenate(coefs, axis=0)
    leaves, leaf_rows = basis.shape[2], basis.shape[3]
    leaf = []
    for k in range(leaves):
        rows = slice(k * leaf_rows, (k + 1) * leaf_rows)
        residual = rhs[0, rows].astype(F32) - dot(row_mats[rows], coefs)
        residual_ref[rows] = residual
        leaf.append(dot_t(basis[0, offs, k], residual.astype(BF16)).astype(BF16))
    leaf = jnp.concatenate(leaf, axis=0)
    coef = dot(other_mats(offs, third_of, up_other), leaf).astype(BF16)
    for i, ref in enumerate(other):
        ref[...] = coef[i * less * rank : (i + 1) * less * rank].reshape(ref.shape)
    put_own(up_own.at[offs], range(radix), leaf, own, 0)


def last_kernel(radix, groups, offs, third, row_mats, residual, *refs):
    crossed, own_in, (out,) = take(refs, groups - 1, radix, 1)
    coefs = jnp.concatenate(group_coefs(offs, own_in, crossed, third, radix), axis=0)
    out[0] = (residual[...] + dot(row_mats[...], coefs)).astype(BF16)


def after(array, *others):
    return lax.optimization_barrier((array, *others))[0]


def on_device(
    row_size, box_size, solved, rhs, leaf_basis, first_level, second_level, third_level, fourth_level, out_basis
):
    radix = first_level.shape[4]
    groups = box_size // radix
    less = groups - 1
    butterflies = leaf_basis.shape[1]
    offs = solved.shape[0]
    columns = solved.shape[2]
    rank = leaf_basis.shape[4]
    rows = rhs.shape[1]
    depth = radix * rank
    tiles = columns // rank

    def over_row(array, mask):
        return lax.ppermute(array, "row", [(r, r ^ mask) for r in range(row_size)])

    def over_members(array, mask):
        pairs = [(b, (b // radix) * radix + ((b % radix) ^ mask)) for b in range(box_size)]
        return array if mask == 0 else lax.ppermute(array, "box", pairs)

    def over_groups(array, delta, mask=0):
        pairs = [
            (b, ((b // radix + delta) % groups) * radix + ((b % radix) ^ mask)) for b in range(box_size)
        ]
        return lax.ppermute(array, "box", pairs)

    def call(kernel, name, flops, outs, *args):
        outs = [jax.ShapeDtypeStruct(shape, dtype) for shape, dtype in outs]
        size = sum(a.size * a.dtype.itemsize for a in [*args, *outs])
        return pl.pallas_call(
            kernel,
            out_shape=outs,
            in_specs=[VMEM] * len(args),
            out_specs=[VMEM] * len(outs),
            compiler_params=pltpu.CompilerParams(vmem_limit_bytes=min(16 * MIB + 2 * size, 56 * MIB)),
            cost_estimate=pl.CostEstimate(flops=int(flops), bytes_accessed=0, transcendentals=0),
            name=name,
        )(*args)

    picked = call(
        functools.partial(pick_kernel, radix, groups),
        "pick_third",
        0,
        [((radix, rank, rank), BF16)] * (butterflies * less),
        third_level,
    )
    picked = [picked[j * less : (j + 1) * less] for j in range(butterflies)]

    up_own, up_other, off_rows, last_rows = call(
        functools.partial(weights_kernel, radix, groups, offs, row_size),
        "weights",
        2 * butterflies * rank * (box_size * rank * depth + rows * groups * rank),
        [
            ((butterflies, radix, rank, depth), BF16),
            ((butterflies, radix, less, rank, depth), BF16),
            ((rows, offs * groups * rank), BF16),
            ((rows, groups * rank), BF16),
        ],
        first_level,
        second_level,
        fourth_level,
        out_basis,
    )

    part = (less, rank, columns)
    other_flops = 2 * columns * rank * radix * less * depth
    own_flops = 2 * columns * rank * radix * depth
    leaf_flops = 2 * columns * rank * rows
    row_flops = 2 * columns * rank * (depth + groups * rows)

    beside = over_row(solved, 1)

    def fetch(j, *come):
        rides = [over_groups(after(a, *come), d + 1) for d, a in enumerate(picked[j])]
        far = []
        if j < offs:
            far = [over_row(after(solved[j : j + 1], *come[:row_size]), mask) for mask in range(2, row_size, 2)]
        return rides, far

    rides, far = fetch(0)
    held = [up_own]
    crossed, owns = [], []
    for j in range(offs):
        far = [after(a, *held, *rides) for a in far]
        shared = call(
            functools.partial(share_kernel, radix),
            "share",
            0,
            [((less, rank, rank), BF16)] * (radix - 1),
            *[after(a, *held) for a in rides],
        )
        shared = [over_members(a, i + 1) for i, a in enumerate(shared)]
        pieces = [solved, beside]
        for a in far:
            pieces += [a, over_row(a, 1)]
        leaf, keep, wait, sent = call(
            functools.partial(off_kernel, j, radix, groups, row_size),
            "off_levels",
            leaf_flops + other_flops,
            [((depth, columns), BF16), (part, BF16), (part, BF16), ((2, *part), BF16)],
            leaf_basis,
            up_other,
            *rides,
            *shared,
            *pieces,
        )
        rides, far = fetch(j + 1, *far, *rides, *shared)
        final = j == offs - 1
        got = over_members(after(sent, *(owns[0][2:] if final else [])), 1)
        (staged,) = call(stage_kernel, "stage", 0, [(part, BF16)], wait, after(got, *rides, *far))
        last = over_members(staged, 2)
        sums = call(total_kernel, "total", 0, [(part[1:], BF16)] * less, keep, got, after(last, *crossed))
        crossed += [over_groups(a, less - d) for d, a in enumerate(sums)]
        own = call(
            functools.partial(own_kernel, j, radix),
            "own_levels",
            own_flops,
            [((tiles + (less if final else 0), rank, rank), BF16)] * radix,
            after(leaf, got) if final else leaf,
            up_own,
            *(rides if final else []),
        )
        owns.append([own[0], own[1]] + [over_members(a, i) for i, a in enumerate(own) if i > 1])
        held = [staged]
    for own in owns:
        own[1] = over_members(after(own[1], got), 1)

    residual, *levels = call(
        functools.partial(middle_kernel, radix, groups, offs),
        "middle_levels",
        offs * row_flops + leaf_flops + other_flops + own_flops,
        [((rows, columns), F32)] + [((tiles, rank, rank), BF16)] * radix + [(part, BF16)] * radix,
        third_level,
        rhs,
        leaf_basis,
        off_rows,
        up_own,
        up_other,
        *crossed,
        *[a for own in owns for a in own],
        *rides,
    )
    own, other = levels[:radix], levels[radix:]
    other = [over_members(a, i) for i, a in enumerate(other)]
    sums = [sum(a[d].astype(F32) for a in other).astype(BF16) for d in range(less)]
    crossed = [over_groups(a, less - d) for d, a in enumerate(sums)]
    own = [over_members(after(a, *sums) if i else a, i) for i, a in enumerate(own)]
    return call(
        functools.partial(last_kernel, radix, groups, offs),
        "last_levels",
        row_flops,
        [((1, rows, columns), BF16)],
        third_level,
        last_rows,
        residual,
        *crossed,
        *own,
    )[0]


def solution(mesh):
    placed = (
        P(None, ("box", "row"), None),
        P("row", "box", None),
        P("row", None, "box", None, None),
        P("row", None, "box", None, None, None, None),
        P("row", None, "box", None, None, None),
        P("row", None, "box", None, None, None),
        P("row", None, "box", None, None, None, None),
        P("row", None, "box", None, None),
    )
    return jax.shard_map(
        functools.partial(on_device, mesh.shape["row"], mesh.shape["box"]),
        mesh=mesh,
        in_specs=placed,
        out_specs=P("row", "box", None),
        check_vma=False,
    )
```

```python
import functools

import jax
import jax.numpy as jnp
from jax import lax
from jax.experimental import pallas as pl
from jax.experimental.pallas import tpu as pltpu
from jax.sharding import PartitionSpec as P

F32 = jnp.float32
BF16 = jnp.bfloat16
MIB = 1024 * 1024
VMEM = pl.BlockSpec(memory_space=pltpu.VMEM)


def dot(a, b):
    return jnp.dot(a, b, preferred_element_type=F32)


def dot_t(a, b):
    return lax.dot_general(a, b, (((0,), (0,)), ((), ())), preferred_element_type=F32)


def place(radix):
    box = lax.axis_index("box")
    return lax.div(box, radix), lax.rem(box, radix)


def wrap(value, size):
    return lax.rem(value + size, size)


def take(refs, *counts):
    refs, out = list(refs), []
    for count in counts:
        out.append(refs[:count])
        refs = refs[count:]
    return out


def pick_kernel(radix, groups, third, *outs):
    group, _ = place(radix)
    start = 0
    for at, out in enumerate(outs):
        base = wrap(group + at % (groups - 1) + 1, groups) * radix
        for j in range(out.shape[0]):
            for k in range(radix):
                out[j, k] = third[0, start + j, 0, base + k]
        start += out.shape[0] if at % (groups - 1) == groups - 2 else 0


def leaf_order(row, leaves, row_size):
    per_leaf = row_size // leaves
    return [jnp.bitwise_xor(lax.div(row, per_leaf), t) for t in range(leaves)]


def weights_kernel(radix, groups, offs, row_size, first, second, fourth, out_basis, *outs):
    up_own, up_other, off_rows, last_rows = outs
    levels = first.shape[3]
    slots = second.shape[3]
    rank = fourth.shape[6]
    half_rows = out_basis.shape[3]
    group, member = place(radix)
    for j in range(first.shape[1]):
        order = leaf_order(lax.axis_index("row"), radix, row_size) if j < offs else range(radix)

        def up(slot):
            level = lax.div(slot, slots // levels)
            mats = jnp.concatenate([first[0, j, 0, level, k] for k in order], axis=1)
            return dot(second[0, j, 0, slot], mats).astype(BF16)

        for i in range(radix):
            box = jnp.bitwise_xor(member, i)
            up_own[j, i] = up(group * radix + box)
            for delta in range(1, groups):
                up_other[j, i, delta - 1] = up(wrap(group - delta, groups) * radix + box)
        out, start = (off_rows, j * groups * rank) if j < offs else (last_rows, 0)
        for h in range(fourth.shape[3]):
            mats = [fourth[0, j, 0, h, wrap(group + delta, groups)] for delta in range(groups)]
            out[h * half_rows : (h + 1) * half_rows, start : start + groups * rank] = dot(
                out_basis[0, j, h], jnp.concatenate(mats, axis=1)
            ).astype(BF16)


def put_other(mats, leaf, other, at):
    radix, less, rank, depth = mats.shape
    coef = dot(mats[...].reshape(radix * less * rank, depth), leaf).astype(BF16)
    for i, ref in enumerate(other):
        ref[at] = coef[i * less * rank : (i + 1) * less * rank].reshape(ref.shape[1:])


def put_own(mats, leaf, own, at):
    radix, rank, depth = mats.shape
    coef = dot(mats[...].reshape(radix * rank, depth), leaf).astype(BF16)
    for i, ref in enumerate(own):
        ref[at] = coef[i * rank : (i + 1) * rank]


def off_kernel(radix, pieces, basis, up_other, *refs):
    parts, (leaf_ref,), other = take(refs, pieces, 1, radix)
    row = lax.axis_index("row")
    leaves, leaf_rows = basis.shape[2], basis.shape[3]
    rows = parts[0].shape[1]
    per_leaf = leaf_rows // rows
    order = leaf_order(row, leaves, pieces)
    for j in range(parts[0].shape[0]):
        leaf = []
        for t in range(leaves):
            total = None
            for u in range(per_leaf):
                start = jnp.bitwise_xor(lax.rem(row, per_leaf), u) * rows
                if per_leaf == 1:
                    mat = basis[0, j, order[t]]
                else:
                    mat = basis[0, j, order[t], pl.ds(pl.multiple_of(start, rows), rows)]
                part = dot_t(mat, parts[t * per_leaf + u][j])
                total = part if total is None else total + part
            leaf.append(total.astype(BF16))
        leaf = jnp.concatenate(leaf, axis=0)
        leaf_ref[j] = leaf
        put_other(up_other.at[j], leaf, other, j)


def own_kernel(leaf, up_own, *own):
    for j in range(leaf.shape[0]):
        put_own(up_own.at[j], leaf[j], own, j)


def sum_kernel(radix, *refs):
    got, thirds, outs = take(refs, radix, (len(refs) - radix) // 2, (len(refs) - radix) // 2)
    _, member = place(radix)
    for d, (third, out) in enumerate(zip(thirds, outs)):
        for j in range(out.shape[0]):
            mats = [third[j, jnp.bitwise_xor(member, i)] for i in range(radix)]
            slots = jnp.concatenate([ref[j, d] for ref in got], axis=0)
            out[j] = dot(jnp.concatenate(mats, axis=1), slots).astype(BF16)


def group_coefs(j, at, own, crossed, third, radix):
    group, member = place(radix)
    mats = [third[0, j, 0, group * radix + jnp.bitwise_xor(member, i)] for i in range(radix)]
    total = dot(jnp.concatenate(mats, axis=1), jnp.concatenate([ref[at] for ref in own], axis=0))
    return [total.astype(BF16)] + [ref[at] for ref in crossed]


def middle_kernel(radix, groups, offs, third, rhs, basis, row_mats, up_own, up_other, *refs):
    crossed, own_in, (residual_ref,), own, other = take(refs, groups - 1, radix, 1, radix, radix)
    coefs = []
    for j in range(offs):
        coefs += group_coefs(j, j, own_in, crossed, third, radix)
    coefs = jnp.concatenate(coefs, axis=0)
    leaves, leaf_rows = basis.shape[2], basis.shape[3]
    leaf = []
    for k in range(leaves):
        rows = slice(k * leaf_rows, (k + 1) * leaf_rows)
        residual = rhs[0, rows].astype(F32) - dot(row_mats[rows], coefs)
        residual_ref[rows] = residual
        leaf.append(dot_t(basis[0, offs, k], residual.astype(BF16)).astype(BF16))
    leaf = jnp.concatenate(leaf, axis=0)
    put_other(up_other.at[offs], leaf, other, 0)
    put_own(up_own.at[offs], leaf, own, 0)


def last_kernel(radix, groups, offs, third, row_mats, residual, *refs):
    crossed, own_in, (out,) = take(refs, groups - 1, radix, 1)
    coefs = jnp.concatenate(group_coefs(offs, 0, own_in, crossed, third, radix), axis=0)
    out[0] = (residual[...] + dot(row_mats[...], coefs)).astype(BF16)


def after(array, *others):
    return lax.optimization_barrier((array, *others))[0]


def on_device(
    row_size, box_size, solved, rhs, leaf_basis, first_level, second_level, third_level, fourth_level, out_basis
):
    radix = first_level.shape[4]
    groups = box_size // radix
    less = groups - 1
    butterflies = leaf_basis.shape[1]
    offs = solved.shape[0]
    columns = solved.shape[2]
    rank = leaf_basis.shape[4]
    rows = rhs.shape[1]
    depth = radix * rank

    def over_row(array, mask):
        return lax.ppermute(array, "row", [(r, r ^ mask) for r in range(row_size)])

    def over_members(array, mask):
        pairs = [(b, (b // radix) * radix + ((b % radix) ^ mask)) for b in range(box_size)]
        return array if mask == 0 else lax.ppermute(array, "box", pairs)

    def over_groups(array, delta, mask=0):
        pairs = [
            (b, ((b // radix + delta) % groups) * radix + ((b % radix) ^ mask)) for b in range(box_size)
        ]
        return lax.ppermute(array, "box", pairs)

    def call(kernel, name, flops, outs, *args):
        outs = [jax.ShapeDtypeStruct(shape, dtype) for shape, dtype in outs]
        size = sum(a.size * a.dtype.itemsize for a in [*args, *outs])
        return pl.pallas_call(
            kernel,
            out_shape=outs,
            in_specs=[VMEM] * len(args),
            out_specs=[VMEM] * len(outs),
            compiler_params=pltpu.CompilerParams(vmem_limit_bytes=min(16 * MIB + 2 * size, 56 * MIB)),
            cost_estimate=pl.CostEstimate(flops=int(flops), bytes_accessed=0, transcendentals=0),
            name=name,
        )(*args)

    picked = call(
        functools.partial(pick_kernel, radix, groups),
        "pick_third",
        0,
        [((offs, radix, rank, rank), BF16)] * less + [((butterflies - offs, radix, rank, rank), BF16)] * less,
        third_level,
    )
    thirds = [over_groups(a, d + 1) for d, a in enumerate(picked[:less])]
    thirds_last = [over_groups(after(a, *thirds), d + 1) for d, a in enumerate(picked[less:])]

    up_own, up_other, off_rows, last_rows = call(
        functools.partial(weights_kernel, radix, groups, offs, row_size),
        "weights",
        2 * butterflies * rank * (box_size * rank * depth + rows * groups * rank),
        [
            ((butterflies, radix, rank, depth), BF16),
            ((butterflies, radix, less, rank, depth), BF16),
            ((rows, offs * groups * rank), BF16),
            ((rows, groups * rank), BF16),
        ],
        first_level,
        second_level,
        fourth_level,
        out_basis,
    )

    pieces = [solved, over_row(solved, 1)]
    for mask in range(2, row_size, 2):
        far = after(over_row(solved, mask), up_own, *thirds)
        pieces += [far, over_row(far, 1)]

    other_flops = 2 * columns * rank * radix * less * depth
    own_flops = 2 * columns * rank * radix * depth
    leaf_flops = 2 * columns * rank * rows
    row_flops = 2 * columns * rank * (depth + groups * rows)

    def own_out(count):
        return [((count, rank, columns), BF16)] * radix

    def other_out(count):
        return [((count, less, rank, columns), BF16)] * radix

    def add(other, thirds):
        other = [over_members(a, i) for i, a in enumerate(other)]
        count = other[0].shape[0]
        sums = call(
            functools.partial(sum_kernel, radix),
            "sums",
            count * less * 2 * columns * rank * depth,
            [((count, rank, columns), BF16)] * less,
            *other,
            *thirds,
        )
        return sums, [over_groups(a, less - d) for d, a in enumerate(sums)]

    leaf, *other = call(
        functools.partial(off_kernel, radix, row_size),
        "off_levels",
        offs * (leaf_flops + other_flops),
        [((offs, depth, columns), BF16)] + other_out(offs),
        leaf_basis,
        up_other,
        *pieces,
    )
    own = call(own_kernel, "own_levels", offs * own_flops, own_out(offs), after(leaf, *thirds_last), up_own)
    sums, crossed = add(other, thirds)
    own = [over_members(after(a, *sums) if i else a, i) for i, a in enumerate(own)]

    residual, *levels = call(
        functools.partial(middle_kernel, radix, groups, offs),
        "middle_levels",
        offs * row_flops + leaf_flops + other_flops + own_flops,
        [((rows, columns), F32)] + own_out(1) + other_out(1),
        third_level,
        rhs,
        leaf_basis,
        off_rows,
        up_own,
        up_other,
        *crossed,
        *own,
    )
    own, other = levels[:radix], levels[radix:]
    sums, crossed = add(other, thirds_last)
    own = [over_members(after(a, *sums) if i else a, i) for i, a in enumerate(own)]
    return call(
        functools.partial(last_kernel, radix, groups, offs),
        "last_levels",
        row_flops,
        [((1, rows, columns), BF16)],
        third_level,
        last_rows,
        residual,
        *crossed,
        *own,
    )[0]


def solution(mesh):
    placed = (
        P(None, ("box", "row"), None),
        P("row", "box", None),
        P("row", None, "box", None, None),
        P("row", None, "box", None, None, None, None),
        P("row", None, "box", None, None, None),
        P("row", None, "box", None, None, None),
        P("row", None, "box", None, None, None, None),
        P("row", None, "box", None, None),
    )
    return jax.shard_map(
        functools.partial(on_device, mesh.shape["row"], mesh.shape["box"]),
        mesh=mesh,
        in_specs=placed,
        out_specs=P("row", "box", None),
        check_vma=False,
    )
```

```python
import functools

import jax
import jax.numpy as jnp
from jax import lax
from jax.experimental import pallas as pl
from jax.experimental.pallas import tpu as pltpu
from jax.sharding import PartitionSpec as P

F32 = jnp.float32
BF16 = jnp.bfloat16
MIB = 1024 * 1024
VMEM = pl.BlockSpec(memory_space=pltpu.VMEM)


def dot(a, b):
    return jnp.dot(a, b, preferred_element_type=F32)


def dot_t(a, b):
    return lax.dot_general(a, b, (((0,), (0,)), ((), ())), preferred_element_type=F32)


def place(radix):
    box = lax.axis_index("box")
    return lax.div(box, radix), lax.rem(box, radix)


def wrap(value, size):
    return lax.rem(value + size, size)


def take(refs, *counts):
    refs, out = list(refs), []
    for count in counts:
        out.append(refs[:count])
        refs = refs[count:]
    return out


def pick_kernel(radix, groups, third, *refs):
    *outs, sem = refs
    group, _ = place(radix)
    copies = []
    for delta, out in enumerate(outs, 1):
        base = wrap(group + delta, groups) * radix
        copies.append(pltpu.make_async_copy(third.at[0, :, 0, pl.ds(base, radix)], out, sem.at[delta - 1]))
    for copy in copies:
        copy.start()
    for copy in copies:
        copy.wait()


def leaf_order(row, leaves, row_size):
    per_leaf = row_size // leaves
    return [jnp.bitwise_xor(lax.div(row, per_leaf), t) for t in range(leaves)]


def weights_kernel(radix, groups, offs, row_size, first, second, fourth, out_basis, *outs):
    up_own, up_other, off_rows, last_rows = outs
    levels = first.shape[3]
    slots = second.shape[3]
    rank = fourth.shape[6]
    half_rows = out_basis.shape[3]
    group, member = place(radix)
    for j in range(first.shape[1]):
        order = leaf_order(lax.axis_index("row"), radix, row_size) if j < offs else range(radix)

        def up(slot):
            level = lax.div(slot, slots // levels)
            mats = jnp.concatenate([first[0, j, 0, level, k] for k in order], axis=1)
            return dot(second[0, j, 0, slot], mats).astype(BF16)

        for i in range(radix):
            box = jnp.bitwise_xor(member, i)
            up_own[j, i] = up(group * radix + box)
            for delta in range(1, groups):
                up_other[j, i, delta - 1] = up(wrap(group - delta, groups) * radix + box)
        out, start = (off_rows, j * groups * rank) if j < offs else (last_rows, 0)
        for h in range(fourth.shape[3]):
            mats = [fourth[0, j, 0, h, wrap(group + delta, groups)] for delta in range(groups)]
            out[h * half_rows : (h + 1) * half_rows, start : start + groups * rank] = dot(
                out_basis[0, j, h], jnp.concatenate(mats, axis=1)
            ).astype(BF16)


def put_other(mats, leaf, other, at):
    radix, less, rank, depth = mats.shape
    coef = dot(mats[...].reshape(radix * less * rank, depth), leaf).astype(BF16)
    for i, ref in enumerate(other):
        ref[at] = coef[i * less * rank : (i + 1) * less * rank].reshape(ref.shape[1:])


def put_own(mats, leaf, own, at):
    radix, rank, depth = mats.shape
    coef = dot(mats[...].reshape(radix * rank, depth), leaf).astype(BF16)
    for i, ref in enumerate(own):
        ref[at] = coef[i * rank : (i + 1) * rank]


def off_kernel(radix, pieces, basis, up_other, *refs):
    parts, (leaf_ref,), other = take(refs, len(refs) - 1 - radix, 1, radix)
    offs = parts[0].shape[0]
    parts = [[ref.at[j] for j in range(offs)] for ref in parts[:2]] + [
        [ref.at[j] for j in range(offs)] if ref.shape[0] == offs else ref for ref in parts[2:]
    ]
    flat, parts = parts, []
    while flat:
        if isinstance(flat[0], list):
            parts.append(flat.pop(0))
        else:
            parts.append([ref.at[0] for ref in flat[:offs]])
            flat = flat[offs:]
    row = lax.axis_index("row")
    leaves, leaf_rows = basis.shape[2], basis.shape[3]
    rows = parts[0][0].shape[0]
    per_leaf = leaf_rows // rows
    order = leaf_order(row, leaves, pieces)
    for j in range(offs):
        leaf = []
        for t in range(leaves):
            total = None
            for u in range(per_leaf):
                start = jnp.bitwise_xor(lax.rem(row, per_leaf), u) * rows
                if per_leaf == 1:
                    mat = basis[0, j, order[t]]
                else:
                    mat = basis[0, j, order[t], pl.ds(pl.multiple_of(start, rows), rows)]
                part = dot_t(mat, parts[t * per_leaf + u][j][...])
                total = part if total is None else total + part
            leaf.append(total.astype(BF16))
        leaf = jnp.concatenate(leaf, axis=0)
        leaf_ref[j] = leaf
        put_other(up_other.at[j], leaf, other, j)


def own_kernel(leaf, up_own, *own):
    for j in range(leaf.shape[0]):
        put_own(up_own.at[j], leaf[j], own, j)


def sum_kernel(radix, start, *refs):
    got, thirds, outs = take(refs, radix, (len(refs) - radix) // 2, (len(refs) - radix) // 2)
    got = got[::-1]
    _, member = place(radix)
    for d, (third, out) in enumerate(zip(thirds, outs)):
        for j in range(out.shape[0]):
            mats = [third[start + j, jnp.bitwise_xor(member, i)] for i in range(radix)]
            slots = jnp.concatenate([ref[j, d] for ref in got], axis=0)
            out[j] = dot(jnp.concatenate(mats, axis=1), slots).astype(BF16)


def group_coefs(j, at, own, crossed, third, radix):
    group, member = place(radix)
    mats = [third[0, j, 0, group * radix + jnp.bitwise_xor(member, i)] for i in range(radix)]
    total = dot(jnp.concatenate(mats, axis=1), jnp.concatenate([ref[at] for ref in own], axis=0))
    return [total.astype(BF16)] + [ref[at] for ref in crossed]


def middle_kernel(radix, groups, offs, third, rhs, basis, row_mats, up_own, up_other, *refs):
    crossed, own_in, (residual_ref,), own, other = take(refs, groups - 1, radix, 1, radix, radix)
    coefs = []
    for j in range(offs):
        coefs += group_coefs(j, j, own_in, crossed, third, radix)
    coefs = jnp.concatenate(coefs, axis=0)
    leaves, leaf_rows = basis.shape[2], basis.shape[3]
    leaf = []
    for k in range(leaves):
        rows = slice(k * leaf_rows, (k + 1) * leaf_rows)
        residual = rhs[0, rows].astype(F32) - dot(row_mats[rows], coefs)
        residual_ref[rows] = residual
        leaf.append(dot_t(basis[0, offs, k], residual.astype(BF16)).astype(BF16))
    leaf = jnp.concatenate(leaf, axis=0)
    put_other(up_other.at[offs], leaf, other, 0)
    put_own(up_own.at[offs], leaf, own, 0)


def last_kernel(radix, groups, offs, third, row_mats, residual, *refs):
    crossed, own_in, (out,) = take(refs, groups - 1, radix, 1)
    own_in = own_in[::-1]
    coefs = jnp.concatenate(group_coefs(offs, 0, own_in, crossed, third, radix), axis=0)
    out[0] = (residual[...] + dot(row_mats[...], coefs)).astype(BF16)


def after(array, *others):
    return lax.optimization_barrier((array, *others))[0]


def on_device(
    row_size, box_size, solved, rhs, leaf_basis, first_level, second_level, third_level, fourth_level, out_basis
):
    radix = first_level.shape[4]
    groups = box_size // radix
    less = groups - 1
    butterflies = leaf_basis.shape[1]
    offs = solved.shape[0]
    columns = solved.shape[2]
    rank = leaf_basis.shape[4]
    rows = rhs.shape[1]
    depth = radix * rank

    def over_row(array, mask):
        return lax.ppermute(array, "row", [(r, r ^ mask) for r in range(row_size)])

    def over_members(array, mask):
        pairs = [(b, (b // radix) * radix + ((b % radix) ^ mask)) for b in range(box_size)]
        return array if mask == 0 else lax.ppermute(array, "box", pairs)

    def over_groups(array, delta, mask=0):
        pairs = [
            (b, ((b // radix + delta) % groups) * radix + ((b % radix) ^ mask)) for b in range(box_size)
        ]
        return lax.ppermute(array, "box", pairs)

    def call(kernel, name, flops, outs, *args):
        outs = [jax.ShapeDtypeStruct(shape, dtype) for shape, dtype in outs]
        size = sum(a.size * a.dtype.itemsize for a in [*args, *outs])
        return pl.pallas_call(
            kernel,
            out_shape=outs,
            in_specs=[VMEM] * len(args),
            out_specs=[VMEM] * len(outs),
            compiler_params=pltpu.CompilerParams(vmem_limit_bytes=min(16 * MIB + 2 * size, 56 * MIB)),
            cost_estimate=pl.CostEstimate(flops=int(flops), bytes_accessed=0, transcendentals=0),
            name=name,
        )(*args)

    picked = pl.pallas_call(
        functools.partial(pick_kernel, radix, groups),
        out_shape=[jax.ShapeDtypeStruct((butterflies, radix, rank, rank), BF16)] * less,
        in_specs=[pl.BlockSpec(memory_space=pltpu.HBM)],
        out_specs=[VMEM] * less,
        scratch_shapes=[pltpu.SemaphoreType.DMA((less,))],
        name="pick_third",
    )(third_level)
    thirds = [over_groups(a, d + 1) for d, a in enumerate(picked)]

    up_own, up_other, off_rows, last_rows = call(
        functools.partial(weights_kernel, radix, groups, offs, row_size),
        "weights",
        2 * butterflies * rank * (box_size * rank * depth + rows * groups * rank),
        [
            ((butterflies, radix, rank, depth), BF16),
            ((butterflies, radix, less, rank, depth), BF16),
            ((rows, offs * groups * rank), BF16),
            ((rows, groups * rank), BF16),
        ],
        first_level,
        second_level,
        fourth_level,
        out_basis,
    )

    pieces = [solved, over_row(solved, 1)]
    for mask in range(2, row_size, 2):
        far = after(over_row(solved, mask), up_own)
        pieces += [far, [over_row(far[j : j + 1], 1) for j in range(offs)]]

    other_flops = 2 * columns * rank * radix * less * depth
    own_flops = 2 * columns * rank * radix * depth
    leaf_flops = 2 * columns * rank * rows
    row_flops = 2 * columns * rank * (depth + groups * rows)

    def own_out(count):
        return [((count, rank, columns), BF16)] * radix

    def other_out(count):
        return [((count, less, rank, columns), BF16)] * radix

    def add(other, thirds, start):
        other = [over_members(a, i) for i, a in reversed(list(enumerate(other)))][::-1]
        count = other[0].shape[0]
        sums = call(
            functools.partial(sum_kernel, radix, start),
            "sums",
            count * less * 2 * columns * rank * depth,
            [((count, rank, columns), BF16)] * less,
            *other[::-1],
            *thirds,
        )
        return sums, [over_groups(a, less - d) for d, a in enumerate(sums)]

    leaf, *other = call(
        functools.partial(off_kernel, radix, row_size),
        "off_levels",
        offs * (leaf_flops + other_flops),
        [((offs, depth, columns), BF16)] + other_out(offs),
        leaf_basis,
        up_other,
        after(solved, *thirds),
        *[a for piece in pieces[1:] for a in (piece if isinstance(piece, list) else [piece])],
    )
    own = call(own_kernel, "own_levels", offs * own_flops, own_out(offs), leaf, up_own)
    sums, crossed = add(other, thirds, 0)
    own = [over_members(after(a, *sums) if i else a, i) for i, a in enumerate(own)]

    residual, *levels = call(
        functools.partial(middle_kernel, radix, groups, offs),
        "middle_levels",
        offs * row_flops + leaf_flops + other_flops + own_flops,
        [((rows, columns), F32)] + own_out(1) + other_out(1),
        third_level,
        rhs,
        leaf_basis,
        off_rows,
        up_own,
        up_other,
        *crossed,
        *own,
    )
    own, other = levels[:radix], levels[radix:]
    sums, crossed = add(other, thirds, offs)
    own = [over_members(after(a, *sums) if i else a, i) for i, a in enumerate(own)]
    return call(
        functools.partial(last_kernel, radix, groups, offs),
        "last_levels",
        row_flops,
        [((1, rows, columns), BF16)],
        third_level,
        last_rows,
        residual,
        *crossed,
        *own[::-1],
    )[0]


def solution(mesh):
    placed = (
        P(None, ("box", "row"), None),
        P("row", "box", None),
        P("row", None, "box", None, None),
        P("row", None, "box", None, None, None, None),
        P("row", None, "box", None, None, None),
        P("row", None, "box", None, None, None),
        P("row", None, "box", None, None, None, None),
        P("row", None, "box", None, None),
    )
    return jax.shard_map(
        functools.partial(on_device, mesh.shape["row"], mesh.shape["box"]),
        mesh=mesh,
        in_specs=placed,
        out_specs=P("row", "box", None),
        check_vma=False,
    )
```

```python
import functools

import jax
import jax.numpy as jnp
from jax import lax
from jax.experimental import pallas as pl
from jax.experimental.pallas import tpu as pltpu
from jax.sharding import PartitionSpec as P

F32 = jnp.float32
BF16 = jnp.bfloat16
MIB = 1024 * 1024
ACROSS, ALONG, BOTH = 1, 2, 3
VMEM = pl.BlockSpec(memory_space=pltpu.VMEM)


def dot(a, b):
    return jnp.dot(a, b, preferred_element_type=F32)


def dot_t(a, b):
    return lax.dot_general(a, b, (((0,), (0,)), ((), ())), preferred_element_type=F32)


def place(radix):
    box = lax.axis_index("box")
    return lax.div(box, radix), lax.rem(box, radix)


def wrap(value, size):
    return lax.rem(value + size, size)


def take(refs, *counts):
    refs, out = list(refs), []
    for count in counts:
        out.append(refs[:count])
        refs = refs[count:]
    return out


def pick_kernel(radix, groups, third, *outs):
    group, _ = place(radix)
    start = 0
    for at, out in enumerate(outs):
        base = wrap(group + at % (groups - 1) + 1, groups) * radix
        for j in range(out.shape[0]):
            for k in range(radix):
                out[j, k] = third[0, start + j, 0, base + k]
        start += out.shape[0] if at % (groups - 1) == groups - 2 else 0


def second_kernel(radix, groups, second, *outs):
    group, member = place(radix)
    for i, out in zip((ALONG, BOTH), outs):
        for j in range(out.shape[0]):
            for delta in range(groups):
                out[j, delta] = second[0, j, 0, wrap(group - delta, groups) * radix + jnp.bitwise_xor(member, i)]


def leaf_order(row, leaves, row_size):
    per_leaf = row_size // leaves
    return [jnp.bitwise_xor(lax.div(row, per_leaf), t) for t in range(leaves)]


def weights_kernel(radix, groups, offs, row_size, first, second, fourth, out_basis, *outs):
    up_own, up_other, up_mid, off_rows, last_rows = outs
    levels = first.shape[3]
    slots = second.shape[3]
    rank = fourth.shape[6]
    half_rows = out_basis.shape[3]
    group, member = place(radix)
    for j in range(first.shape[1]):
        order = leaf_order(lax.axis_index("row"), radix, row_size) if j < offs else range(radix)

        def up(slot):
            level = lax.div(slot, slots // levels)
            mats = jnp.concatenate([first[0, j, 0, level, k] for k in order], axis=1)
            return dot(second[0, j, 0, slot], mats).astype(BF16)

        for i in range(radix):
            box = jnp.bitwise_xor(member, i)
            up_own[j, i] = up(group * radix + box)
            for delta in range(1, groups):
                up_other[j, i, delta - 1] = up(wrap(group - delta, groups) * radix + box)
        if j < offs:
            for delta in range(groups):
                slot = wrap(group - delta, groups) * radix + jnp.bitwise_xor(member, ALONG)
                level = lax.div(slot, slots // levels)
                up_mid[j, delta] = jnp.concatenate([first[0, j, 0, level, k] for k in order], axis=1)
        out, start = (off_rows, j * groups * rank) if j < offs else (last_rows, 0)
        for h in range(fourth.shape[3]):
            mats = [fourth[0, j, 0, h, wrap(group + delta, groups)] for delta in range(groups)]
            out[h * half_rows : (h + 1) * half_rows, start : start + groups * rank] = dot(
                out_basis[0, j, h], jnp.concatenate(mats, axis=1)
            ).astype(BF16)


def put_other(mats, leaf, other, at):
    radix, less, rank, depth = mats.shape
    coef = dot(mats[...].reshape(radix * less * rank, depth), leaf).astype(BF16)
    for i, ref in enumerate(other):
        ref[at] = coef[i * less * rank : (i + 1) * less * rank].reshape(ref.shape[1:])


def put_own(mats, leaf, own, at):
    radix, rank, depth = mats.shape
    coef = dot(mats[...].reshape(radix * rank, depth), leaf).astype(BF16)
    for i, ref in enumerate(own):
        ref[at] = coef[i * rank : (i + 1) * rank]


def off_kernel(pieces, basis, up_other, up_mid, *refs):
    parts, (leaf_ref, keep, across, along) = take(refs, pieces, 4)
    row = lax.axis_index("row")
    leaves, leaf_rows = basis.shape[2], basis.shape[3]
    rows = parts[0].shape[1]
    per_leaf = leaf_rows // rows
    order = leaf_order(row, leaves, pieces)
    less, rank, columns = keep.shape[1:]
    for j in range(parts[0].shape[0]):
        leaf = []
        for t in range(leaves):
            total = None
            for u in range(per_leaf):
                start = jnp.bitwise_xor(lax.rem(row, per_leaf), u) * rows
                if per_leaf == 1:
                    mat = basis[0, j, order[t]]
                else:
                    mat = basis[0, j, order[t], pl.ds(pl.multiple_of(start, rows), rows)]
                part = dot_t(mat, parts[t * per_leaf + u][j])
                total = part if total is None else total + part
            leaf.append(total.astype(BF16))
        leaf = jnp.concatenate(leaf, axis=0)
        leaf_ref[j] = leaf
        mats = [up_other[j, 0], up_other[j, ACROSS], up_mid[j, 1:]]
        mats = jnp.concatenate([m.reshape(less * rank, m.shape[2]) for m in mats], axis=0)
        coef = dot(mats, leaf).astype(BF16)
        for i, ref in enumerate((keep, across, along)):
            ref[j] = coef[i * less * rank : (i + 1) * less * rank].reshape(less, rank, columns)


def own_kernel(leaf, up_own, up_mid, *own):
    rank = up_mid.shape[2]
    for j in range(leaf.shape[0]):
        coef = dot(jnp.concatenate([up_own[j, 0], up_own[j, ACROSS], up_mid[j, 0]], axis=0), leaf[j]).astype(BF16)
        for i, ref in enumerate(own):
            ref[j] = coef[i * rank : (i + 1) * rank]


def slots_of(got, second_along, second_both, j, delta):
    keep, across, along, both = got
    return jnp.concatenate(
        [
            keep,
            across,
            dot(second_along[j, delta], along).astype(BF16),
            dot(second_both[j, delta], both).astype(BF16),
        ],
        axis=0,
    )


def off_sum_kernel(second_along, second_both, *refs):
    got, thirds, outs = take(refs, 4, (len(refs) - 4) // 2, (len(refs) - 4) // 2)
    radix = thirds[0].shape[1]
    _, member = place(radix)
    for d, (third, out) in enumerate(zip(thirds, outs)):
        for j in range(out.shape[0]):
            mats = [third[j, jnp.bitwise_xor(member, i)] for i in range(radix)]
            slots = slots_of([ref[j, d] for ref in got], second_along, second_both, j, d + 1)
            out[j] = dot(jnp.concatenate(mats, axis=1), slots).astype(BF16)


def sum_kernel(radix, *refs):
    got, thirds, outs = take(refs, radix, (len(refs) - radix) // 2, (len(refs) - radix) // 2)
    got = got[::-1]
    _, member = place(radix)
    for d, (third, out) in enumerate(zip(thirds, outs)):
        for j in range(out.shape[0]):
            mats = [third[j, jnp.bitwise_xor(member, i)] for i in range(radix)]
            slots = jnp.concatenate([ref[j, d] for ref in got], axis=0)
            out[j] = dot(jnp.concatenate(mats, axis=1), slots).astype(BF16)


def group_coef(j, slots, third, radix):
    group, member = place(radix)
    mats = [third[0, j, 0, group * radix + jnp.bitwise_xor(member, i)] for i in range(radix)]
    return dot(jnp.concatenate(mats, axis=1), slots).astype(BF16)


def middle_kernel(
    radix, groups, offs, third, rhs, basis, row_mats, up_own, up_other, second_along, second_both, *refs
):
    crossed, own_in, (residual_ref,), own, other = take(refs, groups - 1, radix, 1, radix, radix)
    coefs = []
    for j in range(offs):
        slots = slots_of([ref[j] for ref in own_in], second_along, second_both, j, 0)
        coefs += [group_coef(j, slots, third, radix)] + [ref[j] for ref in crossed]
    coefs = jnp.concatenate(coefs, axis=0)
    leaves, leaf_rows = basis.shape[2], basis.shape[3]
    leaf = []
    for k in range(leaves):
        rows = slice(k * leaf_rows, (k + 1) * leaf_rows)
        residual = rhs[0, rows].astype(F32) - dot(row_mats[rows], coefs)
        residual_ref[rows] = residual
        leaf.append(dot_t(basis[0, offs, k], residual.astype(BF16)).astype(BF16))
    leaf = jnp.concatenate(leaf, axis=0)
    put_other(up_other.at[offs], leaf, other, 0)
    put_own(up_own.at[offs], leaf, own, 0)


def last_kernel(radix, groups, offs, third, row_mats, residual, *refs):
    crossed, own_in, (out,) = take(refs, groups - 1, radix, 1)
    own_in = own_in[::-1]
    slots = jnp.concatenate([ref[0] for ref in own_in], axis=0)
    coefs = [group_coef(offs, slots, third, radix)] + [ref[0] for ref in crossed]
    coefs = jnp.concatenate(coefs, axis=0)
    out[0] = (residual[...] + dot(row_mats[...], coefs)).astype(BF16)


def after(array, *others):
    return lax.optimization_barrier((array, *others))[0]


def on_device(
    row_size, box_size, solved, rhs, leaf_basis, first_level, second_level, third_level, fourth_level, out_basis
):
    radix = first_level.shape[4]
    groups = box_size // radix
    less = groups - 1
    butterflies = leaf_basis.shape[1]
    offs = solved.shape[0]
    columns = solved.shape[2]
    rank = leaf_basis.shape[4]
    rows = rhs.shape[1]
    depth = radix * rank

    def over_row(array, mask):
        return lax.ppermute(array, "row", [(r, r ^ mask) for r in range(row_size)])

    def over_members(array, mask):
        pairs = [(b, (b // radix) * radix + ((b % radix) ^ mask)) for b in range(box_size)]
        return array if mask == 0 else lax.ppermute(array, "box", pairs)

    def over_groups(array, delta, mask=0):
        pairs = [
            (b, ((b // radix + delta) % groups) * radix + ((b % radix) ^ mask)) for b in range(box_size)
        ]
        return lax.ppermute(array, "box", pairs)

    def call(kernel, name, flops, outs, *args):
        outs = [jax.ShapeDtypeStruct(shape, dtype) for shape, dtype in outs]
        size = sum(a.size * a.dtype.itemsize for a in [*args, *outs])
        return pl.pallas_call(
            kernel,
            out_shape=outs,
            in_specs=[VMEM] * len(args),
            out_specs=[VMEM] * len(outs),
            compiler_params=pltpu.CompilerParams(vmem_limit_bytes=min(16 * MIB + 2 * size, 56 * MIB)),
            cost_estimate=pl.CostEstimate(flops=int(flops), bytes_accessed=0, transcendentals=0),
            name=name,
        )(*args)

    picked = call(
        functools.partial(pick_kernel, radix, groups),
        "pick_third",
        0,
        [((offs, radix, rank, rank), BF16)] * less + [((butterflies - offs, radix, rank, rank), BF16)] * less,
        third_level,
    )
    thirds = [over_groups(a, d + 1) for d, a in enumerate(picked[:less])]
    thirds_last = [over_groups(after(a, *thirds), d + 1) for d, a in enumerate(picked[less:])]

    up_own, up_other, up_mid, off_rows, last_rows = call(
        functools.partial(weights_kernel, radix, groups, offs, row_size),
        "weights",
        2 * butterflies * rank * (box_size * rank * depth + rows * groups * rank),
        [
            ((butterflies, radix, rank, depth), BF16),
            ((butterflies, radix, less, rank, depth), BF16),
            ((offs, groups, rank, depth), BF16),
            ((rows, offs * groups * rank), BF16),
            ((rows, groups * rank), BF16),
        ],
        first_level,
        second_level,
        fourth_level,
        out_basis,
    )

    seconds = call(
        functools.partial(second_kernel, radix, groups),
        "pick_second",
        0,
        [((offs, groups, rank, rank), BF16)] * 2,
        second_level,
    )
    seconds = [over_members(a, i) for i, a in zip((ALONG, BOTH), seconds)]

    pieces = [solved, over_row(solved, 1)]
    for mask in range(2, row_size, 2):
        far = after(over_row(solved, mask), up_own, *thirds, *seconds)
        pieces += [far, over_row(far, 1)]

    other_flops = 2 * columns * rank * radix * less * depth
    own_flops = 2 * columns * rank * radix * depth
    leaf_flops = 2 * columns * rank * rows
    row_flops = 2 * columns * rank * (depth + groups * rows)

    def own_out(count):
        return [((count, rank, columns), BF16)] * radix

    def other_out(count):
        return [((count, less, rank, columns), BF16)] * radix

    def cross(sums):
        return [over_groups(a, less - d) for d, a in enumerate(sums)]

    leaf, keep, across, along = call(
        functools.partial(off_kernel, row_size),
        "off_levels",
        offs * (leaf_flops + other_flops),
        [((offs, depth, columns), BF16)] + other_out(offs)[:3],
        leaf_basis,
        up_other,
        up_mid,
        *pieces,
    )
    along = over_members(along, ALONG)
    across = over_members(across, ACROSS)
    both = over_members(after(along, across, *thirds_last), ACROSS)
    own = call(own_kernel, "own_levels", offs * own_flops, own_out(offs)[:3], leaf, up_own, up_mid)
    own_along = over_members(after(own[2], along), ALONG)
    sums = call(
        off_sum_kernel,
        "off_sums",
        offs * less * 2 * columns * rank * depth,
        [((offs, rank, columns), BF16)] * less,
        *seconds,
        keep,
        across,
        along,
        both,
        *thirds,
    )
    crossed = cross(sums)
    own = [
        own[0],
        over_members(after(own[1], both), ACROSS),
        own_along,
    ]
    own.append(over_members(after(own_along, own[1], *sums), ACROSS))

    residual, *levels = call(
        functools.partial(middle_kernel, radix, groups, offs),
        "middle_levels",
        offs * row_flops + leaf_flops + other_flops + own_flops,
        [((rows, columns), F32)] + own_out(1) + other_out(1),
        third_level,
        rhs,
        leaf_basis,
        off_rows,
        up_own,
        up_other,
        *seconds,
        *crossed,
        *own,
    )
    own, other = levels[:radix], levels[radix:]
    other = [over_members(a, i) for i, a in reversed(list(enumerate(other)))]
    sums = call(
        functools.partial(sum_kernel, radix),
        "sums",
        less * 2 * columns * rank * depth,
        [((1, rank, columns), BF16)] * less,
        *other,
        *thirds_last,
    )
    crossed = cross(sums)
    own = [over_members(after(a, *sums) if i else a, i) for i, a in enumerate(own)]
    return call(
        functools.partial(last_kernel, radix, groups, offs),
        "last_levels",
        row_flops,
        [((1, rows, columns), BF16)],
        third_level,
        last_rows,
        residual,
        *crossed,
        *own[::-1],
    )[0]


def solution(mesh):
    placed = (
        P(None, ("box", "row"), None),
        P("row", "box", None),
        P("row", None, "box", None, None),
        P("row", None, "box", None, None, None, None),
        P("row", None, "box", None, None, None),
        P("row", None, "box", None, None, None),
        P("row", None, "box", None, None, None, None),
        P("row", None, "box", None, None),
    )
    return jax.shard_map(
        functools.partial(on_device, mesh.shape["row"], mesh.shape["box"]),
        mesh=mesh,
        in_specs=placed,
        out_specs=P("row", "box", None),
        check_vma=False,
    )
```

```python
import functools

import jax
import jax.numpy as jnp
from jax import lax
from jax.experimental import pallas as pl
from jax.experimental.pallas import tpu as pltpu
from jax.sharding import PartitionSpec as P

F32 = jnp.float32
BF16 = jnp.bfloat16
MIB = 1024 * 1024
ACROSS, ALONG, BOTH = 1, 2, 3
VMEM = pl.BlockSpec(memory_space=pltpu.VMEM)


def dot(a, b):
    return jnp.dot(a, b, preferred_element_type=F32)


def dot_t(a, b):
    return lax.dot_general(a, b, (((0,), (0,)), ((), ())), preferred_element_type=F32)


def place(radix):
    box = lax.axis_index("box")
    return lax.div(box, radix), lax.rem(box, radix)


def wrap(value, size):
    return lax.rem(value + size, size)


def take(refs, *counts):
    refs, out = list(refs), []
    for count in counts:
        out.append(refs[:count])
        refs = refs[count:]
    return out


def pick_kernel(radix, groups, third, *outs):
    group, _ = place(radix)
    start = 0
    for at, out in enumerate(outs):
        base = wrap(group + at % (groups - 1) + 1, groups) * radix
        for j in range(out.shape[0]):
            for k in range(radix):
                out[j, k] = third[0, start + j, 0, base + k]
        start += out.shape[0] if at % (groups - 1) == groups - 2 else 0


def second_kernel(radix, groups, second, *outs):
    group, member = place(radix)
    for i, out in zip((ALONG, BOTH), outs):
        for j in range(out.shape[0]):
            for delta in range(groups):
                out[j, delta] = second[0, j, 0, wrap(group - delta, groups) * radix + jnp.bitwise_xor(member, i)]


def leaf_order(row, leaves, row_size):
    per_leaf = row_size // leaves
    return [jnp.bitwise_xor(lax.div(row, per_leaf), t) for t in range(leaves)]


def weights_kernel(radix, groups, offs, row_size, first, second, fourth, out_basis, *outs):
    up_own, up_other, up_mid, off_rows, last_rows = outs
    levels = first.shape[3]
    slots = second.shape[3]
    rank = fourth.shape[6]
    half_rows = out_basis.shape[3]
    group, member = place(radix)
    for j in range(first.shape[1]):
        order = leaf_order(lax.axis_index("row"), radix, row_size) if j < offs else range(radix)

        def up(slot):
            level = lax.div(slot, slots // levels)
            mats = jnp.concatenate([first[0, j, 0, level, k] for k in order], axis=1)
            return dot(second[0, j, 0, slot], mats).astype(BF16)

        for i in range(radix):
            box = jnp.bitwise_xor(member, i)
            up_own[j, i] = up(group * radix + box)
            for delta in range(1, groups):
                up_other[j, i, delta - 1] = up(wrap(group - delta, groups) * radix + box)
        if j < offs:
            for delta in range(groups):
                slot = wrap(group - delta, groups) * radix + jnp.bitwise_xor(member, ALONG)
                level = lax.div(slot, slots // levels)
                up_mid[j, delta] = jnp.concatenate([first[0, j, 0, level, k] for k in order], axis=1)
        out, start = (off_rows, j * groups * rank) if j < offs else (last_rows, 0)
        for h in range(fourth.shape[3]):
            mats = [fourth[0, j, 0, h, wrap(group + delta, groups)] for delta in range(groups)]
            out[h * half_rows : (h + 1) * half_rows, start : start + groups * rank] = dot(
                out_basis[0, j, h], jnp.concatenate(mats, axis=1)
            ).astype(BF16)


def put_other(mats, leaf, other, at):
    radix, less, rank, depth = mats.shape
    coef = dot(mats[...].reshape(radix * less * rank, depth), leaf).astype(BF16)
    for i, ref in enumerate(other):
        ref[at] = coef[i * less * rank : (i + 1) * less * rank].reshape(ref.shape[1:])


def put_own(mats, leaf, own, at):
    radix, rank, depth = mats.shape
    coef = dot(mats[...].reshape(radix * rank, depth), leaf).astype(BF16)
    for i, ref in enumerate(own):
        ref[at] = coef[i * rank : (i + 1) * rank]


def off_kernel(pieces, basis, up_other, up_mid, *refs):
    parts, (leaf_ref, keep, across, along) = take(refs, pieces, 4)
    row = lax.axis_index("row")
    leaves, leaf_rows = basis.shape[2], basis.shape[3]
    rows = parts[0].shape[1]
    per_leaf = leaf_rows // rows
    order = leaf_order(row, leaves, pieces)
    less, rank, columns = keep.shape[1:]
    for j in range(parts[0].shape[0]):
        leaf = []
        for t in range(leaves):
            total = None
            for u in range(per_leaf):
                start = jnp.bitwise_xor(lax.rem(row, per_leaf), u) * rows
                if per_leaf == 1:
                    mat = basis[0, j, order[t]]
                else:
                    mat = basis[0, j, order[t], pl.ds(pl.multiple_of(start, rows), rows)]
                part = dot_t(mat, parts[t * per_leaf + u][j])
                total = part if total is None else total + part
            leaf.append(total.astype(BF16))
        leaf = jnp.concatenate(leaf, axis=0)
        leaf_ref[j] = leaf
        mats = [up_other[j, 0], up_other[j, ACROSS], up_mid[j, 1:]]
        mats = jnp.concatenate([m.reshape(less * rank, m.shape[2]) for m in mats], axis=0)
        coef = dot(mats, leaf).astype(BF16)
        for i, ref in enumerate((keep, across, along)):
            ref[j] = coef[i * less * rank : (i + 1) * less * rank].reshape(less, rank, columns)


def own_kernel(leaf, up_own, up_mid, *own):
    rank = up_mid.shape[2]
    for j in range(leaf.shape[0]):
        coef = dot(jnp.concatenate([up_own[j, 0], up_own[j, ACROSS], up_mid[j, 0]], axis=0), leaf[j]).astype(BF16)
        for i, ref in enumerate(own):
            ref[j] = coef[i * rank : (i + 1) * rank]


def slots_of(got, second_along, second_both, j, delta):
    keep, across, along, both = got
    return jnp.concatenate(
        [
            keep,
            across,
            dot(second_along[j, delta], along).astype(BF16),
            dot(second_both[j, delta], both).astype(BF16),
        ],
        axis=0,
    )


def off_sum_kernel(second_along, second_both, *refs):
    got, thirds, outs = take(refs, 4, (len(refs) - 4) // 2, (len(refs) - 4) // 2)
    radix = thirds[0].shape[1]
    _, member = place(radix)
    for d, (third, out) in enumerate(zip(thirds, outs)):
        for j in range(out.shape[0]):
            mats = [third[j, jnp.bitwise_xor(member, i)] for i in range(radix)]
            slots = slots_of([ref[j, d] for ref in got], second_along, second_both, j, d + 1)
            out[j] = dot(jnp.concatenate(mats, axis=1), slots).astype(BF16)


def last_own_kernel(leaf, up_own, *own):
    put_own(up_own.at[up_own.shape[0] - 1], leaf[...], own, 0)


def sum_kernel(radix, *refs):
    got, thirds, outs = take(refs, radix, (len(refs) - radix) // 2, (len(refs) - radix) // 2)
    got = got[::-1]
    _, member = place(radix)
    for d, (third, out) in enumerate(zip(thirds, outs)):
        for j in range(out.shape[0]):
            mats = [third[j, jnp.bitwise_xor(member, i)] for i in range(radix)]
            slots = jnp.concatenate([ref[j, d] for ref in got], axis=0)
            out[j] = dot(jnp.concatenate(mats, axis=1), slots).astype(BF16)


def group_coef(j, slots, third, radix):
    group, member = place(radix)
    mats = [third[0, j, 0, group * radix + jnp.bitwise_xor(member, i)] for i in range(radix)]
    return dot(jnp.concatenate(mats, axis=1), slots).astype(BF16)


def middle_kernel(
    radix, groups, offs, third, rhs, basis, row_mats, up_other, second_along, second_both, *refs
):
    crossed, own_in, (residual_ref, leaf_ref), other = take(refs, groups - 1, radix, 2, radix)
    coefs = []
    for j in range(offs):
        slots = slots_of([ref[j] for ref in own_in], second_along, second_both, j, 0)
        coefs += [group_coef(j, slots, third, radix)] + [ref[j] for ref in crossed]
    coefs = jnp.concatenate(coefs, axis=0)
    leaves, leaf_rows = basis.shape[2], basis.shape[3]
    leaf = []
    for k in range(leaves):
        rows = slice(k * leaf_rows, (k + 1) * leaf_rows)
        residual = rhs[0, rows].astype(F32) - dot(row_mats[rows], coefs)
        residual_ref[rows] = residual
        leaf.append(dot_t(basis[0, offs, k], residual.astype(BF16)).astype(BF16))
    leaf = jnp.concatenate(leaf, axis=0)
    leaf_ref[...] = leaf
    put_other(up_other.at[offs], leaf, other, 0)


def crossed_kernel(row_mats, residual, *refs):
    *crossed, out = refs
    rank = crossed[0].shape[1]
    coefs = jnp.concatenate([ref[0] for ref in crossed], axis=0)
    out[...] = residual[...] + dot(row_mats[:, rank:], coefs)


def last_kernel(radix, offs, third, row_mats, residual, *refs):
    own_in, (out,) = take(refs, radix, 1)
    slots = jnp.concatenate([ref[0] for ref in own_in[::-1]], axis=0)
    coef = group_coef(offs, slots, third, radix)
    out[0] = (residual[...] + dot(row_mats[:, : coef.shape[0]], coef)).astype(BF16)


def after(array, *others):
    return lax.optimization_barrier((array, *others))[0]


def on_device(
    row_size, box_size, solved, rhs, leaf_basis, first_level, second_level, third_level, fourth_level, out_basis
):
    radix = first_level.shape[4]
    groups = box_size // radix
    less = groups - 1
    butterflies = leaf_basis.shape[1]
    offs = solved.shape[0]
    columns = solved.shape[2]
    rank = leaf_basis.shape[4]
    rows = rhs.shape[1]
    depth = radix * rank

    def over_row(array, mask):
        return lax.ppermute(array, "row", [(r, r ^ mask) for r in range(row_size)])

    def over_members(array, mask):
        pairs = [(b, (b // radix) * radix + ((b % radix) ^ mask)) for b in range(box_size)]
        return array if mask == 0 else lax.ppermute(array, "box", pairs)

    def over_groups(array, delta, mask=0):
        pairs = [
            (b, ((b // radix + delta) % groups) * radix + ((b % radix) ^ mask)) for b in range(box_size)
        ]
        return lax.ppermute(array, "box", pairs)

    def call(kernel, name, flops, outs, *args):
        outs = [jax.ShapeDtypeStruct(shape, dtype) for shape, dtype in outs]
        size = sum(a.size * a.dtype.itemsize for a in [*args, *outs])
        return pl.pallas_call(
            kernel,
            out_shape=outs,
            in_specs=[VMEM] * len(args),
            out_specs=[VMEM] * len(outs),
            compiler_params=pltpu.CompilerParams(vmem_limit_bytes=min(16 * MIB + 2 * size, 56 * MIB)),
            cost_estimate=pl.CostEstimate(flops=int(flops), bytes_accessed=0, transcendentals=0),
            name=name,
        )(*args)

    picked = call(
        functools.partial(pick_kernel, radix, groups),
        "pick_third",
        0,
        [((offs, radix, rank, rank), BF16)] * less + [((butterflies - offs, radix, rank, rank), BF16)] * less,
        third_level,
    )
    thirds = [over_groups(a, d + 1) for d, a in enumerate(picked[:less])]
    thirds_last = [over_groups(after(a, *thirds), d + 1) for d, a in enumerate(picked[less:])]

    up_own, up_other, up_mid, off_rows, last_rows = call(
        functools.partial(weights_kernel, radix, groups, offs, row_size),
        "weights",
        2 * butterflies * rank * (box_size * rank * depth + rows * groups * rank),
        [
            ((butterflies, radix, rank, depth), BF16),
            ((butterflies, radix, less, rank, depth), BF16),
            ((offs, groups, rank, depth), BF16),
            ((rows, offs * groups * rank), BF16),
            ((rows, groups * rank), BF16),
        ],
        first_level,
        second_level,
        fourth_level,
        out_basis,
    )

    seconds = call(
        functools.partial(second_kernel, radix, groups),
        "pick_second",
        0,
        [((offs, groups, rank, rank), BF16)] * 2,
        second_level,
    )
    seconds = [over_members(a, i) for i, a in zip((ALONG, BOTH), seconds)]

    pieces = [solved, over_row(solved, 1)]
    for mask in range(2, row_size, 2):
        far = after(over_row(solved, mask), up_own, *thirds, *seconds)
        pieces += [far, over_row(far, 1)]

    other_flops = 2 * columns * rank * radix * less * depth
    own_flops = 2 * columns * rank * radix * depth
    leaf_flops = 2 * columns * rank * rows
    row_flops = 2 * columns * rank * (depth + groups * rows)

    def own_out(count):
        return [((count, rank, columns), BF16)] * radix

    def other_out(count):
        return [((count, less, rank, columns), BF16)] * radix

    def cross(sums):
        return [over_groups(a, less - d) for d, a in enumerate(sums)]

    leaf, keep, across, along = call(
        functools.partial(off_kernel, row_size),
        "off_levels",
        offs * (leaf_flops + other_flops),
        [((offs, depth, columns), BF16)] + other_out(offs)[:3],
        leaf_basis,
        up_other,
        up_mid,
        *pieces,
    )
    along = over_members(along, ALONG)
    across = over_members(across, ACROSS)
    both = over_members(after(along, across), ACROSS)
    own = call(own_kernel, "own_levels", offs * own_flops, own_out(offs)[:3], leaf, up_own, up_mid)
    own_along = over_members(after(own[2], along), ALONG)
    sums = call(
        off_sum_kernel,
        "off_sums",
        offs * less * 2 * columns * rank * depth,
        [((offs, rank, columns), BF16)] * less,
        *seconds,
        keep,
        across,
        along,
        both,
        *thirds,
    )
    crossed = cross(sums)
    own = [
        own[0],
        over_members(after(own[1], both, *thirds_last), ACROSS),
        own_along,
    ]
    own.append(over_members(after(own_along, own[1], *sums), ACROSS))

    residual, leaf, *other = call(
        functools.partial(middle_kernel, radix, groups, offs),
        "middle_levels",
        offs * row_flops + leaf_flops + other_flops + own_flops,
        [((rows, columns), F32), ((depth, columns), BF16)] + other_out(1),
        third_level,
        rhs,
        leaf_basis,
        off_rows,
        up_other,
        *seconds,
        *crossed,
        *own,
    )
    own = call(last_own_kernel, "last_own_levels", own_flops, own_out(1), leaf, up_own)
    other = [over_members(a, i) for i, a in reversed(list(enumerate(other)))]
    sums = call(
        functools.partial(sum_kernel, radix),
        "sums",
        less * 2 * columns * rank * depth,
        [((1, rank, columns), BF16)] * less,
        *other,
        *thirds_last,
    )
    crossed = cross(sums)
    own = [over_members(after(a, *sums) if i else a, i) for i, a in enumerate(own)]
    residual = call(
        crossed_kernel,
        "last_crossed",
        2 * columns * rank * less * rows,
        [((rows, columns), F32)],
        last_rows,
        residual,
        *crossed,
    )[0]
    return call(
        functools.partial(last_kernel, radix, offs),
        "last_levels",
        2 * columns * rank * (rows + depth),
        [((1, rows, columns), BF16)],
        third_level,
        last_rows,
        residual,
        *own[::-1],
    )[0]


def solution(mesh):
    placed = (
        P(None, ("box", "row"), None),
        P("row", "box", None),
        P("row", None, "box", None, None),
        P("row", None, "box", None, None, None, None),
        P("row", None, "box", None, None, None),
        P("row", None, "box", None, None, None),
        P("row", None, "box", None, None, None, None),
        P("row", None, "box", None, None),
    )
    return jax.shard_map(
        functools.partial(on_device, mesh.shape["row"], mesh.shape["box"]),
        mesh=mesh,
        in_specs=placed,
        out_specs=P("row", "box", None),
        check_vma=False,
    )
```

```python
import functools

import jax
import jax.numpy as jnp
from jax import lax
from jax.experimental import pallas as pl
from jax.experimental.pallas import tpu as pltpu
from jax.sharding import PartitionSpec as P

F32 = jnp.float32
BF16 = jnp.bfloat16
MIB = 1024 * 1024
ACROSS, ALONG, BOTH = 1, 2, 3
VMEM = pl.BlockSpec(memory_space=pltpu.VMEM)


def dot(a, b):
    return jnp.dot(a, b, preferred_element_type=F32)


def dot_t(a, b):
    return lax.dot_general(a, b, (((0,), (0,)), ((), ())), preferred_element_type=F32)


def place(radix):
    box = lax.axis_index("box")
    return lax.div(box, radix), lax.rem(box, radix)


def wrap(value, size):
    return lax.rem(value + size, size)


def take(refs, *counts):
    refs, out = list(refs), []
    for count in counts:
        out.append(refs[:count])
        refs = refs[count:]
    return out


def pick_kernel(radix, groups, third, *outs):
    group, _ = place(radix)
    start = 0
    for at, out in enumerate(outs):
        base = wrap(group + at % (groups - 1) + 1, groups) * radix
        for j in range(out.shape[0]):
            for k in range(radix):
                out[j, k] = third[0, start + j, 0, base + k]
        start += out.shape[0] if at % (groups - 1) == groups - 2 else 0


def second_kernel(radix, groups, second, *outs):
    group, member = place(radix)
    for i, out in zip((ALONG, BOTH), outs):
        for j in range(out.shape[0]):
            for delta in range(groups):
                out[j, delta] = second[0, j, 0, wrap(group - delta, groups) * radix + jnp.bitwise_xor(member, i)]


def leaf_order(row, leaves, row_size):
    per_leaf = row_size // leaves
    return [jnp.bitwise_xor(lax.div(row, per_leaf), t) for t in range(leaves)]


def weights_kernel(radix, groups, offs, row_size, first, second, fourth, out_basis, *outs):
    up_own, up_other, up_mid, off_rows, last_rows = outs
    levels = first.shape[3]
    slots = second.shape[3]
    rank = fourth.shape[6]
    half_rows = out_basis.shape[3]
    group, member = place(radix)
    for j in range(first.shape[1]):
        order = leaf_order(lax.axis_index("row"), radix, row_size) if j < offs else range(radix)

        def up(slot):
            level = lax.div(slot, slots // levels)
            mats = jnp.concatenate([first[0, j, 0, level, k] for k in order], axis=1)
            return dot(second[0, j, 0, slot], mats).astype(BF16)

        for i in range(radix):
            box = jnp.bitwise_xor(member, i)
            up_own[j, i] = up(group * radix + box)
            for delta in range(1, groups):
                up_other[j, i, delta - 1] = up(wrap(group - delta, groups) * radix + box)
        if j < offs:
            for delta in range(groups):
                slot = wrap(group - delta, groups) * radix + jnp.bitwise_xor(member, ALONG)
                level = lax.div(slot, slots // levels)
                up_mid[j, delta] = jnp.concatenate([first[0, j, 0, level, k] for k in order], axis=1)
        out, start = (off_rows, j * groups * rank) if j < offs else (last_rows, 0)
        for h in range(fourth.shape[3]):
            mats = [fourth[0, j, 0, h, wrap(group + delta, groups)] for delta in range(groups)]
            out[h * half_rows : (h + 1) * half_rows, start : start + groups * rank] = dot(
                out_basis[0, j, h], jnp.concatenate(mats, axis=1)
            ).astype(BF16)


def put_other(mats, leaf, other, at):
    radix, less, rank, depth = mats.shape
    coef = dot(mats[...].reshape(radix * less * rank, depth), leaf).astype(BF16)
    for i, ref in enumerate(other):
        ref[at] = coef[i * less * rank : (i + 1) * less * rank].reshape(ref.shape[1:])


def put_own(mats, leaf, own, at):
    radix, rank, depth = mats.shape
    coef = dot(mats[...].reshape(radix * rank, depth), leaf).astype(BF16)
    for i, ref in enumerate(own):
        ref[at] = coef[i * rank : (i + 1) * rank]


def off_kernel(j, pieces, basis, up_other, up_mid, *refs):
    parts, (leaf_ref, keep, across, along) = take(refs, pieces, 4)
    row = lax.axis_index("row")
    leaves, leaf_rows = basis.shape[2], basis.shape[3]
    rows = parts[0].shape[1]
    per_leaf = leaf_rows // rows
    order = leaf_order(row, leaves, pieces)
    less, rank, columns = keep.shape
    leaf = []
    for t in range(leaves):
        total = None
        for u in range(per_leaf):
            start = jnp.bitwise_xor(lax.rem(row, per_leaf), u) * rows
            if per_leaf == 1:
                mat = basis[0, j, order[t]]
            else:
                mat = basis[0, j, order[t], pl.ds(pl.multiple_of(start, rows), rows)]
            ref = parts[t * per_leaf + u]
            part = dot_t(mat, ref[j] if ref.shape[0] > 1 else ref[0])
            total = part if total is None else total + part
        leaf.append(total.astype(BF16))
    leaf = jnp.concatenate(leaf, axis=0)
    leaf_ref[...] = leaf
    mats = [up_other[j, 0], up_other[j, ACROSS], up_mid[j, 1:]]
    mats = jnp.concatenate([m.reshape(less * rank, m.shape[2]) for m in mats], axis=0)
    coef = dot(mats, leaf).astype(BF16)
    for i, ref in enumerate((keep, across, along)):
        ref[...] = coef[i * less * rank : (i + 1) * less * rank].reshape(less, rank, columns)


def own_kernel(up_own, up_mid, *refs):
    rank = up_mid.shape[2]
    leaves, own = take(refs, up_mid.shape[0], len(refs) - up_mid.shape[0])
    for j, leaf in enumerate(leaves):
        mats = jnp.concatenate([up_own[j, 0], up_own[j, ACROSS], up_mid[j, 0]], axis=0)
        coef = dot(mats, leaf[...]).astype(BF16)
        for i, ref in enumerate(own):
            ref[j] = coef[i * rank : (i + 1) * rank]


def slots_of(got, second_along, second_both, j, delta):
    keep, across, along, both = got
    return jnp.concatenate(
        [
            keep,
            across,
            dot(second_along[j, delta], along).astype(BF16),
            dot(second_both[j, delta], both).astype(BF16),
        ],
        axis=0,
    )


def off_sum_kernel(j, second_along, second_both, *refs):
    got, thirds, outs = take(refs, 4, (len(refs) - 4) // 2, (len(refs) - 4) // 2)
    radix = thirds[0].shape[1]
    _, member = place(radix)
    for d, (third, out) in enumerate(zip(thirds, outs)):
        mats = [third[0, jnp.bitwise_xor(member, i)] for i in range(radix)]
        slots = slots_of([ref[d] for ref in got], second_along, second_both, j, d + 1)
        out[...] = dot(jnp.concatenate(mats, axis=1), slots).astype(BF16)


def sum_kernel(radix, *refs):
    got, thirds, outs = take(refs, radix, (len(refs) - radix) // 2, (len(refs) - radix) // 2)
    got = got[::-1]
    _, member = place(radix)
    for d, (third, out) in enumerate(zip(thirds, outs)):
        for j in range(out.shape[0]):
            mats = [third[j, jnp.bitwise_xor(member, i)] for i in range(radix)]
            slots = jnp.concatenate([ref[j, d] for ref in got], axis=0)
            out[j] = dot(jnp.concatenate(mats, axis=1), slots).astype(BF16)


def group_coef(j, slots, third, radix):
    group, member = place(radix)
    mats = [third[0, j, 0, group * radix + jnp.bitwise_xor(member, i)] for i in range(radix)]
    return dot(jnp.concatenate(mats, axis=1), slots).astype(BF16)


def middle_kernel(
    radix, groups, offs, third, rhs, basis, row_mats, up_own, up_other, second_along, second_both, *refs
):
    crossed, own_in, (residual_ref,), own, other = take(refs, offs * (groups - 1), radix, 1, radix, radix)
    coefs = []
    for j in range(offs):
        slots = slots_of([ref[j] for ref in own_in], second_along, second_both, j, 0)
        coefs += [group_coef(j, slots, third, radix)]
        coefs += [ref[...] for ref in crossed[j * (groups - 1) : (j + 1) * (groups - 1)]]
    coefs = jnp.concatenate(coefs, axis=0)
    leaves, leaf_rows = basis.shape[2], basis.shape[3]
    leaf = []
    for k in range(leaves):
        rows = slice(k * leaf_rows, (k + 1) * leaf_rows)
        residual = rhs[0, rows].astype(F32) - dot(row_mats[rows], coefs)
        residual_ref[rows] = residual
        leaf.append(dot_t(basis[0, offs, k], residual.astype(BF16)).astype(BF16))
    leaf = jnp.concatenate(leaf, axis=0)
    put_other(up_other.at[offs], leaf, other, 0)
    put_own(up_own.at[offs], leaf, own, 0)


def last_kernel(radix, groups, offs, third, row_mats, residual, *refs):
    crossed, own_in, (out,) = take(refs, groups - 1, radix, 1)
    own_in = own_in[::-1]
    slots = jnp.concatenate([ref[0] for ref in own_in], axis=0)
    coefs = [group_coef(offs, slots, third, radix)] + [ref[0] for ref in crossed]
    coefs = jnp.concatenate(coefs, axis=0)
    out[0] = (residual[...] + dot(row_mats[...], coefs)).astype(BF16)


def after(array, *others):
    return lax.optimization_barrier((array, *others))[0]


def on_device(
    row_size, box_size, solved, rhs, leaf_basis, first_level, second_level, third_level, fourth_level, out_basis
):
    radix = first_level.shape[4]
    groups = box_size // radix
    less = groups - 1
    butterflies = leaf_basis.shape[1]
    offs = solved.shape[0]
    columns = solved.shape[2]
    rank = leaf_basis.shape[4]
    rows = rhs.shape[1]
    depth = radix * rank

    def over_row(array, mask):
        return lax.ppermute(array, "row", [(r, r ^ mask) for r in range(row_size)])

    def over_members(array, mask):
        pairs = [(b, (b // radix) * radix + ((b % radix) ^ mask)) for b in range(box_size)]
        return array if mask == 0 else lax.ppermute(array, "box", pairs)

    def over_groups(array, delta, mask=0):
        pairs = [
            (b, ((b // radix + delta) % groups) * radix + ((b % radix) ^ mask)) for b in range(box_size)
        ]
        return lax.ppermute(array, "box", pairs)

    def call(kernel, name, flops, outs, *args):
        outs = [jax.ShapeDtypeStruct(shape, dtype) for shape, dtype in outs]
        size = sum(a.size * a.dtype.itemsize for a in [*args, *outs])
        return pl.pallas_call(
            kernel,
            out_shape=outs,
            in_specs=[VMEM] * len(args),
            out_specs=[VMEM] * len(outs),
            compiler_params=pltpu.CompilerParams(vmem_limit_bytes=min(16 * MIB + 2 * size, 56 * MIB)),
            cost_estimate=pl.CostEstimate(flops=int(flops), bytes_accessed=0, transcendentals=0),
            name=name,
        )(*args)

    picked = call(
        functools.partial(pick_kernel, radix, groups),
        "pick_third",
        0,
        [((1, radix, rank, rank), BF16)] * (butterflies * less),
        third_level,
    )
    thirds = [
        [over_groups(a, d + 1) for d, a in enumerate(picked[j * less : (j + 1) * less])] for j in range(butterflies)
    ]

    up_own, up_other, up_mid, off_rows, last_rows = call(
        functools.partial(weights_kernel, radix, groups, offs, row_size),
        "weights",
        2 * butterflies * rank * (box_size * rank * depth + rows * groups * rank),
        [
            ((butterflies, radix, rank, depth), BF16),
            ((butterflies, radix, less, rank, depth), BF16),
            ((offs, groups, rank, depth), BF16),
            ((rows, offs * groups * rank), BF16),
            ((rows, groups * rank), BF16),
        ],
        first_level,
        second_level,
        fourth_level,
        out_basis,
    )

    seconds = call(
        functools.partial(second_kernel, radix, groups),
        "pick_second",
        0,
        [((offs, groups, rank, rank), BF16)] * 2,
        second_level,
    )
    seconds = [over_members(a, i) for i, a in zip((ALONG, BOTH), seconds)]

    other_flops = 2 * columns * rank * radix * less * depth
    own_flops = 2 * columns * rank * radix * depth
    leaf_flops = 2 * columns * rank * rows
    row_flops = 2 * columns * rank * (depth + groups * rows)

    def own_out(count):
        return [((count, rank, columns), BF16)] * radix

    def other_out(count):
        return [((count, less, rank, columns), BF16)] * radix

    def cross(sums):
        return [over_groups(a, less - d) for d, a in enumerate(sums)]

    beside = over_row(solved, 1)
    far, held, leaves, sums, crossed = [], [up_own, *seconds, *thirds[0]], [], [], []
    for j in range(offs):
        pieces = [solved, beside]
        come = far
        far = [over_row(after(solved[j : j + 1], *come), mask) for mask in range(2, row_size, 2)]
        for a in far:
            a = after(a, *held)
            pieces += [a, over_row(a, 1)]
        leaf, keep, across, along = call(
            functools.partial(off_kernel, j, row_size),
            "off_levels",
            leaf_flops + other_flops,
            [((depth, columns), BF16)] + [((less, rank, columns), BF16)] * 3,
            leaf_basis,
            up_other,
            up_mid,
            *pieces,
        )
        leaves.append(leaf)
        along = over_members(along, ALONG)
        across = over_members(across, ACROSS)
        both = over_members(after(along, across, *sums, *(thirds[j] if j else [])), ACROSS)
        sums = call(
            functools.partial(off_sum_kernel, j),
            "off_sums",
            less * 2 * columns * rank * depth,
            [((rank, columns), BF16)] * less,
            *seconds,
            keep,
            across,
            along,
            both,
            *thirds[j],
        )
        crossed += cross(sums)
        held = [across, along]
    own = call(own_kernel, "own_levels", offs * own_flops, own_out(offs)[:3], up_own, up_mid, *leaves)
    own_along = over_members(after(own[2], along), ALONG)
    own = [own[0], over_members(after(own[1], both, *thirds[offs], *crossed[:less]), ACROSS), own_along]
    own.append(over_members(after(own_along, own[1], *sums), ACROSS))

    residual, *levels = call(
        functools.partial(middle_kernel, radix, groups, offs),
        "middle_levels",
        offs * row_flops + leaf_flops + other_flops + own_flops,
        [((rows, columns), F32)] + own_out(1) + other_out(1),
        third_level,
        rhs,
        leaf_basis,
        off_rows,
        up_own,
        up_other,
        *seconds,
        *crossed,
        *own,
    )
    own, other = levels[:radix], levels[radix:]
    other = [over_members(a, i) for i, a in reversed(list(enumerate(other)))]
    sums = call(
        functools.partial(sum_kernel, radix),
        "sums",
        less * 2 * columns * rank * depth,
        [((1, rank, columns), BF16)] * less,
        *other,
        *thirds[offs],
    )
    crossed = cross(sums)
    own = [over_members(after(a, *sums) if i else a, i) for i, a in enumerate(own)]
    return call(
        functools.partial(last_kernel, radix, groups, offs),
        "last_levels",
        row_flops,
        [((1, rows, columns), BF16)],
        third_level,
        last_rows,
        residual,
        *crossed,
        *own[::-1],
    )[0]


def solution(mesh):
    placed = (
        P(None, ("box", "row"), None),
        P("row", "box", None),
        P("row", None, "box", None, None),
        P("row", None, "box", None, None, None, None),
        P("row", None, "box", None, None, None),
        P("row", None, "box", None, None, None),
        P("row", None, "box", None, None, None, None),
        P("row", None, "box", None, None),
    )
    return jax.shard_map(
        functools.partial(on_device, mesh.shape["row"], mesh.shape["box"]),
        mesh=mesh,
        in_specs=placed,
        out_specs=P("row", "box", None),
        check_vma=False,
    )
```

```python
import functools

import jax
import jax.numpy as jnp
from jax import lax
from jax.experimental import pallas as pl
from jax.experimental.pallas import tpu as pltpu
from jax.sharding import PartitionSpec as P

F32 = jnp.float32
BF16 = jnp.bfloat16
MIB = 1024 * 1024
ACROSS, ALONG, BOTH = 1, 2, 3
VMEM = pl.BlockSpec(memory_space=pltpu.VMEM)


def dot(a, b):
    return jnp.dot(a, b, preferred_element_type=F32)


def dot_t(a, b):
    return lax.dot_general(a, b, (((0,), (0,)), ((), ())), preferred_element_type=F32)


def place(radix):
    box = lax.axis_index("box")
    return lax.div(box, radix), lax.rem(box, radix)


def wrap(value, size):
    return lax.rem(value + size, size)


def take(refs, *counts):
    refs, out = list(refs), []
    for count in counts:
        out.append(refs[:count])
        refs = refs[count:]
    return out


def pick_kernel(radix, groups, third, *outs):
    group, _ = place(radix)
    start = 0
    for at, out in enumerate(outs):
        base = wrap(group + at % (groups - 1) + 1, groups) * radix
        for j in range(out.shape[0]):
            for k in range(radix):
                out[j, k] = third[0, start + j, 0, base + k]
        start += out.shape[0] if at % (groups - 1) == groups - 2 else 0


def second_kernel(radix, groups, second, *outs):
    group, member = place(radix)
    for i, out in zip((ALONG, BOTH), outs):
        for j in range(out.shape[0]):
            for delta in range(groups):
                out[j, delta] = second[0, j, 0, wrap(group - delta, groups) * radix + jnp.bitwise_xor(member, i)]


def leaf_order(row, leaves, row_size):
    per_leaf = row_size // leaves
    return [jnp.bitwise_xor(lax.div(row, per_leaf), t) for t in range(leaves)]


def weights_kernel(radix, groups, offs, row_size, first, second, fourth, out_basis, *outs):
    up_own, up_other, up_mid, off_rows, last_rows = outs
    levels = first.shape[3]
    slots = second.shape[3]
    rank = fourth.shape[6]
    half_rows = out_basis.shape[3]
    group, member = place(radix)
    for j in range(first.shape[1]):
        order = leaf_order(lax.axis_index("row"), radix, row_size) if j < offs else range(radix)

        def up(slot):
            level = lax.div(slot, slots // levels)
            mats = jnp.concatenate([first[0, j, 0, level, k] for k in order], axis=1)
            return dot(second[0, j, 0, slot], mats).astype(BF16)

        for i in range(radix):
            box = jnp.bitwise_xor(member, i)
            up_own[j, i] = up(group * radix + box)
            for delta in range(1, groups):
                up_other[j, i, delta - 1] = up(wrap(group - delta, groups) * radix + box)
        if j < offs:
            for delta in range(groups):
                slot = wrap(group - delta, groups) * radix + jnp.bitwise_xor(member, ALONG)
                level = lax.div(slot, slots // levels)
                up_mid[j, delta] = jnp.concatenate([first[0, j, 0, level, k] for k in order], axis=1)
        out, start = (off_rows, j * groups * rank) if j < offs else (last_rows, 0)
        for h in range(fourth.shape[3]):
            mats = [fourth[0, j, 0, h, wrap(group + delta, groups)] for delta in range(groups)]
            out[h * half_rows : (h + 1) * half_rows, start : start + groups * rank] = dot(
                out_basis[0, j, h], jnp.concatenate(mats, axis=1)
            ).astype(BF16)


def put_other(mats, leaf, other, at):
    radix, less, rank, depth = mats.shape
    coef = dot(mats[...].reshape(radix * less * rank, depth), leaf).astype(BF16)
    for i, ref in enumerate(other):
        ref[at] = coef[i * less * rank : (i + 1) * less * rank].reshape(ref.shape[1:])


def put_own(mats, leaf, own, at):
    radix, rank, depth = mats.shape
    coef = dot(mats[...].reshape(radix * rank, depth), leaf).astype(BF16)
    for i, ref in enumerate(own):
        ref[at] = coef[i * rank : (i + 1) * rank]


def off_kernel(j, pieces, basis, up_other, up_mid, *refs):
    parts, (leaf_ref, keep, across, along) = take(refs, pieces, 4)
    row = lax.axis_index("row")
    leaves, leaf_rows = basis.shape[2], basis.shape[3]
    rows = parts[0].shape[1]
    per_leaf = leaf_rows // rows
    order = leaf_order(row, leaves, pieces)
    less, rank, columns = keep.shape
    leaf = []
    for t in range(leaves):
        total = None
        for u in range(per_leaf):
            start = jnp.bitwise_xor(lax.rem(row, per_leaf), u) * rows
            if per_leaf == 1:
                mat = basis[0, j, order[t]]
            else:
                mat = basis[0, j, order[t], pl.ds(pl.multiple_of(start, rows), rows)]
            ref = parts[t * per_leaf + u]
            part = dot_t(mat, ref[j] if ref.shape[0] > 1 else ref[0])
            total = part if total is None else total + part
        leaf.append(total.astype(BF16))
    leaf = jnp.concatenate(leaf, axis=0)
    leaf_ref[...] = leaf
    mats = [up_other[j, 0], up_other[j, ACROSS], up_mid[j, 1:]]
    mats = jnp.concatenate([m.reshape(less * rank, m.shape[2]) for m in mats], axis=0)
    coef = dot(mats, leaf).astype(BF16)
    for i, ref in enumerate((keep, across, along)):
        ref[...] = coef[i * less * rank : (i + 1) * less * rank].reshape(less, rank, columns)


def own_kernel(up_own, up_mid, *refs):
    rank = up_mid.shape[2]
    leaves, own = take(refs, up_mid.shape[0], len(refs) - up_mid.shape[0])
    for j, leaf in enumerate(leaves):
        mats = jnp.concatenate([up_own[j, 0], up_own[j, ACROSS], up_mid[j, 0]], axis=0)
        coef = dot(mats, leaf[...]).astype(BF16)
        for i, ref in enumerate(own):
            ref[j] = coef[i * rank : (i + 1) * rank]


def slots_of(got, second_along, second_both, j, delta):
    keep, across, along, both = got
    return jnp.concatenate(
        [
            keep,
            across,
            dot(second_along[j, delta], along).astype(BF16),
            dot(second_both[j, delta], both).astype(BF16),
        ],
        axis=0,
    )


def off_sum_kernel(j, second_along, second_both, *refs):
    got, thirds, outs = take(refs, 4, (len(refs) - 4) // 2, (len(refs) - 4) // 2)
    radix = thirds[0].shape[1]
    _, member = place(radix)
    for d, (third, out) in enumerate(zip(thirds, outs)):
        mats = [third[0, jnp.bitwise_xor(member, i)] for i in range(radix)]
        slots = slots_of([ref[d] for ref in got], second_along, second_both, j, d + 1)
        out[...] = dot(jnp.concatenate(mats, axis=1), slots).astype(BF16)


def sum_kernel(radix, *refs):
    got, thirds, outs = take(refs, radix, (len(refs) - radix) // 2, (len(refs) - radix) // 2)
    got = got[::-1]
    _, member = place(radix)
    for d, (third, out) in enumerate(zip(thirds, outs)):
        for j in range(out.shape[0]):
            mats = [third[j, jnp.bitwise_xor(member, i)] for i in range(radix)]
            slots = jnp.concatenate([ref[j, d] for ref in got], axis=0)
            out[j] = dot(jnp.concatenate(mats, axis=1), slots).astype(BF16)


def group_coef(j, slots, third, radix):
    group, member = place(radix)
    mats = [third[0, j, 0, group * radix + jnp.bitwise_xor(member, i)] for i in range(radix)]
    return dot(jnp.concatenate(mats, axis=1), slots).astype(BF16)


def crossed_kernel(groups, offs, rhs, row_mats, *refs):
    *crossed, out = refs
    rank = crossed[0].shape[0]
    mats = [
        row_mats[:, (j * groups + delta) * rank : (j * groups + delta + 1) * rank]
        for j in range(offs)
        for delta in range(1, groups)
    ]
    coefs = jnp.concatenate([ref[...] for ref in crossed], axis=0)
    out[...] = rhs[0].astype(F32) - dot(jnp.concatenate(mats, axis=1), coefs)


def middle_kernel(radix, groups, offs, third, part, basis, row_mats, up_own, up_other, second_along, second_both, *refs):
    own_in, (residual_ref,), own, other = take(refs, radix, 1, radix, radix)
    rank = third.shape[5]
    coefs = []
    for j in range(offs):
        slots = slots_of([ref[j] for ref in own_in], second_along, second_both, j, 0)
        coefs += [group_coef(j, slots, third, radix)]
    coefs = jnp.concatenate(coefs, axis=0)
    mats = [row_mats[:, j * groups * rank : (j * groups + 1) * rank] for j in range(offs)]
    mats = jnp.concatenate(mats, axis=1)
    leaves, leaf_rows = basis.shape[2], basis.shape[3]
    leaf = []
    for k in range(leaves):
        rows = slice(k * leaf_rows, (k + 1) * leaf_rows)
        residual = part[rows] - dot(mats[rows], coefs)
        residual_ref[rows] = residual
        leaf.append(dot_t(basis[0, offs, k], residual.astype(BF16)).astype(BF16))
    leaf = jnp.concatenate(leaf, axis=0)
    put_other(up_other.at[offs], leaf, other, 0)
    put_own(up_own.at[offs], leaf, own, 0)


def last_kernel(radix, groups, offs, third, row_mats, residual, *refs):
    crossed, own_in, (out,) = take(refs, groups - 1, radix, 1)
    own_in = own_in[::-1]
    slots = jnp.concatenate([ref[0] for ref in own_in], axis=0)
    coefs = [group_coef(offs, slots, third, radix)] + [ref[0] for ref in crossed]
    coefs = jnp.concatenate(coefs, axis=0)
    out[0] = (residual[...] + dot(row_mats[...], coefs)).astype(BF16)


def after(array, *others):
    return lax.optimization_barrier((array, *others))[0]


def on_device(
    row_size, box_size, solved, rhs, leaf_basis, first_level, second_level, third_level, fourth_level, out_basis
):
    radix = first_level.shape[4]
    groups = box_size // radix
    less = groups - 1
    butterflies = leaf_basis.shape[1]
    offs = solved.shape[0]
    columns = solved.shape[2]
    rank = leaf_basis.shape[4]
    rows = rhs.shape[1]
    depth = radix * rank

    def over_row(array, mask):
        return lax.ppermute(array, "row", [(r, r ^ mask) for r in range(row_size)])

    def over_members(array, mask):
        pairs = [(b, (b // radix) * radix + ((b % radix) ^ mask)) for b in range(box_size)]
        return array if mask == 0 else lax.ppermute(array, "box", pairs)

    def over_groups(array, delta, mask=0):
        pairs = [
            (b, ((b // radix + delta) % groups) * radix + ((b % radix) ^ mask)) for b in range(box_size)
        ]
        return lax.ppermute(array, "box", pairs)

    def call(kernel, name, flops, outs, *args):
        outs = [jax.ShapeDtypeStruct(shape, dtype) for shape, dtype in outs]
        size = sum(a.size * a.dtype.itemsize for a in [*args, *outs])
        return pl.pallas_call(
            kernel,
            out_shape=outs,
            in_specs=[VMEM] * len(args),
            out_specs=[VMEM] * len(outs),
            compiler_params=pltpu.CompilerParams(vmem_limit_bytes=min(16 * MIB + 2 * size, 56 * MIB)),
            cost_estimate=pl.CostEstimate(flops=int(flops), bytes_accessed=0, transcendentals=0),
            name=name,
        )(*args)

    picked = call(
        functools.partial(pick_kernel, radix, groups),
        "pick_third",
        0,
        [((1, radix, rank, rank), BF16)] * (butterflies * less),
        third_level,
    )
    thirds = [
        [over_groups(a, d + 1) for d, a in enumerate(picked[j * less : (j + 1) * less])] for j in range(butterflies)
    ]

    up_own, up_other, up_mid, off_rows, last_rows = call(
        functools.partial(weights_kernel, radix, groups, offs, row_size),
        "weights",
        2 * butterflies * rank * (box_size * rank * depth + rows * groups * rank),
        [
            ((butterflies, radix, rank, depth), BF16),
            ((butterflies, radix, less, rank, depth), BF16),
            ((offs, groups, rank, depth), BF16),
            ((rows, offs * groups * rank), BF16),
            ((rows, groups * rank), BF16),
        ],
        first_level,
        second_level,
        fourth_level,
        out_basis,
    )

    seconds = call(
        functools.partial(second_kernel, radix, groups),
        "pick_second",
        0,
        [((offs, groups, rank, rank), BF16)] * 2,
        second_level,
    )
    seconds = [over_members(a, i) for i, a in zip((ALONG, BOTH), seconds)]

    other_flops = 2 * columns * rank * radix * less * depth
    own_flops = 2 * columns * rank * radix * depth
    leaf_flops = 2 * columns * rank * rows
    row_flops = 2 * columns * rank * (depth + groups * rows)

    def own_out(count):
        return [((count, rank, columns), BF16)] * radix

    def other_out(count):
        return [((count, less, rank, columns), BF16)] * radix

    def cross(sums):
        return [over_groups(a, less - d) for d, a in enumerate(sums)]

    beside = over_row(solved, 1)
    far, held, leaves, sums, crossed = [], [up_own, *seconds], [], [], []
    for j in range(offs):
        pieces = [solved, beside]
        come = far
        far = [over_row(after(solved[j : j + 1], *come), mask) for mask in range(2, row_size, 2)]
        for a in far:
            a = after(a, *held)
            pieces += [a, over_row(a, 1)]
        leaf, keep, across, along = call(
            functools.partial(off_kernel, j, row_size),
            "off_levels",
            leaf_flops + other_flops,
            [((depth, columns), BF16)] + [((less, rank, columns), BF16)] * 3,
            leaf_basis,
            up_other,
            up_mid,
            *pieces,
        )
        leaves.append(leaf)
        along = over_members(along, ALONG)
        across = over_members(across, ACROSS)
        both = over_members(after(along, across, *sums, *(thirds[j] if j else [])), ACROSS)
        sums = call(
            functools.partial(off_sum_kernel, j),
            "off_sums",
            less * 2 * columns * rank * depth,
            [((rank, columns), BF16)] * less,
            *seconds,
            keep,
            across,
            along,
            both,
            *thirds[j],
        )
        crossed += cross(sums)
        held = [across, along, *thirds[0]]
    own = call(own_kernel, "own_levels", offs * own_flops, own_out(offs)[:3], up_own, up_mid, *leaves)
    own_along = over_members(after(own[2], along), ALONG)
    own = [own[0], over_members(after(own[1], both, *thirds[offs]), ACROSS), own_along]
    own.append(over_members(after(own_along, *crossed[:less]), ACROSS))

    part = call(
        functools.partial(crossed_kernel, groups, offs),
        "middle_crossed",
        2 * offs * less * columns * rank * rows,
        [((rows, columns), F32)],
        rhs,
        off_rows,
        *crossed,
    )[0]
    residual, *levels = call(
        functools.partial(middle_kernel, radix, groups, offs),
        "middle_levels",
        offs * row_flops + leaf_flops + other_flops + own_flops,
        [((rows, columns), F32)] + own_out(1) + other_out(1),
        third_level,
        part,
        leaf_basis,
        off_rows,
        up_own,
        up_other,
        *seconds,
        *own,
    )
    own, other = levels[:radix], levels[radix:]
    other = [over_members(a, i) for i, a in reversed(list(enumerate(other)))]
    sums = call(
        functools.partial(sum_kernel, radix),
        "sums",
        less * 2 * columns * rank * depth,
        [((1, rank, columns), BF16)] * less,
        *other,
        *thirds[offs],
    )
    crossed = cross(sums)
    own = [over_members(after(a, *sums) if i else a, i) for i, a in enumerate(own)]
    return call(
        functools.partial(last_kernel, radix, groups, offs),
        "last_levels",
        row_flops,
        [((1, rows, columns), BF16)],
        third_level,
        last_rows,
        residual,
        *crossed,
        *own[::-1],
    )[0]


def solution(mesh):
    placed = (
        P(None, ("box", "row"), None),
        P("row", "box", None),
        P("row", None, "box", None, None),
        P("row", None, "box", None, None, None, None),
        P("row", None, "box", None, None, None),
        P("row", None, "box", None, None, None),
        P("row", None, "box", None, None, None, None),
        P("row", None, "box", None, None),
    )
    return jax.shard_map(
        functools.partial(on_device, mesh.shape["row"], mesh.shape["box"]),
        mesh=mesh,
        in_specs=placed,
        out_specs=P("row", "box", None),
        check_vma=False,
    )
```

```python
import functools

import jax
import jax.numpy as jnp
from jax import lax
from jax.experimental import pallas as pl
from jax.experimental.pallas import tpu as pltpu
from jax.sharding import PartitionSpec as P

F32 = jnp.float32
BF16 = jnp.bfloat16
MIB = 1024 * 1024
ACROSS, ALONG, BOTH = 1, 2, 3
VMEM = pl.BlockSpec(memory_space=pltpu.VMEM)


def dot(a, b):
    return jnp.dot(a, b, preferred_element_type=F32)


def dot_t(a, b):
    return lax.dot_general(a, b, (((0,), (0,)), ((), ())), preferred_element_type=F32)


def place(radix):
    box = lax.axis_index("box")
    return lax.div(box, radix), lax.rem(box, radix)


def wrap(value, size):
    return lax.rem(value + size, size)


def take(refs, *counts):
    refs, out = list(refs), []
    for count in counts:
        out.append(refs[:count])
        refs = refs[count:]
    return out


def pick_kernel(radix, groups, third, *outs):
    group, _ = place(radix)
    start = 0
    for at, out in enumerate(outs):
        base = wrap(group + at % (groups - 1) + 1, groups) * radix
        for j in range(out.shape[0]):
            for k in range(radix):
                out[j, k] = third[0, start + j, 0, base + k]
        start += out.shape[0] if at % (groups - 1) == groups - 2 else 0


def second_kernel(radix, groups, second, *outs):
    group, member = place(radix)
    for i, out in zip((ALONG, BOTH), outs):
        for j in range(out.shape[0]):
            for delta in range(groups):
                out[j, delta] = second[0, j, 0, wrap(group - delta, groups) * radix + jnp.bitwise_xor(member, i)]


def leaf_order(row, leaves, row_size):
    per_leaf = row_size // leaves
    return [jnp.bitwise_xor(lax.div(row, per_leaf), t) for t in range(leaves)]


def weights_kernel(radix, groups, offs, row_size, first, second, fourth, out_basis, *outs):
    up_own, up_other, up_mid, off_rows, last_rows = outs
    levels = first.shape[3]
    slots = second.shape[3]
    rank = fourth.shape[6]
    half_rows = out_basis.shape[3]
    group, member = place(radix)
    for j in range(first.shape[1]):
        order = leaf_order(lax.axis_index("row"), radix, row_size) if j < offs else range(radix)

        def up(slot):
            level = lax.div(slot, slots // levels)
            mats = jnp.concatenate([first[0, j, 0, level, k] for k in order], axis=1)
            return dot(second[0, j, 0, slot], mats).astype(BF16)

        for i in range(radix):
            box = jnp.bitwise_xor(member, i)
            up_own[j, i] = up(group * radix + box)
            for delta in range(1, groups):
                up_other[j, i, delta - 1] = up(wrap(group - delta, groups) * radix + box)
        if j < offs:
            for delta in range(groups):
                slot = wrap(group - delta, groups) * radix + jnp.bitwise_xor(member, ALONG)
                level = lax.div(slot, slots // levels)
                up_mid[j, delta] = jnp.concatenate([first[0, j, 0, level, k] for k in order], axis=1)
        out, start = (off_rows, j * groups * rank) if j < offs else (last_rows, 0)
        for h in range(fourth.shape[3]):
            mats = [fourth[0, j, 0, h, wrap(group + delta, groups)] for delta in range(groups)]
            out[h * half_rows : (h + 1) * half_rows, start : start + groups * rank] = dot(
                out_basis[0, j, h], jnp.concatenate(mats, axis=1)
            ).astype(BF16)


def put_other(mats, leaf, other, at):
    radix, less, rank, depth = mats.shape
    coef = dot(mats[...].reshape(radix * less * rank, depth), leaf).astype(BF16)
    for i, ref in enumerate(other):
        ref[at] = coef[i * less * rank : (i + 1) * less * rank].reshape(ref.shape[1:])


def put_own(mats, leaf, own, at):
    radix, rank, depth = mats.shape
    coef = dot(mats[...].reshape(radix * rank, depth), leaf).astype(BF16)
    for i, ref in enumerate(own):
        ref[at] = coef[i * rank : (i + 1) * rank]


def off_kernel(pieces, basis, up_other, up_mid, *refs):
    parts, (leaf_ref, keep, across, along) = take(refs, pieces, 4)
    row = lax.axis_index("row")
    leaves, leaf_rows = basis.shape[2], basis.shape[3]
    rows = parts[0].shape[1]
    per_leaf = leaf_rows // rows
    order = leaf_order(row, leaves, pieces)
    less, rank, columns = keep.shape[1:]
    for j in range(parts[0].shape[0]):
        leaf = []
        for t in range(leaves):
            total = None
            for u in range(per_leaf):
                start = jnp.bitwise_xor(lax.rem(row, per_leaf), u) * rows
                if per_leaf == 1:
                    mat = basis[0, j, order[t]]
                else:
                    mat = basis[0, j, order[t], pl.ds(pl.multiple_of(start, rows), rows)]
                part = dot_t(mat, parts[t * per_leaf + u][j])
                total = part if total is None else total + part
            leaf.append(total.astype(BF16))
        leaf = jnp.concatenate(leaf, axis=0)
        leaf_ref[j] = leaf
        mats = [up_other[j, 0], up_other[j, ACROSS], up_mid[j, 1:]]
        mats = jnp.concatenate([m.reshape(less * rank, m.shape[2]) for m in mats], axis=0)
        coef = dot(mats, leaf).astype(BF16)
        for i, ref in enumerate((keep, across, along)):
            ref[j] = coef[i * less * rank : (i + 1) * less * rank].reshape(less, rank, columns)


def own_kernel(leaf, up_own, up_mid, *own):
    rank = up_mid.shape[2]
    for j in range(leaf.shape[0]):
        coef = dot(jnp.concatenate([up_own[j, 0], up_own[j, ACROSS], up_mid[j, 0]], axis=0), leaf[j]).astype(BF16)
        for i, ref in enumerate(own):
            ref[j] = coef[i * rank : (i + 1) * rank]


def slots_of(got, second_along, second_both, j, delta):
    keep, across, along, both = got
    return jnp.concatenate(
        [
            keep,
            across,
            dot(second_along[j, delta], along).astype(BF16),
            dot(second_both[j, delta], both).astype(BF16),
        ],
        axis=0,
    )


def off_sum_kernel(second_along, second_both, *refs):
    offs = second_along.shape[0]
    less = (len(refs) - 4) // (offs + 1)
    got, thirds, outs = take(refs, 4, offs * less, less)
    radix = thirds[0].shape[1]
    _, member = place(radix)
    for d, out in enumerate(outs):
        for j in range(offs):
            mats = [thirds[j * less + d][0, jnp.bitwise_xor(member, i)] for i in range(radix)]
            slots = slots_of([ref[j, d] for ref in got], second_along, second_both, j, d + 1)
            out[j] = dot(jnp.concatenate(mats, axis=1), slots).astype(BF16)


def sum_kernel(radix, *refs):
    got, thirds, outs = take(refs, radix, (len(refs) - radix) // 2, (len(refs) - radix) // 2)
    got = got[::-1]
    _, member = place(radix)
    for d, (third, out) in enumerate(zip(thirds, outs)):
        for j in range(out.shape[0]):
            mats = [third[j, jnp.bitwise_xor(member, i)] for i in range(radix)]
            slots = jnp.concatenate([ref[j, d] for ref in got], axis=0)
            out[j] = dot(jnp.concatenate(mats, axis=1), slots).astype(BF16)


def group_coef(j, slots, third, radix):
    group, member = place(radix)
    mats = [third[0, j, 0, group * radix + jnp.bitwise_xor(member, i)] for i in range(radix)]
    return dot(jnp.concatenate(mats, axis=1), slots).astype(BF16)


def middle_kernel(
    radix, groups, offs, third, rhs, basis, row_mats, up_own, up_other, second_along, second_both, *refs
):
    crossed, own_in, (residual_ref,), own, other = take(refs, groups - 1, radix, 1, radix, radix)
    coefs = []
    for j in range(offs):
        slots = slots_of([ref[j] for ref in own_in], second_along, second_both, j, 0)
        coefs += [group_coef(j, slots, third, radix)] + [ref[j] for ref in crossed]
    coefs = jnp.concatenate(coefs, axis=0)
    leaves, leaf_rows = basis.shape[2], basis.shape[3]
    leaf = []
    for k in range(leaves):
        rows = slice(k * leaf_rows, (k + 1) * leaf_rows)
        residual = rhs[0, rows].astype(F32) - dot(row_mats[rows], coefs)
        residual_ref[rows] = residual
        leaf.append(dot_t(basis[0, offs, k], residual.astype(BF16)).astype(BF16))
    leaf = jnp.concatenate(leaf, axis=0)
    put_other(up_other.at[offs], leaf, other, 0)
    put_own(up_own.at[offs], leaf, own, 0)


def last_kernel(radix, groups, offs, third, row_mats, residual, *refs):
    crossed, own_in, (out,) = take(refs, groups - 1, radix, 1)
    own_in = own_in[::-1]
    slots = jnp.concatenate([ref[0] for ref in own_in], axis=0)
    coefs = [group_coef(offs, slots, third, radix)] + [ref[0] for ref in crossed]
    coefs = jnp.concatenate(coefs, axis=0)
    out[0] = (residual[...] + dot(row_mats[...], coefs)).astype(BF16)


def after(array, *others):
    return lax.optimization_barrier((array, *others))[0]


def on_device(
    row_size, box_size, solved, rhs, leaf_basis, first_level, second_level, third_level, fourth_level, out_basis
):
    radix = first_level.shape[4]
    groups = box_size // radix
    less = groups - 1
    butterflies = leaf_basis.shape[1]
    offs = solved.shape[0]
    columns = solved.shape[2]
    rank = leaf_basis.shape[4]
    rows = rhs.shape[1]
    depth = radix * rank

    def over_row(array, mask):
        return lax.ppermute(array, "row", [(r, r ^ mask) for r in range(row_size)])

    def over_members(array, mask):
        pairs = [(b, (b // radix) * radix + ((b % radix) ^ mask)) for b in range(box_size)]
        return array if mask == 0 else lax.ppermute(array, "box", pairs)

    def over_groups(array, delta, mask=0):
        pairs = [
            (b, ((b // radix + delta) % groups) * radix + ((b % radix) ^ mask)) for b in range(box_size)
        ]
        return lax.ppermute(array, "box", pairs)

    def call(kernel, name, flops, outs, *args):
        outs = [jax.ShapeDtypeStruct(shape, dtype) for shape, dtype in outs]
        size = sum(a.size * a.dtype.itemsize for a in [*args, *outs])
        return pl.pallas_call(
            kernel,
            out_shape=outs,
            in_specs=[VMEM] * len(args),
            out_specs=[VMEM] * len(outs),
            compiler_params=pltpu.CompilerParams(vmem_limit_bytes=min(16 * MIB + 2 * size, 56 * MIB)),
            cost_estimate=pl.CostEstimate(flops=int(flops), bytes_accessed=0, transcendentals=0),
            name=name,
        )(*args)

    picked = call(
        functools.partial(pick_kernel, radix, groups),
        "pick_third",
        0,
        [((1, radix, rank, rank), BF16)] * (butterflies * less),
        third_level,
    )
    thirds = [
        [over_groups(a, d + 1) for d, a in enumerate(picked[j * less : (j + 1) * less])]
        for j in range(butterflies)
    ]

    up_own, up_other, up_mid, off_rows, last_rows = call(
        functools.partial(weights_kernel, radix, groups, offs, row_size),
        "weights",
        2 * butterflies * rank * (box_size * rank * depth + rows * groups * rank),
        [
            ((butterflies, radix, rank, depth), BF16),
            ((butterflies, radix, less, rank, depth), BF16),
            ((offs, groups, rank, depth), BF16),
            ((rows, offs * groups * rank), BF16),
            ((rows, groups * rank), BF16),
        ],
        first_level,
        second_level,
        fourth_level,
        out_basis,
    )

    seconds = call(
        functools.partial(second_kernel, radix, groups),
        "pick_second",
        0,
        [((offs, groups, rank, rank), BF16)] * 2,
        second_level,
    )
    seconds = [over_members(a, i) for i, a in zip((ALONG, BOTH), seconds)]

    pieces = [solved, over_row(solved, 1)]
    for mask in range(2, row_size, 2):
        far = after(over_row(solved, mask), up_own, *thirds[0], *seconds)
        pieces += [far, over_row(far, 1)]

    other_flops = 2 * columns * rank * radix * less * depth
    own_flops = 2 * columns * rank * radix * depth
    leaf_flops = 2 * columns * rank * rows
    row_flops = 2 * columns * rank * (depth + groups * rows)

    def own_out(count):
        return [((count, rank, columns), BF16)] * radix

    def other_out(count):
        return [((count, less, rank, columns), BF16)] * radix

    def cross(sums):
        return [over_groups(a, less - d) for d, a in enumerate(sums)]

    leaf, keep, across, along = call(
        functools.partial(off_kernel, row_size),
        "off_levels",
        offs * (leaf_flops + other_flops),
        [((offs, depth, columns), BF16)] + other_out(offs)[:3],
        leaf_basis,
        up_other,
        up_mid,
        *pieces,
    )
    along = over_members(along, ALONG)
    across = over_members(across, ACROSS)
    both = over_members(after(along, across, *[a for t in thirds[:offs] for a in t]), ACROSS)
    own = call(own_kernel, "own_levels", offs * own_flops, own_out(offs)[:3], leaf, up_own, up_mid)
    own_along = over_members(after(own[2], along), ALONG)
    sums = call(
        off_sum_kernel,
        "off_sums",
        offs * less * 2 * columns * rank * depth,
        [((offs, rank, columns), BF16)] * less,
        *seconds,
        keep,
        across,
        along,
        both,
        *[a for j in range(offs) for a in thirds[j]],
    )
    crossed = cross(sums)
    own = [
        own[0],
        over_members(after(own[1], both, *thirds[-1]), ACROSS),
        own_along,
    ]
    own.append(over_members(after(own_along, own[1], *sums), ACROSS))

    residual, *levels = call(
        functools.partial(middle_kernel, radix, groups, offs),
        "middle_levels",
        offs * row_flops + leaf_flops + other_flops + own_flops,
        [((rows, columns), F32)] + own_out(1) + other_out(1),
        third_level,
        rhs,
        leaf_basis,
        off_rows,
        up_own,
        up_other,
        *seconds,
        *crossed,
        *own,
    )
    own, other = levels[:radix], levels[radix:]
    other = [over_members(a, i) for i, a in reversed(list(enumerate(other)))]
    sums = call(
        functools.partial(sum_kernel, radix),
        "sums",
        less * 2 * columns * rank * depth,
        [((1, rank, columns), BF16)] * less,
        *other,
        *thirds[offs],
    )
    crossed = cross(sums)
    own = [over_members(after(a, *sums) if i else a, i) for i, a in enumerate(own)]
    return call(
        functools.partial(last_kernel, radix, groups, offs),
        "last_levels",
        row_flops,
        [((1, rows, columns), BF16)],
        third_level,
        last_rows,
        residual,
        *crossed,
        *own[::-1],
    )[0]


def solution(mesh):
    placed = (
        P(None, ("box", "row"), None),
        P("row", "box", None),
        P("row", None, "box", None, None),
        P("row", None, "box", None, None, None, None),
        P("row", None, "box", None, None, None),
        P("row", None, "box", None, None, None),
        P("row", None, "box", None, None, None, None),
        P("row", None, "box", None, None),
    )
    return jax.shard_map(
        functools.partial(on_device, mesh.shape["row"], mesh.shape["box"]),
        mesh=mesh,
        in_specs=placed,
        out_specs=P("row", "box", None),
        check_vma=False,
    )
```

```python
import functools

import jax
import jax.numpy as jnp
from jax import lax
from jax.experimental import pallas as pl
from jax.experimental.pallas import tpu as pltpu
from jax.sharding import PartitionSpec as P

F32 = jnp.float32
BF16 = jnp.bfloat16
MIB = 1024 * 1024
ACROSS, ALONG, BOTH = 1, 2, 3
VMEM = pl.BlockSpec(memory_space=pltpu.VMEM)


def dot(a, b):
    return jnp.dot(a, b, preferred_element_type=F32)


def dot_t(a, b):
    return lax.dot_general(a, b, (((0,), (0,)), ((), ())), preferred_element_type=F32)


def place(radix):
    box = lax.axis_index("box")
    return lax.div(box, radix), lax.rem(box, radix)


def wrap(value, size):
    return lax.rem(value + size, size)


def take(refs, *counts):
    refs, out = list(refs), []
    for count in counts:
        out.append(refs[:count])
        refs = refs[count:]
    return out


def pick_kernel(radix, groups, third, *outs):
    group, _ = place(radix)
    start = 0
    for at, out in enumerate(outs):
        base = wrap(group + at % (groups - 1) + 1, groups) * radix
        for j in range(out.shape[0]):
            for k in range(radix):
                out[j, k] = third[0, start + j, 0, base + k]
        start += out.shape[0] if at % (groups - 1) == groups - 2 else 0


def second_kernel(radix, groups, second, *outs):
    group, member = place(radix)
    for i, out in zip((ALONG, BOTH), outs):
        for j in range(out.shape[0]):
            for delta in range(groups):
                out[j, delta] = second[0, j, 0, wrap(group - delta, groups) * radix + jnp.bitwise_xor(member, i)]


def leaf_order(row, leaves, row_size):
    per_leaf = row_size // leaves
    return [jnp.bitwise_xor(lax.div(row, per_leaf), t) for t in range(leaves)]


def weights_kernel(radix, groups, offs, row_size, first, second, fourth, out_basis, *outs):
    up_own, up_other, up_mid, off_rows, last_rows = outs
    levels = first.shape[3]
    slots = second.shape[3]
    rank = fourth.shape[6]
    half_rows = out_basis.shape[3]
    group, member = place(radix)
    for j in range(first.shape[1]):
        order = leaf_order(lax.axis_index("row"), radix, row_size) if j < offs else range(radix)

        def up(slot):
            level = lax.div(slot, slots // levels)
            mats = jnp.concatenate([first[0, j, 0, level, k] for k in order], axis=1)
            return dot(second[0, j, 0, slot], mats).astype(BF16)

        for i in range(radix):
            box = jnp.bitwise_xor(member, i)
            up_own[j, i] = up(group * radix + box)
            for delta in range(1, groups):
                up_other[j, i, delta - 1] = up(wrap(group - delta, groups) * radix + box)
        if j < offs:
            for delta in range(groups):
                slot = wrap(group - delta, groups) * radix + jnp.bitwise_xor(member, ALONG)
                level = lax.div(slot, slots // levels)
                up_mid[j, delta] = jnp.concatenate([first[0, j, 0, level, k] for k in order], axis=1)
        out, start = (off_rows, j * groups * rank) if j < offs else (last_rows, 0)
        for h in range(fourth.shape[3]):
            mats = [fourth[0, j, 0, h, wrap(group + delta, groups)] for delta in range(groups)]
            out[h * half_rows : (h + 1) * half_rows, start : start + groups * rank] = dot(
                out_basis[0, j, h], jnp.concatenate(mats, axis=1)
            ).astype(BF16)


def put_other(mats, leaf, other, at):
    radix, less, rank, depth = mats.shape
    coef = dot(mats[...].reshape(radix * less * rank, depth), leaf).astype(BF16)
    for i, ref in enumerate(other):
        ref[at] = coef[i * less * rank : (i + 1) * less * rank].reshape(ref.shape[1:])


def put_own(mats, leaf, own, at):
    radix, rank, depth = mats.shape
    coef = dot(mats[...].reshape(radix * rank, depth), leaf).astype(BF16)
    for i, ref in enumerate(own):
        ref[at] = coef[i * rank : (i + 1) * rank]


def off_kernel(pieces, basis, up_other, up_mid, *refs):
    parts, (leaf_ref, keep, across, along) = take(refs, pieces, 4)
    row = lax.axis_index("row")
    leaves, leaf_rows = basis.shape[2], basis.shape[3]
    rows = parts[0].shape[1]
    per_leaf = leaf_rows // rows
    order = leaf_order(row, leaves, pieces)
    less, rank, columns = keep.shape[1:]
    for j in range(parts[0].shape[0]):
        leaf = []
        for t in range(leaves):
            total = None
            for u in range(per_leaf):
                start = jnp.bitwise_xor(lax.rem(row, per_leaf), u) * rows
                if per_leaf == 1:
                    mat = basis[0, j, order[t]]
                else:
                    mat = basis[0, j, order[t], pl.ds(pl.multiple_of(start, rows), rows)]
                part = dot_t(mat, parts[t * per_leaf + u][j])
                total = part if total is None else total + part
            leaf.append(total.astype(BF16))
        leaf = jnp.concatenate(leaf, axis=0)
        leaf_ref[j] = leaf
        mats = [up_other[j, 0], up_other[j, ACROSS], up_mid[j, 1:]]
        mats = jnp.concatenate([m.reshape(less * rank, m.shape[2]) for m in mats], axis=0)
        coef = dot(mats, leaf).astype(BF16)
        for i, ref in enumerate((keep, across, along)):
            ref[j] = coef[i * less * rank : (i + 1) * less * rank].reshape(less, rank, columns)


def own_kernel(leaf, up_own, up_mid, *own):
    rank = up_mid.shape[2]
    for j in range(leaf.shape[0]):
        coef = dot(jnp.concatenate([up_own[j, 0], up_own[j, ACROSS], up_mid[j, 0]], axis=0), leaf[j]).astype(BF16)
        for i, ref in enumerate(own):
            ref[j] = coef[i * rank : (i + 1) * rank]


def slots_of(got, second_along, second_both, j, delta):
    keep, across, along, both = got
    return jnp.concatenate(
        [
            keep,
            across,
            dot(second_along[j, delta], along).astype(BF16),
            dot(second_both[j, delta], both).astype(BF16),
        ],
        axis=0,
    )


def off_sum_kernel(second_along, second_both, *refs):
    offs = second_along.shape[0]
    less = (len(refs) - 4) // (offs + 1)
    got, thirds, outs = take(refs, 4, offs * less, less)
    radix = thirds[0].shape[1]
    _, member = place(radix)
    for d, out in enumerate(outs):
        for j in range(offs):
            mats = [thirds[j * less + d][0, jnp.bitwise_xor(member, i)] for i in range(radix)]
            slots = slots_of([ref[j, d] for ref in got], second_along, second_both, j, d + 1)
            out[j] = dot(jnp.concatenate(mats, axis=1), slots).astype(BF16)


def last_own_kernel(leaf, up_own, *own):
    put_own(up_own.at[up_own.shape[0] - 1], leaf[...], own, 0)


def sum_kernel(radix, *refs):
    got, thirds, outs = take(refs, radix, (len(refs) - radix) // 2, (len(refs) - radix) // 2)
    got = got[::-1]
    _, member = place(radix)
    for d, (third, out) in enumerate(zip(thirds, outs)):
        for j in range(out.shape[0]):
            mats = [third[j, jnp.bitwise_xor(member, i)] for i in range(radix)]
            slots = jnp.concatenate([ref[j, d] for ref in got], axis=0)
            out[j] = dot(jnp.concatenate(mats, axis=1), slots).astype(BF16)


def group_coef(j, slots, third, radix):
    group, member = place(radix)
    mats = [third[0, j, 0, group * radix + jnp.bitwise_xor(member, i)] for i in range(radix)]
    return dot(jnp.concatenate(mats, axis=1), slots).astype(BF16)


def middle_kernel(
    radix, groups, offs, third, rhs, basis, row_mats, up_other, second_along, second_both, *refs
):
    crossed, own_in, (residual_ref, leaf_ref), other = take(refs, groups - 1, radix, 2, radix)
    coefs = []
    for j in range(offs):
        slots = slots_of([ref[j] for ref in own_in], second_along, second_both, j, 0)
        coefs += [group_coef(j, slots, third, radix)] + [ref[j] for ref in crossed]
    coefs = jnp.concatenate(coefs, axis=0)
    leaves, leaf_rows = basis.shape[2], basis.shape[3]
    leaf = []
    for k in range(leaves):
        rows = slice(k * leaf_rows, (k + 1) * leaf_rows)
        residual = rhs[0, rows].astype(F32) - dot(row_mats[rows], coefs)
        residual_ref[rows] = residual
        leaf.append(dot_t(basis[0, offs, k], residual.astype(BF16)).astype(BF16))
    leaf = jnp.concatenate(leaf, axis=0)
    leaf_ref[...] = leaf
    put_other(up_other.at[offs], leaf, other, 0)


def last_kernel(radix, groups, offs, third, row_mats, residual, *refs):
    crossed, own_in, (out, held, sem) = take(refs, groups - 1, radix, 3)
    slots = jnp.concatenate([ref[0] for ref in own_in[::-1]], axis=0)
    coefs = [group_coef(offs, slots, third, radix)] + [ref[0] for ref in crossed]
    coefs = jnp.concatenate(coefs, axis=0)
    count = sem.shape[0]
    height = residual.shape[0] // count
    copies = []
    for i in range(count):
        rows = pl.ds(i * height, height)
        held[rows] = (residual[rows] + dot(row_mats[rows], coefs)).astype(BF16)
        copies.append(pltpu.make_async_copy(held.at[rows], out.at[0, rows], sem.at[i]))
        copies[-1].start()
    for copy in copies:
        copy.wait()


def after(array, *others):
    return lax.optimization_barrier((array, *others))[0]


def on_device(
    row_size, box_size, solved, rhs, leaf_basis, first_level, second_level, third_level, fourth_level, out_basis
):
    radix = first_level.shape[4]
    groups = box_size // radix
    less = groups - 1
    butterflies = leaf_basis.shape[1]
    offs = solved.shape[0]
    columns = solved.shape[2]
    rank = leaf_basis.shape[4]
    rows = rhs.shape[1]
    depth = radix * rank

    def over_row(array, mask):
        return lax.ppermute(array, "row", [(r, r ^ mask) for r in range(row_size)])

    def over_members(array, mask):
        pairs = [(b, (b // radix) * radix + ((b % radix) ^ mask)) for b in range(box_size)]
        return array if mask == 0 else lax.ppermute(array, "box", pairs)

    def over_groups(array, delta, mask=0):
        pairs = [
            (b, ((b // radix + delta) % groups) * radix + ((b % radix) ^ mask)) for b in range(box_size)
        ]
        return lax.ppermute(array, "box", pairs)

    def call(kernel, name, flops, outs, *args):
        outs = [jax.ShapeDtypeStruct(shape, dtype) for shape, dtype in outs]
        size = sum(a.size * a.dtype.itemsize for a in [*args, *outs])
        return pl.pallas_call(
            kernel,
            out_shape=outs,
            in_specs=[VMEM] * len(args),
            out_specs=[VMEM] * len(outs),
            compiler_params=pltpu.CompilerParams(vmem_limit_bytes=min(16 * MIB + 2 * size, 56 * MIB)),
            cost_estimate=pl.CostEstimate(flops=int(flops), bytes_accessed=0, transcendentals=0),
            name=name,
        )(*args)

    picked = call(
        functools.partial(pick_kernel, radix, groups),
        "pick_third",
        0,
        [((1, radix, rank, rank), BF16)] * (butterflies * less),
        third_level,
    )
    thirds = [
        [over_groups(a, d + 1) for d, a in enumerate(picked[j * less : (j + 1) * less])]
        for j in range(butterflies)
    ]

    up_own, up_other, up_mid, off_rows, last_rows = call(
        functools.partial(weights_kernel, radix, groups, offs, row_size),
        "weights",
        2 * butterflies * rank * (box_size * rank * depth + rows * groups * rank),
        [
            ((butterflies, radix, rank, depth), BF16),
            ((butterflies, radix, less, rank, depth), BF16),
            ((offs, groups, rank, depth), BF16),
            ((rows, offs * groups * rank), BF16),
            ((rows, groups * rank), BF16),
        ],
        first_level,
        second_level,
        fourth_level,
        out_basis,
    )

    seconds = call(
        functools.partial(second_kernel, radix, groups),
        "pick_second",
        0,
        [((offs, groups, rank, rank), BF16)] * 2,
        second_level,
    )
    seconds = [over_members(a, i) for i, a in zip((ALONG, BOTH), seconds)]

    pieces = [solved, over_row(solved, 1)]
    for mask in range(2, row_size, 2):
        far = after(over_row(solved, mask), up_own, *seconds, *thirds[0])
        pieces += [far, over_row(far, 1)]

    other_flops = 2 * columns * rank * radix * less * depth
    own_flops = 2 * columns * rank * radix * depth
    leaf_flops = 2 * columns * rank * rows
    row_flops = 2 * columns * rank * (depth + groups * rows)

    def own_out(count):
        return [((count, rank, columns), BF16)] * radix

    def other_out(count):
        return [((count, less, rank, columns), BF16)] * radix

    def cross(sums):
        return [over_groups(a, less - d) for d, a in enumerate(sums)]

    leaf, keep, across, along = call(
        functools.partial(off_kernel, row_size),
        "off_levels",
        offs * (leaf_flops + other_flops),
        [((offs, depth, columns), BF16)] + other_out(offs)[:3],
        leaf_basis,
        up_other,
        up_mid,
        *pieces,
    )
    along = over_members(along, ALONG)
    across = over_members(across, ACROSS)
    both = over_members(after(along, across, *[a for t in thirds[:offs] for a in t]), ACROSS)
    own = call(own_kernel, "own_levels", offs * own_flops, own_out(offs)[:3], leaf, up_own, up_mid)
    own_along = over_members(after(own[2], along), ALONG)
    sums = call(
        off_sum_kernel,
        "off_sums",
        offs * less * 2 * columns * rank * depth,
        [((offs, rank, columns), BF16)] * less,
        *seconds,
        keep,
        across,
        along,
        both,
        *[a for j in range(offs) for a in thirds[j]],
    )
    crossed = cross(sums)
    own = [
        own[0],
        over_members(after(own[1], both, *thirds[-1]), ACROSS),
        own_along,
    ]
    own.append(over_members(after(own_along, own[1], *sums), ACROSS))

    residual, leaf, *other = call(
        functools.partial(middle_kernel, radix, groups, offs),
        "middle_levels",
        offs * row_flops + leaf_flops + other_flops + own_flops,
        [((rows, columns), F32), ((depth, columns), BF16)] + other_out(1),
        third_level,
        rhs,
        leaf_basis,
        off_rows,
        up_other,
        *seconds,
        *crossed,
        *own,
    )
    own = call(last_own_kernel, "last_own_levels", own_flops, own_out(1), leaf, up_own)
    other = [over_members(a, i) for i, a in reversed(list(enumerate(other)))]
    sums = call(
        functools.partial(sum_kernel, radix),
        "sums",
        less * 2 * columns * rank * depth,
        [((1, rank, columns), BF16)] * less,
        *other,
        *thirds[offs],
    )
    crossed = cross(sums)
    own = [over_members(after(a, *sums) if i else a, i) for i, a in enumerate(own)]
    args = [third_level, last_rows, residual, *crossed, *own[::-1]]
    return pl.pallas_call(
        functools.partial(last_kernel, radix, groups, offs),
        out_shape=jax.ShapeDtypeStruct((1, rows, columns), BF16),
        in_specs=[VMEM] * len(args),
        out_specs=pl.BlockSpec(memory_space=pltpu.HBM),
        scratch_shapes=[pltpu.VMEM((rows, columns), BF16), pltpu.SemaphoreType.DMA((4,))],
        compiler_params=pltpu.CompilerParams(vmem_limit_bytes=32 * MIB),
        cost_estimate=pl.CostEstimate(flops=row_flops, bytes_accessed=0, transcendentals=0),
        name="last_levels",
    )(*args)


def solution(mesh):
    placed = (
        P(None, ("box", "row"), None),
        P("row", "box", None),
        P("row", None, "box", None, None),
        P("row", None, "box", None, None, None, None),
        P("row", None, "box", None, None, None),
        P("row", None, "box", None, None, None),
        P("row", None, "box", None, None, None, None),
        P("row", None, "box", None, None),
    )
    return jax.shard_map(
        functools.partial(on_device, mesh.shape["row"], mesh.shape["box"]),
        mesh=mesh,
        in_specs=placed,
        out_specs=P("row", "box", None),
        check_vma=False,
    )
```

```python
import functools

import jax
import jax.numpy as jnp
from jax import lax
from jax.experimental import pallas as pl
from jax.experimental.pallas import tpu as pltpu
from jax.sharding import PartitionSpec as P

F32 = jnp.float32
BF16 = jnp.bfloat16
MIB = 1024 * 1024
ACROSS, ALONG, BOTH = 1, 2, 3
VMEM = pl.BlockSpec(memory_space=pltpu.VMEM)


def dot(a, b):
    return jnp.dot(a, b, preferred_element_type=F32)


def dot_t(a, b):
    return lax.dot_general(a, b, (((0,), (0,)), ((), ())), preferred_element_type=F32)


def place(radix):
    box = lax.axis_index("box")
    return lax.div(box, radix), lax.rem(box, radix)


def wrap(value, size):
    return lax.rem(value + size, size)


def take(refs, *counts):
    refs, out = list(refs), []
    for count in counts:
        out.append(refs[:count])
        refs = refs[count:]
    return out


def pick_kernel(radix, groups, third, *outs):
    group, _ = place(radix)
    start = 0
    for at in range(0, len(outs), groups - 1):
        count = outs[at].shape[0]
        for delta in range(1, groups):
            base = wrap(group + delta, groups) * radix
            for p in range(count):
                j, k = divmod(start + p, radix)
                outs[at + delta - 1][p] = third[0, j, 0, base + k]
        start += count


def second_kernel(radix, groups, second, *outs):
    group, member = place(radix)
    for i, out in zip((ALONG, BOTH), outs):
        for j in range(out.shape[0]):
            for delta in range(groups):
                out[j, delta] = second[0, j, 0, wrap(group - delta, groups) * radix + jnp.bitwise_xor(member, i)]


def leaf_order(row, leaves, row_size):
    per_leaf = row_size // leaves
    return [jnp.bitwise_xor(lax.div(row, per_leaf), t) for t in range(leaves)]


def weights_kernel(radix, groups, offs, row_size, first, second, fourth, out_basis, *outs):
    up_own, up_other, up_mid, off_rows, last_rows = outs
    levels = first.shape[3]
    slots = second.shape[3]
    rank = fourth.shape[6]
    half_rows = out_basis.shape[3]
    group, member = place(radix)
    for j in range(first.shape[1]):
        order = leaf_order(lax.axis_index("row"), radix, row_size) if j < offs else range(radix)

        def up(slot):
            level = lax.div(slot, slots // levels)
            mats = jnp.concatenate([first[0, j, 0, level, k] for k in order], axis=1)
            return dot(second[0, j, 0, slot], mats).astype(BF16)

        for i in range(radix):
            box = jnp.bitwise_xor(member, i)
            up_own[j, i] = up(group * radix + box)
            for delta in range(1, groups):
                up_other[j, i, delta - 1] = up(wrap(group - delta, groups) * radix + box)
        if j < offs:
            for delta in range(groups):
                slot = wrap(group - delta, groups) * radix + jnp.bitwise_xor(member, ALONG)
                level = lax.div(slot, slots // levels)
                up_mid[j, delta] = jnp.concatenate([first[0, j, 0, level, k] for k in order], axis=1)
        out, start = (off_rows, j * groups * rank) if j < offs else (last_rows, 0)
        for h in range(fourth.shape[3]):
            mats = [fourth[0, j, 0, h, wrap(group + delta, groups)] for delta in range(groups)]
            out[h * half_rows : (h + 1) * half_rows, start : start + groups * rank] = dot(
                out_basis[0, j, h], jnp.concatenate(mats, axis=1)
            ).astype(BF16)


def put_other(mats, leaf, other, at):
    radix, less, rank, depth = mats.shape
    coef = dot(mats[...].reshape(radix * less * rank, depth), leaf).astype(BF16)
    for i, ref in enumerate(other):
        ref[at] = coef[i * less * rank : (i + 1) * less * rank].reshape(ref.shape[1:])


def put_own(mats, leaf, own, at):
    radix, rank, depth = mats.shape
    coef = dot(mats[...].reshape(radix * rank, depth), leaf).astype(BF16)
    for i, ref in enumerate(own):
        ref[at] = coef[i * rank : (i + 1) * rank]


def off_kernel(pieces, basis, up_other, up_mid, *refs):
    parts, (leaf_ref, keep, across, along) = take(refs, pieces, 4)
    row = lax.axis_index("row")
    leaves, leaf_rows = basis.shape[2], basis.shape[3]
    rows = parts[0].shape[1]
    per_leaf = leaf_rows // rows
    order = leaf_order(row, leaves, pieces)
    less, rank, columns = keep.shape[1:]
    for j in range(parts[0].shape[0]):
        leaf = []
        for t in range(leaves):
            total = None
            for u in range(per_leaf):
                start = jnp.bitwise_xor(lax.rem(row, per_leaf), u) * rows
                if per_leaf == 1:
                    mat = basis[0, j, order[t]]
                else:
                    mat = basis[0, j, order[t], pl.ds(pl.multiple_of(start, rows), rows)]
                part = dot_t(mat, parts[t * per_leaf + u][j])
                total = part if total is None else total + part
            leaf.append(total.astype(BF16))
        leaf = jnp.concatenate(leaf, axis=0)
        leaf_ref[j] = leaf
        mats = [up_other[j, 0], up_other[j, ACROSS], up_mid[j, 1:]]
        mats = jnp.concatenate([m.reshape(less * rank, m.shape[2]) for m in mats], axis=0)
        coef = dot(mats, leaf).astype(BF16)
        for i, ref in enumerate((keep, across, along)):
            ref[j] = coef[i * less * rank : (i + 1) * less * rank].reshape(less, rank, columns)


def own_kernel(leaf, up_own, up_mid, *own):
    rank = up_mid.shape[2]
    for j in range(leaf.shape[0]):
        coef = dot(jnp.concatenate([up_own[j, 0], up_own[j, ACROSS], up_mid[j, 0]], axis=0), leaf[j]).astype(BF16)
        for i, ref in enumerate(own):
            ref[j] = coef[i * rank : (i + 1) * rank]


def slots_of(got, second_along, second_both, j, delta):
    keep, across, along, both = got
    return jnp.concatenate(
        [
            keep,
            across,
            dot(second_along[j, delta], along).astype(BF16),
            dot(second_both[j, delta], both).astype(BF16),
        ],
        axis=0,
    )


def off_sum_kernel(radix, second_along, second_both, *refs):
    less = (len(refs) - 5) // 3
    got, early, late, outs, (held,) = take(refs, 4, less, less, less, 1)
    _, member = place(radix)
    for d, out in enumerate(outs):
        count = early[d].shape[0]
        held[:count] = early[d][...]
        held[count:] = late[d][...]
        for j in range(out.shape[0]):
            mats = [held[j * radix + jnp.bitwise_xor(member, i)] for i in range(radix)]
            slots = slots_of([ref[j, d] for ref in got], second_along, second_both, j, d + 1)
            out[j] = dot(jnp.concatenate(mats, axis=1), slots).astype(BF16)


def last_own_kernel(leaf, up_own, *own):
    put_own(up_own.at[up_own.shape[0] - 1], leaf[...], own, 0)


def sum_kernel(radix, *refs):
    got, thirds, outs = take(refs, radix, (len(refs) - radix) // 2, (len(refs) - radix) // 2)
    got = got[::-1]
    _, member = place(radix)
    for d, (third, out) in enumerate(zip(thirds, outs)):
        for j in range(out.shape[0]):
            mats = [third[jnp.bitwise_xor(member, i)] for i in range(radix)]
            slots = jnp.concatenate([ref[j, d] for ref in got], axis=0)
            out[j] = dot(jnp.concatenate(mats, axis=1), slots).astype(BF16)


def group_coef(j, slots, third, radix):
    group, member = place(radix)
    mats = [third[0, j, 0, group * radix + jnp.bitwise_xor(member, i)] for i in range(radix)]
    return dot(jnp.concatenate(mats, axis=1), slots).astype(BF16)


def middle_kernel(
    radix, groups, offs, third, rhs, basis, row_mats, up_other, second_along, second_both, *refs
):
    crossed, own_in, (residual_ref, leaf_ref), other = take(refs, groups - 1, radix, 2, radix)
    coefs = []
    for j in range(offs):
        slots = slots_of([ref[j] for ref in own_in], second_along, second_both, j, 0)
        coefs += [group_coef(j, slots, third, radix)] + [ref[j] for ref in crossed]
    coefs = jnp.concatenate(coefs, axis=0)
    leaves, leaf_rows = basis.shape[2], basis.shape[3]
    leaf = []
    for k in range(leaves):
        rows = slice(k * leaf_rows, (k + 1) * leaf_rows)
        residual = rhs[0, rows].astype(F32) - dot(row_mats[rows], coefs)
        residual_ref[rows] = residual
        leaf.append(dot_t(basis[0, offs, k], residual.astype(BF16)).astype(BF16))
    leaf = jnp.concatenate(leaf, axis=0)
    leaf_ref[...] = leaf
    put_other(up_other.at[offs], leaf, other, 0)


def last_kernel(radix, groups, offs, third, row_mats, residual, *refs):
    crossed, own_in, (out, held, sem) = take(refs, groups - 1, radix, 3)
    slots = jnp.concatenate([ref[0] for ref in own_in[::-1]], axis=0)
    coefs = [group_coef(offs, slots, third, radix)] + [ref[0] for ref in crossed]
    coefs = jnp.concatenate(coefs, axis=0)
    count = sem.shape[0]
    height = residual.shape[0] // count
    copies = []
    for i in range(count):
        rows = pl.ds(i * height, height)
        held[rows] = (residual[rows] + dot(row_mats[rows], coefs)).astype(BF16)
        copies.append(pltpu.make_async_copy(held.at[rows], out.at[0, rows], sem.at[i]))
        copies[-1].start()
    for copy in copies:
        copy.wait()


def after(array, *others):
    return lax.optimization_barrier((array, *others))[0]


def on_device(
    row_size, box_size, solved, rhs, leaf_basis, first_level, second_level, third_level, fourth_level, out_basis
):
    radix = first_level.shape[4]
    groups = box_size // radix
    less = groups - 1
    butterflies = leaf_basis.shape[1]
    offs = solved.shape[0]
    columns = solved.shape[2]
    rank = leaf_basis.shape[4]
    rows = rhs.shape[1]
    depth = radix * rank

    def over_row(array, mask):
        return lax.ppermute(array, "row", [(r, r ^ mask) for r in range(row_size)])

    def over_members(array, mask):
        pairs = [(b, (b // radix) * radix + ((b % radix) ^ mask)) for b in range(box_size)]
        return array if mask == 0 else lax.ppermute(array, "box", pairs)

    def over_groups(array, delta, mask=0):
        pairs = [
            (b, ((b // radix + delta) % groups) * radix + ((b % radix) ^ mask)) for b in range(box_size)
        ]
        return lax.ppermute(array, "box", pairs)

    def call(kernel, name, flops, outs, *args, scratch=()):
        outs = [jax.ShapeDtypeStruct(shape, dtype) for shape, dtype in outs]
        size = sum(a.size * a.dtype.itemsize for a in [*args, *outs])
        return pl.pallas_call(
            kernel,
            out_shape=outs,
            in_specs=[VMEM] * len(args),
            out_specs=[VMEM] * len(outs),
            scratch_shapes=list(scratch),
            compiler_params=pltpu.CompilerParams(vmem_limit_bytes=min(16 * MIB + 2 * size, 56 * MIB)),
            cost_estimate=pl.CostEstimate(flops=int(flops), bytes_accessed=0, transcendentals=0),
            name=name,
        )(*args)

    early = radix + (offs - 1) * radix // 4
    counts = [early, offs * radix - early, (butterflies - offs) * radix]
    picked = call(
        functools.partial(pick_kernel, radix, groups),
        "pick_third",
        0,
        [((count, rank, rank), BF16) for count in counts for _ in range(less)],
        third_level,
    )
    thirds = [
        [over_groups(a, d + 1) for d, a in enumerate(picked[at : at + less])] for at in range(0, len(picked), less)
    ]

    up_own, up_other, up_mid, off_rows, last_rows = call(
        functools.partial(weights_kernel, radix, groups, offs, row_size),
        "weights",
        2 * butterflies * rank * (box_size * rank * depth + rows * groups * rank),
        [
            ((butterflies, radix, rank, depth), BF16),
            ((butterflies, radix, less, rank, depth), BF16),
            ((offs, groups, rank, depth), BF16),
            ((rows, offs * groups * rank), BF16),
            ((rows, groups * rank), BF16),
        ],
        first_level,
        second_level,
        fourth_level,
        out_basis,
    )

    seconds = call(
        functools.partial(second_kernel, radix, groups),
        "pick_second",
        0,
        [((offs, groups, rank, rank), BF16)] * 2,
        second_level,
    )
    seconds = [over_members(a, i) for i, a in zip((ALONG, BOTH), seconds)]

    pieces = [solved, over_row(solved, 1)]
    for mask in range(2, row_size, 2):
        far = after(over_row(solved, mask), up_own, *seconds, *thirds[0])
        pieces += [far, over_row(far, 1)]

    other_flops = 2 * columns * rank * radix * less * depth
    own_flops = 2 * columns * rank * radix * depth
    leaf_flops = 2 * columns * rank * rows
    row_flops = 2 * columns * rank * (depth + groups * rows)

    def own_out(count):
        return [((count, rank, columns), BF16)] * radix

    def other_out(count):
        return [((count, less, rank, columns), BF16)] * radix

    def cross(sums):
        return [over_groups(a, less - d) for d, a in enumerate(sums)]

    leaf, keep, across, along = call(
        functools.partial(off_kernel, row_size),
        "off_levels",
        offs * (leaf_flops + other_flops),
        [((offs, depth, columns), BF16)] + other_out(offs)[:3],
        leaf_basis,
        up_other,
        up_mid,
        *pieces,
    )
    along = over_members(along, ALONG)
    across = over_members(across, ACROSS)
    both = over_members(after(along, across, *thirds[0], *thirds[1]), ACROSS)
    own = call(own_kernel, "own_levels", offs * own_flops, own_out(offs)[:3], leaf, up_own, up_mid)
    own_along = over_members(after(own[2], along), ALONG)
    sums = call(
        functools.partial(off_sum_kernel, radix),
        "off_sums",
        offs * less * 2 * columns * rank * depth,
        [((offs, rank, columns), BF16)] * less,
        *seconds,
        keep,
        across,
        along,
        both,
        *thirds[0],
        *thirds[1],
        scratch=[pltpu.VMEM((offs * radix, rank, rank), BF16)],
    )
    crossed = cross(sums)
    own = [
        own[0],
        over_members(after(own[1], both, *thirds[2]), ACROSS),
        own_along,
    ]
    own.append(over_members(after(own_along, own[1], *sums), ACROSS))

    residual, leaf, *other = call(
        functools.partial(middle_kernel, radix, groups, offs),
        "middle_levels",
        offs * row_flops + leaf_flops + other_flops + own_flops,
        [((rows, columns), F32), ((depth, columns), BF16)] + other_out(1),
        third_level,
        rhs,
        leaf_basis,
        off_rows,
        up_other,
        *seconds,
        *crossed,
        *own,
    )
    own = call(last_own_kernel, "last_own_levels", own_flops, own_out(1), leaf, up_own)
    other = [over_members(a, i) for i, a in reversed(list(enumerate(other)))]
    sums = call(
        functools.partial(sum_kernel, radix),
        "sums",
        less * 2 * columns * rank * depth,
        [((1, rank, columns), BF16)] * less,
        *other,
        *thirds[2],
    )
    crossed = cross(sums)
    own = [over_members(after(a, *sums) if i else a, i) for i, a in enumerate(own)]
    args = [third_level, last_rows, residual, *crossed, *own[::-1]]
    return pl.pallas_call(
        functools.partial(last_kernel, radix, groups, offs),
        out_shape=jax.ShapeDtypeStruct((1, rows, columns), BF16),
        in_specs=[VMEM] * len(args),
        out_specs=pl.BlockSpec(memory_space=pltpu.HBM),
        scratch_shapes=[pltpu.VMEM((rows, columns), BF16), pltpu.SemaphoreType.DMA((4,))],
        compiler_params=pltpu.CompilerParams(vmem_limit_bytes=32 * MIB),
        cost_estimate=pl.CostEstimate(flops=row_flops, bytes_accessed=0, transcendentals=0),
        name="last_levels",
    )(*args)


def solution(mesh):
    placed = (
        P(None, ("box", "row"), None),
        P("row", "box", None),
        P("row", None, "box", None, None),
        P("row", None, "box", None, None, None, None),
        P("row", None, "box", None, None, None),
        P("row", None, "box", None, None, None),
        P("row", None, "box", None, None, None, None),
        P("row", None, "box", None, None),
    )
    return jax.shard_map(
        functools.partial(on_device, mesh.shape["row"], mesh.shape["box"]),
        mesh=mesh,
        in_specs=placed,
        out_specs=P("row", "box", None),
        check_vma=False,
    )
```

```python
import functools

import jax
import jax.numpy as jnp
from jax import lax
from jax.experimental import pallas as pl
from jax.experimental.pallas import tpu as pltpu
from jax.sharding import PartitionSpec as P

F32 = jnp.float32
BF16 = jnp.bfloat16
MIB = 1024 * 1024
ACROSS, ALONG, BOTH = 1, 2, 3
VMEM = pl.BlockSpec(memory_space=pltpu.VMEM)


def dot(a, b):
    return jnp.dot(a, b, preferred_element_type=F32)


def dot_t(a, b):
    return lax.dot_general(a, b, (((0,), (0,)), ((), ())), preferred_element_type=F32)


def place(radix):
    box = lax.axis_index("box")
    return lax.div(box, radix), lax.rem(box, radix)


def wrap(value, size):
    return lax.rem(value + size, size)


def take(refs, *counts):
    refs, out = list(refs), []
    for count in counts:
        out.append(refs[:count])
        refs = refs[count:]
    return out


def pick_kernel(radix, groups, third, *outs):
    group, _ = place(radix)
    start = 0
    for at, out in enumerate(outs):
        base = wrap(group + at % (groups - 1) + 1, groups) * radix
        for j in range(out.shape[0]):
            for k in range(radix):
                out[j, k] = third[0, start + j, 0, base + k]
        start += out.shape[0] if at % (groups - 1) == groups - 2 else 0


def second_kernel(radix, groups, second, *outs):
    group, member = place(radix)
    for i, out in zip((ALONG, BOTH), outs):
        for j in range(out.shape[0]):
            for delta in range(groups):
                out[j, delta] = second[0, j, 0, wrap(group - delta, groups) * radix + jnp.bitwise_xor(member, i)]


def leaf_order(row, leaves, row_size):
    per_leaf = row_size // leaves
    return [jnp.bitwise_xor(lax.div(row, per_leaf), t) for t in range(leaves)]


def weights_kernel(radix, groups, offs, row_size, first, second, fourth, out_basis, *outs):
    up_own, up_other, up_mid, off_rows, last_rows = outs
    levels = first.shape[3]
    slots = second.shape[3]
    rank = fourth.shape[6]
    half_rows = out_basis.shape[3]
    group, member = place(radix)
    for j in range(first.shape[1]):
        order = leaf_order(lax.axis_index("row"), radix, row_size) if j < offs else range(radix)

        def up(slot):
            level = lax.div(slot, slots // levels)
            mats = jnp.concatenate([first[0, j, 0, level, k] for k in order], axis=1)
            return dot(second[0, j, 0, slot], mats).astype(BF16)

        for i in range(radix):
            box = jnp.bitwise_xor(member, i)
            up_own[j, i] = up(group * radix + box)
            for delta in range(1, groups):
                up_other[j, i, delta - 1] = up(wrap(group - delta, groups) * radix + box)
        if j < offs:
            for delta in range(groups):
                slot = wrap(group - delta, groups) * radix + jnp.bitwise_xor(member, ALONG)
                level = lax.div(slot, slots // levels)
                up_mid[j, delta] = jnp.concatenate([first[0, j, 0, level, k] for k in order], axis=1)
        out, start = (off_rows, j * groups * rank) if j < offs else (last_rows, 0)
        for h in range(fourth.shape[3]):
            mats = [fourth[0, j, 0, h, wrap(group + delta, groups)] for delta in range(groups)]
            out[h * half_rows : (h + 1) * half_rows, start : start + groups * rank] = dot(
                out_basis[0, j, h], jnp.concatenate(mats, axis=1)
            ).astype(BF16)


def put_other(mats, leaf, other, at):
    radix, less, rank, depth = mats.shape
    coef = dot(mats[...].reshape(radix * less * rank, depth), leaf).astype(BF16)
    for i, ref in enumerate(other):
        ref[at] = coef[i * less * rank : (i + 1) * less * rank].reshape(ref.shape[1:])


def put_own(mats, leaf, own, at):
    radix, rank, depth = mats.shape
    coef = dot(mats[...].reshape(radix * rank, depth), leaf).astype(BF16)
    for i, ref in enumerate(own):
        ref[at] = coef[i * rank : (i + 1) * rank]


def off_kernel(pieces, basis, up_other, up_mid, *refs):
    parts, (leaf_ref, keep, across, along) = take(refs, pieces, 4)
    row = lax.axis_index("row")
    leaves, leaf_rows = basis.shape[2], basis.shape[3]
    rows = parts[0].shape[1]
    per_leaf = leaf_rows // rows
    order = leaf_order(row, leaves, pieces)
    less, rank, columns = keep.shape[1:]
    for j in range(parts[0].shape[0]):
        leaf = []
        for t in range(leaves):
            total = None
            for u in range(per_leaf):
                start = jnp.bitwise_xor(lax.rem(row, per_leaf), u) * rows
                if per_leaf == 1:
                    mat = basis[0, j, order[t]]
                else:
                    mat = basis[0, j, order[t], pl.ds(pl.multiple_of(start, rows), rows)]
                part = dot_t(mat, parts[t * per_leaf + u][j])
                total = part if total is None else total + part
            leaf.append(total.astype(BF16))
        leaf = jnp.concatenate(leaf, axis=0)
        leaf_ref[j] = leaf
        mats = [up_other[j, 0], up_other[j, ACROSS], up_mid[j, 1:]]
        mats = jnp.concatenate([m.reshape(less * rank, m.shape[2]) for m in mats], axis=0)
        coef = dot(mats, leaf).astype(BF16)
        for i, ref in enumerate((keep, across, along)):
            ref[j] = coef[i * less * rank : (i + 1) * less * rank].reshape(less, rank, columns)


def own_kernel(leaf, up_own, up_mid, *own):
    rank = up_mid.shape[2]
    for j in range(leaf.shape[0]):
        coef = dot(jnp.concatenate([up_own[j, 0], up_own[j, ACROSS], up_mid[j, 0]], axis=0), leaf[j]).astype(BF16)
        for i, ref in enumerate(own):
            ref[j] = coef[i * rank : (i + 1) * rank]


def slots_of(got, second_along, second_both, j, delta):
    keep, along, across, both = got
    return jnp.concatenate(
        [
            keep,
            across,
            dot(second_along[j, delta], along).astype(BF16),
            dot(second_both[j, delta], both).astype(BF16),
        ],
        axis=0,
    )


def off_sum_kernel(second_along, second_both, *refs):
    offs = second_along.shape[0]
    less = (len(refs) - 4) // (offs + 1)
    got, thirds, outs = take(refs, 4, offs * less, less)
    radix = thirds[0].shape[1]
    _, member = place(radix)
    for d, out in enumerate(outs):
        for j in range(offs):
            mats = [thirds[j * less + d][0, jnp.bitwise_xor(member, i)] for i in range(radix)]
            slots = slots_of([ref[j, d] for ref in got], second_along, second_both, j, d + 1)
            out[j] = dot(jnp.concatenate(mats, axis=1), slots).astype(BF16)


def last_own_kernel(leaf, up_own, *own):
    put_own(up_own.at[up_own.shape[0] - 1], leaf[...], own, 0)


def sum_kernel(radix, *refs):
    got, thirds, outs = take(refs, radix, (len(refs) - radix) // 2, (len(refs) - radix) // 2)
    got = got[::-1]
    _, member = place(radix)
    for d, (third, out) in enumerate(zip(thirds, outs)):
        for j in range(out.shape[0]):
            mats = [third[j, jnp.bitwise_xor(member, i)] for i in range(radix)]
            slots = jnp.concatenate([ref[j, d] for ref in got], axis=0)
            out[j] = dot(jnp.concatenate(mats, axis=1), slots).astype(BF16)


def group_coef(j, slots, third, radix):
    group, member = place(radix)
    mats = [third[0, j, 0, group * radix + jnp.bitwise_xor(member, i)] for i in range(radix)]
    return dot(jnp.concatenate(mats, axis=1), slots).astype(BF16)


def middle_kernel(
    radix, groups, offs, third, rhs, basis, row_mats, up_other, second_along, second_both, *refs
):
    crossed, own_in, (residual_ref, leaf_ref), other = take(refs, groups - 1, radix, 2, radix)
    coefs = []
    for j in range(offs):
        slots = slots_of([ref[j] for ref in own_in], second_along, second_both, j, 0)
        coefs += [group_coef(j, slots, third, radix)] + [ref[j] for ref in crossed]
    coefs = jnp.concatenate(coefs, axis=0)
    leaves, leaf_rows = basis.shape[2], basis.shape[3]
    leaf = []
    for k in range(leaves):
        rows = slice(k * leaf_rows, (k + 1) * leaf_rows)
        residual = rhs[0, rows].astype(F32) - dot(row_mats[rows], coefs)
        residual_ref[rows] = residual
        leaf.append(dot_t(basis[0, offs, k], residual.astype(BF16)).astype(BF16))
    leaf = jnp.concatenate(leaf, axis=0)
    leaf_ref[...] = leaf
    put_other(up_other.at[offs], leaf, other, 0)


def last_kernel(radix, groups, offs, third, row_mats, residual, *refs):
    crossed, own_in, (out, held, sem) = take(refs, groups - 1, radix, 3)
    slots = jnp.concatenate([ref[0] for ref in own_in[::-1]], axis=0)
    coefs = [group_coef(offs, slots, third, radix)] + [ref[0] for ref in crossed]
    coefs = jnp.concatenate(coefs, axis=0)
    count = sem.shape[0]
    height = residual.shape[0] // count
    copies = []
    for i in range(count):
        rows = pl.ds(i * height, height)
        held[rows] = (residual[rows] + dot(row_mats[rows], coefs)).astype(BF16)
        copies.append(pltpu.make_async_copy(held.at[rows], out.at[0, rows], sem.at[i]))
        copies[-1].start()
    for copy in copies:
        copy.wait()


def after(array, *others):
    return lax.optimization_barrier((array, *others))[0]


def on_device(
    row_size, box_size, solved, rhs, leaf_basis, first_level, second_level, third_level, fourth_level, out_basis
):
    radix = first_level.shape[4]
    groups = box_size // radix
    less = groups - 1
    butterflies = leaf_basis.shape[1]
    offs = solved.shape[0]
    columns = solved.shape[2]
    rank = leaf_basis.shape[4]
    rows = rhs.shape[1]
    depth = radix * rank

    def over_row(array, mask):
        return lax.ppermute(array, "row", [(r, r ^ mask) for r in range(row_size)])

    def over_members(array, mask):
        pairs = [(b, (b // radix) * radix + ((b % radix) ^ mask)) for b in range(box_size)]
        return array if mask == 0 else lax.ppermute(array, "box", pairs)

    def over_groups(array, delta, mask=0):
        pairs = [
            (b, ((b // radix + delta) % groups) * radix + ((b % radix) ^ mask)) for b in range(box_size)
        ]
        return lax.ppermute(array, "box", pairs)

    def call(kernel, name, flops, outs, *args):
        outs = [jax.ShapeDtypeStruct(shape, dtype) for shape, dtype in outs]
        size = sum(a.size * a.dtype.itemsize for a in [*args, *outs])
        return pl.pallas_call(
            kernel,
            out_shape=outs,
            in_specs=[VMEM] * len(args),
            out_specs=[VMEM] * len(outs),
            compiler_params=pltpu.CompilerParams(vmem_limit_bytes=min(16 * MIB + 2 * size, 56 * MIB)),
            cost_estimate=pl.CostEstimate(flops=int(flops), bytes_accessed=0, transcendentals=0),
            name=name,
        )(*args)

    picked = call(
        functools.partial(pick_kernel, radix, groups),
        "pick_third",
        0,
        [((1, radix, rank, rank), BF16)] * (butterflies * less),
        third_level,
    )
    thirds = [
        [over_groups(a, d + 1) for d, a in enumerate(picked[j * less : (j + 1) * less])]
        for j in range(butterflies)
    ]

    up_own, up_other, up_mid, off_rows, last_rows = call(
        functools.partial(weights_kernel, radix, groups, offs, row_size),
        "weights",
        2 * butterflies * rank * (box_size * rank * depth + rows * groups * rank),
        [
            ((butterflies, radix, rank, depth), BF16),
            ((butterflies, radix, less, rank, depth), BF16),
            ((offs, groups, rank, depth), BF16),
            ((rows, offs * groups * rank), BF16),
            ((rows, groups * rank), BF16),
        ],
        first_level,
        second_level,
        fourth_level,
        out_basis,
    )

    seconds = call(
        functools.partial(second_kernel, radix, groups),
        "pick_second",
        0,
        [((offs, groups, rank, rank), BF16)] * 2,
        second_level,
    )
    seconds = [over_members(a, i) for i, a in zip((ALONG, BOTH), seconds)]

    pieces = [solved, over_row(solved, 1)]
    for mask in range(2, row_size, 2):
        far = after(over_row(solved, mask), up_own, *seconds, *thirds[0])
        pieces += [far, over_row(far, 1)]

    other_flops = 2 * columns * rank * radix * less * depth
    own_flops = 2 * columns * rank * radix * depth
    leaf_flops = 2 * columns * rank * rows
    row_flops = 2 * columns * rank * (depth + groups * rows)

    def own_out(count):
        return [((count, rank, columns), BF16)] * radix

    def other_out(count):
        return [((count, less, rank, columns), BF16)] * radix

    def cross(sums):
        return [over_groups(a, less - d) for d, a in enumerate(sums)]

    leaf, keep, across, along = call(
        functools.partial(off_kernel, row_size),
        "off_levels",
        offs * (leaf_flops + other_flops),
        [((offs, depth, columns), BF16)] + other_out(offs)[:3],
        leaf_basis,
        up_other,
        up_mid,
        *pieces,
    )
    along = over_members(along, ALONG)
    across = over_members(across, ACROSS)
    own = call(own_kernel, "own_levels", offs * own_flops, own_out(offs)[:3], leaf, up_own, up_mid)
    both = over_members(after(along, across, own[2], *[a for t in thirds[:offs] for a in t]), ACROSS)
    own_along = over_members(after(own[2], along), ALONG)
    sums = call(
        off_sum_kernel,
        "off_sums",
        offs * less * 2 * columns * rank * depth,
        [((offs, rank, columns), BF16)] * less,
        *seconds,
        keep,
        along,
        across,
        both,
        *[a for j in range(offs) for a in thirds[j]],
    )
    crossed = cross(sums)
    own = [
        own[0],
        own_along,
        over_members(after(own[1], both, *thirds[-1]), ACROSS),
    ]
    own.append(over_members(after(own_along, own[2], *sums), ACROSS))

    residual, leaf, *other = call(
        functools.partial(middle_kernel, radix, groups, offs),
        "middle_levels",
        offs * row_flops + leaf_flops + other_flops + own_flops,
        [((rows, columns), F32), ((depth, columns), BF16)] + other_out(1),
        third_level,
        rhs,
        leaf_basis,
        off_rows,
        up_other,
        *seconds,
        *crossed,
        *own,
    )
    own = call(last_own_kernel, "last_own_levels", own_flops, own_out(1), leaf, up_own)
    other = [over_members(a, i) for i, a in reversed(list(enumerate(other)))]
    sums = call(
        functools.partial(sum_kernel, radix),
        "sums",
        less * 2 * columns * rank * depth,
        [((1, rank, columns), BF16)] * less,
        *other,
        *thirds[offs],
    )
    crossed = cross(sums)
    own = [over_members(after(a, *sums) if i else a, i) for i, a in enumerate(own)]
    args = [third_level, last_rows, residual, *crossed, *own[::-1]]
    return pl.pallas_call(
        functools.partial(last_kernel, radix, groups, offs),
        out_shape=jax.ShapeDtypeStruct((1, rows, columns), BF16),
        in_specs=[VMEM] * len(args),
        out_specs=pl.BlockSpec(memory_space=pltpu.HBM),
        scratch_shapes=[pltpu.VMEM((rows, columns), BF16), pltpu.SemaphoreType.DMA((4,))],
        compiler_params=pltpu.CompilerParams(vmem_limit_bytes=32 * MIB),
        cost_estimate=pl.CostEstimate(flops=row_flops, bytes_accessed=0, transcendentals=0),
        name="last_levels",
    )(*args)


def solution(mesh):
    placed = (
        P(None, ("box", "row"), None),
        P("row", "box", None),
        P("row", None, "box", None, None),
        P("row", None, "box", None, None, None, None),
        P("row", None, "box", None, None, None),
        P("row", None, "box", None, None, None),
        P("row", None, "box", None, None, None, None),
        P("row", None, "box", None, None),
    )
    return jax.shard_map(
        functools.partial(on_device, mesh.shape["row"], mesh.shape["box"]),
        mesh=mesh,
        in_specs=placed,
        out_specs=P("row", "box", None),
        check_vma=False,
    )
```

```python
import functools

import jax
import jax.numpy as jnp
from jax import lax
from jax.experimental import pallas as pl
from jax.experimental.pallas import tpu as pltpu
from jax.sharding import PartitionSpec as P

F32 = jnp.float32
BF16 = jnp.bfloat16
MIB = 1024 * 1024
ACROSS, ALONG, BOTH = 1, 2, 3
VMEM = pl.BlockSpec(memory_space=pltpu.VMEM)


def dot(a, b):
    return jnp.dot(a, b, preferred_element_type=F32)


def dot_t(a, b):
    return lax.dot_general(a, b, (((0,), (0,)), ((), ())), preferred_element_type=F32)


def place(radix):
    box = lax.axis_index("box")
    return lax.div(box, radix), lax.rem(box, radix)


def wrap(value, size):
    return lax.rem(value + size, size)


def take(refs, *counts):
    refs, out = list(refs), []
    for count in counts:
        out.append(refs[:count])
        refs = refs[count:]
    return out


def pick_kernel(radix, groups, third, *outs):
    group, _ = place(radix)
    start = 0
    for at, out in enumerate(outs):
        base = wrap(group + at % (groups - 1) + 1, groups) * radix
        for j in range(out.shape[0]):
            for k in range(radix):
                out[j, k] = third[0, start + j, 0, base + k]
        start += out.shape[0] if at % (groups - 1) == groups - 2 else 0


def second_kernel(radix, groups, second, *outs):
    group, member = place(radix)
    for i, out in zip((ALONG, BOTH), outs):
        for j in range(out.shape[0]):
            for delta in range(groups):
                out[j, delta] = second[0, j, 0, wrap(group - delta, groups) * radix + jnp.bitwise_xor(member, i)]


def leaf_order(row, leaves, row_size):
    per_leaf = row_size // leaves
    return [jnp.bitwise_xor(lax.div(row, per_leaf), t) for t in range(leaves)]


def weights_kernel(radix, groups, offs, row_size, first, second, fourth, out_basis, *outs):
    up_own, up_other, up_mid, off_rows, last_rows = outs
    levels = first.shape[3]
    slots = second.shape[3]
    rank = fourth.shape[6]
    half_rows = out_basis.shape[3]
    group, member = place(radix)
    for j in range(first.shape[1]):
        order = leaf_order(lax.axis_index("row"), radix, row_size) if j < offs else range(radix)

        def up(slot):
            level = lax.div(slot, slots // levels)
            mats = jnp.concatenate([first[0, j, 0, level, k] for k in order], axis=1)
            return dot(second[0, j, 0, slot], mats).astype(BF16)

        for i in range(radix):
            box = jnp.bitwise_xor(member, i)
            up_own[j, i] = up(group * radix + box)
            for delta in range(1, groups):
                up_other[j, i, delta - 1] = up(wrap(group - delta, groups) * radix + box)
        if j < offs:
            for delta in range(groups):
                slot = wrap(group - delta, groups) * radix + jnp.bitwise_xor(member, ALONG)
                level = lax.div(slot, slots // levels)
                up_mid[j, delta] = jnp.concatenate([first[0, j, 0, level, k] for k in order], axis=1)
        out, start = (off_rows, j * groups * rank) if j < offs else (last_rows, 0)
        for h in range(fourth.shape[3]):
            mats = [fourth[0, j, 0, h, wrap(group + delta, groups)] for delta in range(groups)]
            out[h * half_rows : (h + 1) * half_rows, start : start + groups * rank] = dot(
                out_basis[0, j, h], jnp.concatenate(mats, axis=1)
            ).astype(BF16)


def put_other(mats, leaf, other, at):
    radix, less, rank, depth = mats.shape
    coef = dot(mats[...].reshape(radix * less * rank, depth), leaf).astype(BF16)
    for i, ref in enumerate(other):
        ref[at] = coef[i * less * rank : (i + 1) * less * rank].reshape(ref.shape[1:])


def put_own(mats, leaf, own, at):
    radix, rank, depth = mats.shape
    coef = dot(mats[...].reshape(radix * rank, depth), leaf).astype(BF16)
    for i, ref in enumerate(own):
        ref[at] = coef[i * rank : (i + 1) * rank]


def off_kernel(pieces, basis, up_other, up_mid, *refs):
    parts, (leaf_ref, keep, across, along) = take(refs, pieces, 4)
    row = lax.axis_index("row")
    leaves, leaf_rows = basis.shape[2], basis.shape[3]
    rows = parts[0].shape[1]
    per_leaf = leaf_rows // rows
    order = leaf_order(row, leaves, pieces)
    less, rank, columns = keep.shape[1:]
    for j in range(parts[0].shape[0]):
        leaf = []
        for t in range(leaves):
            total = None
            for u in range(per_leaf):
                start = jnp.bitwise_xor(lax.rem(row, per_leaf), u) * rows
                if per_leaf == 1:
                    mat = basis[0, j, order[t]]
                else:
                    mat = basis[0, j, order[t], pl.ds(pl.multiple_of(start, rows), rows)]
                part = dot_t(mat, parts[t * per_leaf + u][j])
                total = part if total is None else total + part
            leaf.append(total.astype(BF16))
        leaf = jnp.concatenate(leaf, axis=0)
        leaf_ref[j] = leaf
        mats = [up_other[j, 0], up_other[j, ACROSS], up_mid[j, 1:]]
        mats = jnp.concatenate([m.reshape(less * rank, m.shape[2]) for m in mats], axis=0)
        coef = dot(mats, leaf).astype(BF16)
        for i, ref in enumerate((keep, across, along)):
            ref[j] = coef[i * less * rank : (i + 1) * less * rank].reshape(less, rank, columns)


def own_kernel(leaf, up_own, up_mid, *own):
    rank = up_mid.shape[2]
    for j in range(leaf.shape[0]):
        coef = dot(jnp.concatenate([up_own[j, 0], up_own[j, ACROSS], up_mid[j, 0]], axis=0), leaf[j]).astype(BF16)
        for i, ref in enumerate(own):
            ref[j] = coef[i * rank : (i + 1) * rank]


def slots_of(got, second_along, second_both, j, delta):
    keep, across, along, both = got
    return jnp.concatenate(
        [
            keep,
            across,
            dot(second_along[j, delta], along).astype(BF16),
            dot(second_both[j, delta], both).astype(BF16),
        ],
        axis=0,
    )


def off_sum_kernel(second_along, second_both, *refs):
    offs = second_along.shape[0]
    less = (len(refs) - 4) // (offs + 1)
    got, thirds, outs = take(refs, 4, offs * less, less)
    radix = thirds[0].shape[1]
    _, member = place(radix)
    for d, out in enumerate(outs):
        for j in range(offs):
            mats = [thirds[j * less + d][0, jnp.bitwise_xor(member, i)] for i in range(radix)]
            slots = slots_of([ref[j, d] for ref in got], second_along, second_both, j, d + 1)
            out[j] = dot(jnp.concatenate(mats, axis=1), slots).astype(BF16)


def last_own_kernel(leaf, up_own, *own):
    put_own(up_own.at[up_own.shape[0] - 1], leaf[...], own, 0)


def sum_kernel(radix, *refs):
    got, thirds, outs = take(refs, radix, (len(refs) - radix) // 2, (len(refs) - radix) // 2)
    got = got[::-1]
    _, member = place(radix)
    for d, (third, out) in enumerate(zip(thirds, outs)):
        for j in range(out.shape[0]):
            mats = [third[j, jnp.bitwise_xor(member, i)] for i in range(radix)]
            slots = jnp.concatenate([ref[j, d] for ref in got], axis=0)
            out[j] = dot(jnp.concatenate(mats, axis=1), slots).astype(BF16)


def group_coef(j, slots, third, radix):
    group, member = place(radix)
    mats = [third[0, j, 0, group * radix + jnp.bitwise_xor(member, i)] for i in range(radix)]
    return dot(jnp.concatenate(mats, axis=1), slots).astype(BF16)


def middle_kernel(
    radix, groups, offs, third, rhs, basis, row_mats, up_other, second_along, second_both, *refs
):
    crossed, own_in, (residual_ref, leaf_ref), other = take(refs, groups - 1, radix, 2, radix)
    coefs = []
    for j in range(offs):
        slots = slots_of([ref[j] for ref in own_in], second_along, second_both, j, 0)
        coefs += [group_coef(j, slots, third, radix)] + [ref[j] for ref in crossed]
    coefs = jnp.concatenate(coefs, axis=0)
    leaves, leaf_rows = basis.shape[2], basis.shape[3]
    leaf = []
    for k in range(leaves):
        rows = slice(k * leaf_rows, (k + 1) * leaf_rows)
        residual = rhs[0, rows].astype(F32) - dot(row_mats[rows], coefs)
        residual_ref[rows] = residual
        leaf.append(dot_t(basis[0, offs, k], residual.astype(BF16)).astype(BF16))
    leaf = jnp.concatenate(leaf, axis=0)
    leaf_ref[...] = leaf
    put_other(up_other.at[offs], leaf, other, 0)


def last_kernel(radix, groups, offs, third, row_mats, residual, *refs):
    crossed, own_in, (out, held, sem) = take(refs, groups - 1, radix, 3)
    slots = jnp.concatenate([ref[0] for ref in own_in[::-1]], axis=0)
    coefs = [group_coef(offs, slots, third, radix)] + [ref[0] for ref in crossed]
    coefs = jnp.concatenate(coefs, axis=0)
    count = sem.shape[0]
    height = residual.shape[0] // count
    copies = []
    for i in range(count):
        rows = pl.ds(i * height, height)
        held[rows] = (residual[rows] + dot(row_mats[rows], coefs)).astype(BF16)
        copies.append(pltpu.make_async_copy(held.at[rows], out.at[0, rows], sem.at[i]))
        copies[-1].start()
    for copy in copies:
        copy.wait()


def after(array, *others):
    return lax.optimization_barrier((array, *others))[0]


def on_device(
    row_size, box_size, solved, rhs, leaf_basis, first_level, second_level, third_level, fourth_level, out_basis
):
    radix = first_level.shape[4]
    groups = box_size // radix
    less = groups - 1
    butterflies = leaf_basis.shape[1]
    offs = solved.shape[0]
    columns = solved.shape[2]
    rank = leaf_basis.shape[4]
    rows = rhs.shape[1]
    depth = radix * rank

    def over_row(array, mask):
        return lax.ppermute(array, "row", [(r, r ^ mask) for r in range(row_size)])

    def over_members(array, mask):
        pairs = [(b, (b // radix) * radix + ((b % radix) ^ mask)) for b in range(box_size)]
        return array if mask == 0 else lax.ppermute(array, "box", pairs)

    def over_groups(array, delta, mask=0):
        pairs = [
            (b, ((b // radix + delta) % groups) * radix + ((b % radix) ^ mask)) for b in range(box_size)
        ]
        return lax.ppermute(array, "box", pairs)

    def call(kernel, name, flops, outs, *args):
        outs = [jax.ShapeDtypeStruct(shape, dtype) for shape, dtype in outs]
        size = sum(a.size * a.dtype.itemsize for a in [*args, *outs])
        return pl.pallas_call(
            kernel,
            out_shape=outs,
            in_specs=[VMEM] * len(args),
            out_specs=[VMEM] * len(outs),
            compiler_params=pltpu.CompilerParams(vmem_limit_bytes=min(16 * MIB + 2 * size, 56 * MIB)),
            cost_estimate=pl.CostEstimate(flops=int(flops), bytes_accessed=0, transcendentals=0),
            name=name,
        )(*args)

    picked = call(
        functools.partial(pick_kernel, radix, groups),
        "pick_third",
        0,
        [((1, radix, rank, rank), BF16)] * (butterflies * less),
        third_level,
    )
    thirds = [
        [over_groups(a, d + 1) for d, a in enumerate(picked[j * less : (j + 1) * less])]
        for j in range(offs)
    ]

    up_own, up_other, up_mid, off_rows, last_rows = call(
        functools.partial(weights_kernel, radix, groups, offs, row_size),
        "weights",
        2 * butterflies * rank * (box_size * rank * depth + rows * groups * rank),
        [
            ((butterflies, radix, rank, depth), BF16),
            ((butterflies, radix, less, rank, depth), BF16),
            ((offs, groups, rank, depth), BF16),
            ((rows, offs * groups * rank), BF16),
            ((rows, groups * rank), BF16),
        ],
        first_level,
        second_level,
        fourth_level,
        out_basis,
    )

    seconds = call(
        functools.partial(second_kernel, radix, groups),
        "pick_second",
        0,
        [((offs, groups, rank, rank), BF16)] * 2,
        second_level,
    )
    seconds = [over_members(a, i) for i, a in zip((ALONG, BOTH), seconds)]

    pieces = [solved, over_row(solved, 1)]
    for mask in range(2, row_size, 2):
        far = after(over_row(solved, mask), up_own, *seconds, *thirds[0])
        pieces += [far, over_row(far, 1)]

    other_flops = 2 * columns * rank * radix * less * depth
    own_flops = 2 * columns * rank * radix * depth
    leaf_flops = 2 * columns * rank * rows
    row_flops = 2 * columns * rank * (depth + groups * rows)

    def own_out(count):
        return [((count, rank, columns), BF16)] * radix

    def other_out(count):
        return [((count, less, rank, columns), BF16)] * radix

    def cross(sums):
        return [over_groups(a, less - d) for d, a in enumerate(sums)]

    leaf, keep, across, along = call(
        functools.partial(off_kernel, row_size),
        "off_levels",
        offs * (leaf_flops + other_flops),
        [((offs, depth, columns), BF16)] + other_out(offs)[:3],
        leaf_basis,
        up_other,
        up_mid,
        *pieces,
    )
    along = over_members(along, ALONG)
    across = over_members(across, ACROSS)
    both = over_members(after(along, across), ACROSS)
    own = call(own_kernel, "own_levels", offs * own_flops, own_out(offs)[:3], leaf, up_own, up_mid)
    own_along = over_members(after(own[2], along), ALONG)
    sums = call(
        off_sum_kernel,
        "off_sums",
        offs * less * 2 * columns * rank * depth,
        [((offs, rank, columns), BF16)] * less,
        *seconds,
        keep,
        across,
        along,
        both,
        *[a for j in range(offs) for a in thirds[j]],
    )
    crossed = cross(sums)
    own = [
        own[0],
        over_members(after(own[1], both, *[a for t in thirds for a in t]), ACROSS),
        own_along,
    ]
    own.append(over_members(after(own_along, own[1], *sums), ACROSS))

    residual, leaf, *other = call(
        functools.partial(middle_kernel, radix, groups, offs),
        "middle_levels",
        offs * row_flops + leaf_flops + other_flops + own_flops,
        [((rows, columns), F32), ((depth, columns), BF16)] + other_out(1),
        third_level,
        rhs,
        leaf_basis,
        off_rows,
        up_other,
        *seconds,
        *crossed,
        *own,
    )
    own = call(last_own_kernel, "last_own_levels", own_flops, own_out(1), leaf, up_own)
    thirds_last = [over_groups(after(a, residual), d + 1) for d, a in enumerate(picked[offs * less :])]
    other = [over_members(a, i) for i, a in reversed(list(enumerate(other)))]
    sums = call(
        functools.partial(sum_kernel, radix),
        "sums",
        less * 2 * columns * rank * depth,
        [((1, rank, columns), BF16)] * less,
        *other,
        *thirds_last,
    )
    crossed = cross(sums)
    own = [over_members(after(a, *sums) if i else a, i) for i, a in enumerate(own)]
    args = [third_level, last_rows, residual, *crossed, *own[::-1]]
    return pl.pallas_call(
        functools.partial(last_kernel, radix, groups, offs),
        out_shape=jax.ShapeDtypeStruct((1, rows, columns), BF16),
        in_specs=[VMEM] * len(args),
        out_specs=pl.BlockSpec(memory_space=pltpu.HBM),
        scratch_shapes=[pltpu.VMEM((rows, columns), BF16), pltpu.SemaphoreType.DMA((4,))],
        compiler_params=pltpu.CompilerParams(vmem_limit_bytes=32 * MIB),
        cost_estimate=pl.CostEstimate(flops=row_flops, bytes_accessed=0, transcendentals=0),
        name="last_levels",
    )(*args)


def solution(mesh):
    placed = (
        P(None, ("box", "row"), None),
        P("row", "box", None),
        P("row", None, "box", None, None),
        P("row", None, "box", None, None, None, None),
        P("row", None, "box", None, None, None),
        P("row", None, "box", None, None, None),
        P("row", None, "box", None, None, None, None),
        P("row", None, "box", None, None),
    )
    return jax.shard_map(
        functools.partial(on_device, mesh.shape["row"], mesh.shape["box"]),
        mesh=mesh,
        in_specs=placed,
        out_specs=P("row", "box", None),
        check_vma=False,
    )
```

```python
import functools

import jax
import jax.numpy as jnp
from jax import lax
from jax.experimental import pallas as pl
from jax.experimental.pallas import tpu as pltpu
from jax.sharding import PartitionSpec as P

F32 = jnp.float32
BF16 = jnp.bfloat16
MIB = 1024 * 1024
ACROSS, ALONG, BOTH = 1, 2, 3
VMEM = pl.BlockSpec(memory_space=pltpu.VMEM)


def dot(a, b):
    return jnp.dot(a, b, preferred_element_type=F32)


def dot_t(a, b):
    return lax.dot_general(a, b, (((0,), (0,)), ((), ())), preferred_element_type=F32)


def place(radix):
    box = lax.axis_index("box")
    return lax.div(box, radix), lax.rem(box, radix)


def wrap(value, size):
    return lax.rem(value + size, size)


def take(refs, *counts):
    refs, out = list(refs), []
    for count in counts:
        out.append(refs[:count])
        refs = refs[count:]
    return out


def pick_kernel(radix, groups, third, *outs):
    group, _ = place(radix)
    start = 0
    for at, out in enumerate(outs):
        base = wrap(group + at % (groups - 1) + 1, groups) * radix
        for j in range(out.shape[0]):
            for k in range(radix):
                out[j, k] = third[0, start + j, 0, base + k]
        start += out.shape[0] if at % (groups - 1) == groups - 2 else 0


def second_kernel(radix, groups, second, *outs):
    group, member = place(radix)
    for i, out in zip((ALONG, BOTH), outs):
        for j in range(out.shape[0]):
            for delta in range(groups):
                out[j, delta] = second[0, j, 0, wrap(group - delta, groups) * radix + jnp.bitwise_xor(member, i)]


def leaf_order(row, leaves, row_size):
    per_leaf = row_size // leaves
    return [jnp.bitwise_xor(lax.div(row, per_leaf), t) for t in range(leaves)]


def weights_kernel(radix, groups, offs, row_size, first, second, fourth, out_basis, *outs):
    up_own, up_other, up_mid, off_rows, last_rows = outs
    levels = first.shape[3]
    slots = second.shape[3]
    rank = fourth.shape[6]
    half_rows = out_basis.shape[3]
    group, member = place(radix)
    for j in range(first.shape[1]):
        order = leaf_order(lax.axis_index("row"), radix, row_size) if j < offs else range(radix)

        def up(slot):
            level = lax.div(slot, slots // levels)
            mats = jnp.concatenate([first[0, j, 0, level, k] for k in order], axis=1)
            return dot(second[0, j, 0, slot], mats).astype(BF16)

        for i in range(radix):
            box = jnp.bitwise_xor(member, i)
            up_own[j, i] = up(group * radix + box)
            for delta in range(1, groups):
                up_other[j, i, delta - 1] = up(wrap(group - delta, groups) * radix + box)
        if j < offs:
            for delta in range(groups):
                slot = wrap(group - delta, groups) * radix + jnp.bitwise_xor(member, ALONG)
                level = lax.div(slot, slots // levels)
                up_mid[j, delta] = jnp.concatenate([first[0, j, 0, level, k] for k in order], axis=1)
        out, start = (off_rows, j * groups * rank) if j < offs else (last_rows, 0)
        for h in range(fourth.shape[3]):
            mats = [fourth[0, j, 0, h, wrap(group + delta, groups)] for delta in range(groups)]
            out[h * half_rows : (h + 1) * half_rows, start : start + groups * rank] = dot(
                out_basis[0, j, h], jnp.concatenate(mats, axis=1)
            ).astype(BF16)


def put_other(mats, leaf, other, at):
    radix, less, rank, depth = mats.shape
    coef = dot(mats[...].reshape(radix * less * rank, depth), leaf).astype(BF16)
    for i, ref in enumerate(other):
        ref[at] = coef[i * less * rank : (i + 1) * less * rank].reshape(ref.shape[1:])


def put_own(mats, leaf, own, at):
    radix, rank, depth = mats.shape
    coef = dot(mats[...].reshape(radix * rank, depth), leaf).astype(BF16)
    for i, ref in enumerate(own):
        ref[at] = coef[i * rank : (i + 1) * rank]


def off_kernel(pieces, basis, up_other, up_mid, *refs):
    parts, (leaf_ref, keep, across, along) = take(refs, pieces, 4)
    row = lax.axis_index("row")
    leaves, leaf_rows = basis.shape[2], basis.shape[3]
    rows = parts[0].shape[1]
    per_leaf = leaf_rows // rows
    order = leaf_order(row, leaves, pieces)
    less, rank, columns = keep.shape[1:]
    for j in range(parts[0].shape[0]):
        leaf = []
        for t in range(leaves):
            total = None
            for u in range(per_leaf):
                start = jnp.bitwise_xor(lax.rem(row, per_leaf), u) * rows
                if per_leaf == 1:
                    mat = basis[0, j, order[t]]
                else:
                    mat = basis[0, j, order[t], pl.ds(pl.multiple_of(start, rows), rows)]
                part = dot_t(mat, parts[t * per_leaf + u][j])
                total = part if total is None else total + part
            leaf.append(total.astype(BF16))
        leaf = jnp.concatenate(leaf, axis=0)
        leaf_ref[j] = leaf
        mats = [up_other[j, 0], up_other[j, ACROSS], up_mid[j, 1:]]
        mats = jnp.concatenate([m.reshape(less * rank, m.shape[2]) for m in mats], axis=0)
        coef = dot(mats, leaf).astype(BF16)
        for i, ref in enumerate((keep, across, along)):
            ref[j] = coef[i * less * rank : (i + 1) * less * rank].reshape(less, rank, columns)


def own_kernel(leaf, up_own, up_mid, *own):
    rank = up_mid.shape[2]
    for j in range(leaf.shape[0]):
        coef = dot(jnp.concatenate([up_own[j, 0], up_own[j, ACROSS], up_mid[j, 0]], axis=0), leaf[j]).astype(BF16)
        for i, ref in enumerate(own):
            ref[j] = coef[i * rank : (i + 1) * rank]


def slots_of(got, second_along, second_both, j, delta):
    keep, across, along, both = got
    return jnp.concatenate(
        [
            keep,
            across,
            dot(second_along[j, delta], along).astype(BF16),
            dot(second_both[j, delta], both).astype(BF16),
        ],
        axis=0,
    )


def off_sum_kernel(second_along, second_both, *refs):
    offs = second_along.shape[0]
    less = (len(refs) - 4) // (offs + 1)
    got, thirds, outs = take(refs, 4, offs * less, less)
    radix = thirds[0].shape[1]
    _, member = place(radix)
    for d, out in enumerate(outs):
        for j in range(offs):
            mats = [thirds[j * less + d][0, jnp.bitwise_xor(member, i)] for i in range(radix)]
            slots = slots_of([ref[j, d] for ref in got], second_along, second_both, j, d + 1)
            out[j] = dot(jnp.concatenate(mats, axis=1), slots).astype(BF16)


def last_own_kernel(leaf, up_own, *own):
    put_own(up_own.at[up_own.shape[0] - 1], leaf[...], own, 0)


def sum_kernel(radix, *refs):
    got, thirds, outs = take(refs, radix, (len(refs) - radix) // 2, (len(refs) - radix) // 2)
    got = got[::-1]
    _, member = place(radix)
    for d, (third, out) in enumerate(zip(thirds, outs)):
        for j in range(out.shape[0]):
            mats = [third[j, jnp.bitwise_xor(member, i)] for i in range(radix)]
            slots = jnp.concatenate([ref[j, d] for ref in got], axis=0)
            out[j] = dot(jnp.concatenate(mats, axis=1), slots).astype(BF16)


def group_coef(j, slots, third, radix):
    group, member = place(radix)
    mats = [third[0, j, 0, group * radix + jnp.bitwise_xor(member, i)] for i in range(radix)]
    return dot(jnp.concatenate(mats, axis=1), slots).astype(BF16)


def middle_kernel(
    radix, groups, offs, third, rhs, basis, row_mats, up_other, second_along, second_both, *refs
):
    crossed, own_in, (residual_ref, leaf_ref), other = take(refs, groups - 1, radix, 2, radix)
    coefs = []
    for j in range(offs):
        slots = slots_of([ref[j] for ref in own_in], second_along, second_both, j, 0)
        coefs += [group_coef(j, slots, third, radix)] + [ref[j] for ref in crossed]
    coefs = jnp.concatenate(coefs, axis=0)
    leaves, leaf_rows = basis.shape[2], basis.shape[3]
    leaf = []
    for k in range(leaves):
        rows = slice(k * leaf_rows, (k + 1) * leaf_rows)
        residual = rhs[0, rows].astype(F32) - dot(row_mats[rows], coefs)
        residual_ref[rows] = residual
        leaf.append(dot_t(basis[0, offs, k], residual.astype(BF16)).astype(BF16))
    leaf = jnp.concatenate(leaf, axis=0)
    leaf_ref[...] = leaf
    put_other(up_other.at[offs], leaf, other, 0)


def last_kernel(radix, groups, offs, third, row_mats, residual, *refs):
    crossed, own_in, (out, held, sem) = take(refs, groups - 1, radix, 3)
    slots = jnp.concatenate([ref[0] for ref in own_in[::-1]], axis=0)
    coefs = [group_coef(offs, slots, third, radix)] + [ref[0] for ref in crossed]
    coefs = jnp.concatenate(coefs, axis=0)
    count = sem.shape[0]
    height = residual.shape[0] // count
    copies = []
    for i in range(count):
        rows = pl.ds(i * height, height)
        held[rows] = (residual[rows] + dot(row_mats[rows], coefs)).astype(BF16)
        copies.append(pltpu.make_async_copy(held.at[rows], out.at[0, rows], sem.at[i]))
        copies[-1].start()
    for copy in copies:
        copy.wait()


def after(array, *others):
    return lax.optimization_barrier((array, *others))[0]


def on_device(
    row_size, box_size, solved, rhs, leaf_basis, first_level, second_level, third_level, fourth_level, out_basis
):
    radix = first_level.shape[4]
    groups = box_size // radix
    less = groups - 1
    butterflies = leaf_basis.shape[1]
    offs = solved.shape[0]
    columns = solved.shape[2]
    rank = leaf_basis.shape[4]
    rows = rhs.shape[1]
    depth = radix * rank

    def over_row(array, mask):
        return lax.ppermute(array, "row", [(r, r ^ mask) for r in range(row_size)])

    def over_members(array, mask):
        pairs = [(b, (b // radix) * radix + ((b % radix) ^ mask)) for b in range(box_size)]
        return array if mask == 0 else lax.ppermute(array, "box", pairs)

    def over_groups(array, delta, mask=0):
        pairs = [
            (b, ((b // radix + delta) % groups) * radix + ((b % radix) ^ mask)) for b in range(box_size)
        ]
        return lax.ppermute(array, "box", pairs)

    def call(kernel, name, flops, outs, *args):
        outs = [jax.ShapeDtypeStruct(shape, dtype) for shape, dtype in outs]
        size = sum(a.size * a.dtype.itemsize for a in [*args, *outs])
        return pl.pallas_call(
            kernel,
            out_shape=outs,
            in_specs=[VMEM] * len(args),
            out_specs=[VMEM] * len(outs),
            compiler_params=pltpu.CompilerParams(vmem_limit_bytes=min(16 * MIB + 2 * size, 56 * MIB)),
            cost_estimate=pl.CostEstimate(flops=int(flops), bytes_accessed=0, transcendentals=0),
            name=name,
        )(*args)

    picked = call(
        functools.partial(pick_kernel, radix, groups),
        "pick_third",
        0,
        [((1, radix, rank, rank), BF16)] * (butterflies * less),
        third_level,
    )
    thirds = [
        [over_groups(a, d + 1) for d, a in enumerate(picked[j * less : (j + 1) * less])]
        for j in range(butterflies)
    ]

    up_own, up_other, up_mid, off_rows, last_rows = call(
        functools.partial(weights_kernel, radix, groups, offs, row_size),
        "weights",
        2 * butterflies * rank * (box_size * rank * depth + rows * groups * rank),
        [
            ((butterflies, radix, rank, depth), BF16),
            ((butterflies, radix, less, rank, depth), BF16),
            ((offs, groups, rank, depth), BF16),
            ((rows, offs * groups * rank), BF16),
            ((rows, groups * rank), BF16),
        ],
        first_level,
        second_level,
        fourth_level,
        out_basis,
    )

    seconds = call(
        functools.partial(second_kernel, radix, groups),
        "pick_second",
        0,
        [((offs, groups, rank, rank), BF16)] * 2,
        second_level,
    )
    seconds = [over_members(a, i) for i, a in zip((ALONG, BOTH), seconds)]

    pieces = [solved, over_row(solved, 1)]
    for mask in range(2, row_size, 2):
        far = after(over_row(solved, mask), up_own, *seconds, *thirds[0])
        pieces += [far, over_row(far, 1)]

    other_flops = 2 * columns * rank * radix * less * depth
    own_flops = 2 * columns * rank * radix * depth
    leaf_flops = 2 * columns * rank * rows
    row_flops = 2 * columns * rank * (depth + groups * rows)

    def own_out(count):
        return [((count, rank, columns), BF16)] * radix

    def other_out(count):
        return [((count, less, rank, columns), BF16)] * radix

    def cross(sums):
        return [over_groups(a, less - d) for d, a in enumerate(sums)]

    leaf, keep, across, along = call(
        functools.partial(off_kernel, row_size),
        "off_levels",
        offs * (leaf_flops + other_flops),
        [((offs, depth, columns), BF16)] + other_out(offs)[:3],
        leaf_basis,
        up_other,
        up_mid,
        *pieces,
    )
    along = over_members(along, ALONG)
    across = over_members(across, ACROSS)
    both = over_members(after(along, across, *[a for t in thirds[:offs] for a in t]), ACROSS)
    own = call(own_kernel, "own_levels", offs * own_flops, own_out(offs)[:3], leaf, up_own, up_mid)
    own_along = over_members(after(own[2], along), ALONG)
    sums = call(
        off_sum_kernel,
        "off_sums",
        offs * less * 2 * columns * rank * depth,
        [((offs, rank, columns), BF16)] * less,
        *seconds,
        keep,
        across,
        along,
        both,
        *[a for j in range(offs) for a in thirds[j]],
    )
    crossed = cross(sums)
    own = [
        own[0],
        over_members(after(own[1], both, *thirds[-1]), ACROSS),
        own_along,
    ]
    own.append(over_members(after(own_along, own[1], *sums), ACROSS))

    residual, leaf, *other = call(
        functools.partial(middle_kernel, radix, groups, offs),
        "middle_levels",
        offs * row_flops + leaf_flops + other_flops + own_flops,
        [((rows, columns), F32), ((depth, columns), BF16)] + other_out(1),
        third_level,
        rhs,
        leaf_basis,
        off_rows,
        up_other,
        *seconds,
        *crossed,
        *own,
    )
    own = call(last_own_kernel, "last_own_levels", own_flops, own_out(1), leaf, up_own)
    other = [over_members(a, i) for i, a in reversed(list(enumerate(other)))]
    sums = call(
        functools.partial(sum_kernel, radix),
        "sums",
        less * 2 * columns * rank * depth,
        [((1, rank, columns), BF16)] * less,
        *other,
        *thirds[offs],
    )
    crossed = cross(sums)
    own = [over_members(after(a, *([other[0]] if i == ACROSS else sums)) if i else a, i) for i, a in enumerate(own)]
    args = [third_level, last_rows, residual, *crossed, *own[::-1]]
    return pl.pallas_call(
        functools.partial(last_kernel, radix, groups, offs),
        out_shape=jax.ShapeDtypeStruct((1, rows, columns), BF16),
        in_specs=[VMEM] * len(args),
        out_specs=pl.BlockSpec(memory_space=pltpu.HBM),
        scratch_shapes=[pltpu.VMEM((rows, columns), BF16), pltpu.SemaphoreType.DMA((4,))],
        compiler_params=pltpu.CompilerParams(vmem_limit_bytes=32 * MIB),
        cost_estimate=pl.CostEstimate(flops=row_flops, bytes_accessed=0, transcendentals=0),
        name="last_levels",
    )(*args)


def solution(mesh):
    placed = (
        P(None, ("box", "row"), None),
        P("row", "box", None),
        P("row", None, "box", None, None),
        P("row", None, "box", None, None, None, None),
        P("row", None, "box", None, None, None),
        P("row", None, "box", None, None, None),
        P("row", None, "box", None, None, None, None),
        P("row", None, "box", None, None),
    )
    return jax.shard_map(
        functools.partial(on_device, mesh.shape["row"], mesh.shape["box"]),
        mesh=mesh,
        in_specs=placed,
        out_specs=P("row", "box", None),
        check_vma=False,
    )
```
